32 devices in a mesh: pts: 16 (over z, y, core), freq: 2 (over x).
Axes of the slice: x: 2, y: 2, z: 4, core: 2. Of those that a mesh axis runs over, the one named last changes fastest.
Arguments:
- snapshots: float32 [2112, 12288], P(None, ('pts', 'freq')), may hold values from -6 to 6
- weight: float32 [12288], P('pts'), may hold values from 0.1 to 10
- start_vec: float32 [64, 2, 32], replicated, may hold values from -6 to 6
Outputs:
- gram_mine: float32 [64, 2, 32, 32], P('freq')
- modes: float32 [64, 2, 12288], P('freq', None, 'pts')
The draws below stay inside these ranges and needn't reach their ends.
All inputs are finite; a program needn't handle non-finite values.
Results may differ from the reference program's by a relative error of at most 0.0003.
Values sent between devices are 32-bit elements; how exact they have to be, the bound alone decides.
No kernel may reach another device: no remote copies, remote signals or barrier semaphores. Data moves between devices by JAX's collectives and lax.ppermute only.
A program may use at most 64 MiB of HBM per device.

```python
import math
import jax
import jax.numpy as jnp
from jax import lax

NFFT = 128
NB = 32
NF = 64
ROWS = 12288
TIMES = 2112
N_PTS = 16


def draw_snapshots(key, part):
    key_offset = jax.random.fold_in(key, 11)
    key_noise = jax.random.fold_in(key, 23)
    offset = jax.random.uniform(key_offset, (1, ROWS), jnp.float32, -2.0, 2.0)
    fluct_part = jnp.clip(jax.random.normal(key_noise, (TIMES, ROWS), jnp.float32), -3.5, 3.5)
    return (offset + fluct_part).astype(jnp.float32)


def block_scale(own_key, dims, cuts, smallest, top_value):
    level = 1.0
    for position, parts in cuts:
        draws = jax.random.uniform(jax.random.fold_in(jax.random.fold_in(own_key, 6), position), (parts,), jnp.float32, smallest / len(cuts), top_value / len(cuts))
        level = level * jnp.repeat(jnp.exp(draws), dims[position] // parts).reshape((-1,) + (1,) * (len(dims) - 1 - position))
    return level


def bell_draw(key, extent, deviation, reach, kind=jnp.bfloat16):
    return jnp.clip(deviation * jax.random.normal(key, extent, jnp.float32), -reach, reach).astype(kind)


def setup_inputs(seed: int = 0) -> dict:
    seeds = jax.random.split(jax.random.key(seed), 4)
    snapshots = draw_snapshots(jax.random.fold_in(seeds[3], 71), 0)
    weight = jnp.clip(jnp.exp(math.log(10.0) - 4.6051702 * jax.random.uniform(seeds[1], (ROWS,), jnp.float32) ** block_scale(seeds[1], (ROWS,), ((0, 16),), -0.2, 0.2)), 0.1, 10.0)
    start_vec = bell_draw(seeds[2], (NF, 2, NB), 1.0, 6.0, jnp.float32)
    return dict(snapshots=snapshots, weight=weight, start_vec=start_vec)


def dft_table():
    times = jnp.arange(NFFT, dtype=jnp.int32)
    freqs = jnp.arange(NF, dtype=jnp.int32)
    phases = (freqs[:, None] * times[None, :] % NFFT).astype(jnp.float32) * (2.0 * math.pi / NFFT)
    window = 0.5 - 0.5 * jnp.cos(times.astype(jnp.float32) * (2.0 * math.pi / NFFT))
    weighted = window / jnp.sqrt(jnp.sum(window * window))
    return jnp.stack([jnp.cos(phases) * weighted, -jnp.sin(phases) * weighted], axis=1)

def spectra_of(block, dft_rows):
    fluct_rows = block - lax.optimization_barrier(jnp.mean(block, axis=0, keepdims=True))
    halves = fluct_rows.reshape(NB + 1, NFFT // 2, block.shape[1])
    early = jnp.einsum('kct,btr->kcbr', dft_rows[:, :, :NFFT // 2], halves[:-1], precision=lax.Precision.HIGHEST)
    later = jnp.einsum('kct,btr->kcbr', dft_rows[:, :, NFFT // 2:], halves[1:], precision=lax.Precision.HIGHEST)
    return early + later

def gram_of(spectra, weight, total_rows):
    real_part = spectra[:, 0]
    imag_part = spectra[:, 1]
    real_w = real_part * weight
    imag_w = imag_part * weight
    gram_real = jnp.einsum('fjr,fkr->fjk', real_w, real_part, precision=lax.Precision.HIGHEST) + jnp.einsum('fjr,fkr->fjk', imag_w, imag_part, precision=lax.Precision.HIGHEST)
    gram_imag = jnp.einsum('fjr,fkr->fjk', real_w, imag_part, precision=lax.Precision.HIGHEST) - jnp.einsum('fjr,fkr->fjk', imag_w, real_part, precision=lax.Precision.HIGHEST)
    return jnp.stack([gram_real, gram_imag], axis=1) / total_rows

def response_of(gram, start_vec):
    resp_real = jnp.einsum('fjk,fk->fj', gram[:, 0], start_vec[:, 0], precision=lax.Precision.HIGHEST) - jnp.einsum('fjk,fk->fj', gram[:, 1], start_vec[:, 1], precision=lax.Precision.HIGHEST)
    resp_imag = jnp.einsum('fjk,fk->fj', gram[:, 0], start_vec[:, 1], precision=lax.Precision.HIGHEST) + jnp.einsum('fjk,fk->fj', gram[:, 1], start_vec[:, 0], precision=lax.Precision.HIGHEST)
    scaling = 1.0 / jnp.sqrt(lax.optimization_barrier(jnp.mean(resp_real * resp_real + resp_imag * resp_imag, axis=1, keepdims=True)) + 1e-06)
    return jnp.stack([resp_real * scaling, resp_imag * scaling], axis=1)

def project(spectra, response):
    real_part = spectra[:, 0]
    imag_part = spectra[:, 1]
    mode_real = jnp.einsum('fjr,fj->fr', real_part, response[:, 0], precision=lax.Precision.HIGHEST) - jnp.einsum('fjr,fj->fr', imag_part, response[:, 1], precision=lax.Precision.HIGHEST)
    mode_imag = jnp.einsum('fjr,fj->fr', real_part, response[:, 1], precision=lax.Precision.HIGHEST) + jnp.einsum('fjr,fj->fr', imag_part, response[:, 0], precision=lax.Precision.HIGHEST)
    return jnp.stack([mode_real, mode_imag], axis=1)

def reference(snapshots, weight, start_vec):
    dft_rows = dft_table()
    block_rows = ROWS // N_PTS
    indices = jnp.arange(N_PTS, dtype=jnp.int32)

    def block_gram(index):
        first = (index * block_rows).astype(jnp.int32)
        block = lax.dynamic_slice_in_dim(snapshots, first, block_rows, 1)
        weights_block = lax.dynamic_slice_in_dim(weight, first, block_rows, 0)
        return gram_of(spectra_of(block, dft_rows), weights_block, ROWS)
    gram_full = lax.optimization_barrier(jnp.sum(lax.map(block_gram, indices), axis=0))
    response = response_of(gram_full, start_vec)

    def block_modes(index):
        first = (index * block_rows).astype(jnp.int32)
        block = lax.dynamic_slice_in_dim(snapshots, first, block_rows, 1)
        return project(spectra_of(block, dft_rows), response)
    pieces = lax.map(block_modes, indices)
    modes = jnp.transpose(pieces, (1, 2, 0, 3)).reshape(NF, 2, ROWS)
    return (gram_full, modes)
```

```python
import functools
import math

import jax
import jax.numpy as jnp
import numpy as np
from jax import lax
from jax.experimental import pallas as pl
from jax.experimental.pallas import tpu as pltpu
from jax.sharding import PartitionSpec as P

NFFT = 128
HALF = NFFT // 2
NF = 64
NB = 32
LANES = 128
PACK = 4
VMEM_LIMIT = 48 * 1024 * 1024
VMEM = pl.BlockSpec(memory_space=pltpu.VMEM)


def dft_values():
    times = np.arange(NFFT)
    freqs = np.arange(NF)
    phases = (freqs[:, None] * times[None, :] % NFFT) * (2.0 * math.pi / NFFT)
    window = 0.5 - 0.5 * np.cos(times * (2.0 * math.pi / NFFT))
    weighted = window / np.sqrt(np.sum(window * window))
    return np.cos(phases) * weighted, -np.sin(phases) * weighted


def split_table(table):
    high = table.astype(jnp.bfloat16)
    low = (table - high.astype(np.float64)).astype(jnp.bfloat16)
    return high, low


def dft_operand():
    real, imag = dft_values()
    high, low = split_table(np.concatenate([real, imag], axis=0))
    return np.concatenate([high, high, low], axis=1)


def mode_tables():
    real, imag = dft_values()
    order = np.concatenate([np.arange(0, NF, 2), np.arange(1, NF, 2)])
    real, imag = real[order].T, imag[order].T
    first = np.concatenate([real, imag], axis=1)
    second = np.concatenate([-imag, real], axis=1)
    return np.stack([first, second]).astype(np.float32)


def split(value):
    high = value.astype(jnp.bfloat16)
    low = (value - high.astype(jnp.float32)).astype(jnp.bfloat16)
    return high, low


def gram_kernel(total_rows, x_ref, w_ref, dft_ref, out_ref, high_ref, low_ref, spec_ref):
    times, cols = x_ref.shape
    halves = times // HALF
    col_tiles = cols // LANES

    def add_half(i, acc):
        return acc + x_ref[pl.ds(pl.multiple_of(i * HALF, HALF), HALF), :]

    acc = lax.fori_loop(0, halves, add_half, jnp.zeros((HALF, cols), jnp.float32), unroll=3)
    mean = jnp.sum(acc, axis=0, keepdims=True) / times
    scale = jnp.sqrt(w_ref[...] / total_rows)

    def center(i, carry):
        rows = pl.ds(pl.multiple_of(i * HALF, HALF), HALF)
        high, low = split((x_ref[rows, :] - mean) * scale)
        high_ref[rows, :] = high
        low_ref[rows, :] = low
        return carry

    lax.fori_loop(0, halves, center, 0, unroll=3)
    pad = high_ref.shape[0] - times
    if pad:
        high_ref[pl.ds(times, pad), :] = jnp.zeros((pad, cols), jnp.bfloat16)
        low_ref[pl.ds(times, pad), :] = jnp.zeros((pad, cols), jnp.bfloat16)

    for b in range(NB):
        rows = pl.ds(b * HALF, NFFT)
        high = high_ref[rows, :]
        block = jnp.concatenate([high, low_ref[rows, :], high], axis=0)
        spectrum = jnp.dot(dft_ref[...], block, preferred_element_type=jnp.float32)
        for c in range(col_tiles):
            spec_ref[c, pl.ds(b, 2 * NF, stride=NB), :] = spectrum[:, c * LANES : (c + 1) * LANES]

    row = lax.broadcasted_iota(jnp.int32, (NB, LANES), 0)
    lane = lax.broadcasted_iota(jnp.int32, (NB, LANES), 1)
    upper = row <= lane % NB
    left = lane[: NB // 2] < LANES // 2
    for g in range(NF // PACK):
        real_rows = pl.ds(g * LANES, LANES)
        imag_rows = pl.ds(NF * NB + g * LANES, LANES)
        real = jnp.concatenate([spec_ref[c, real_rows, :] for c in range(col_tiles)], axis=1)
        imag = jnp.concatenate([spec_ref[c, imag_rows, :] for c in range(col_tiles)], axis=1)
        real_h, real_l = split(real)
        imag_h, imag_l = split(imag)
        lhs = jnp.concatenate([real_h, imag_h, real_h, imag_h, real_l, imag_l], axis=1)
        same = jnp.concatenate([real_h, imag_h, real_l, imag_l, real_h, imag_h], axis=1)
        turned = jnp.concatenate([imag_h, -real_h, imag_l, -real_l, imag_h, -real_h], axis=1)
        product = lax.dot_general(
            lhs,
            jnp.concatenate([same, turned], axis=0),
            (((1,), (1,)), ((), ())),
            preferred_element_type=jnp.float32,
        )
        gram_real = jnp.zeros((NB, LANES), jnp.float32)
        gram_imag = jnp.zeros((NB, LANES), jnp.float32)
        for q in range(PACK):
            mine = lane // NB == q
            part = product[q * NB : (q + 1) * NB]
            gram_real = jnp.where(mine, part[:, :LANES], gram_real)
            gram_imag = jnp.where(mine, part[:, LANES:], gram_imag)
        packed = jnp.where(upper, gram_real, gram_imag)
        top = packed[: NB // 2]
        bottom = packed[NB // 2 :]
        out_ref[2 * g] = jnp.where(left, top, pltpu.roll(bottom, LANES // 2, 1))
        out_ref[2 * g + 1] = jnp.where(left, pltpu.roll(top, LANES // 2, 1), bottom)


def gram_parts(snapshots, weight_row, total_rows):
    times, cols = snapshots.shape
    padded = -(-times // 256) * 256
    return pl.pallas_call(
        functools.partial(gram_kernel, total_rows),
        out_shape=(
            jax.ShapeDtypeStruct((NF // 2, NB // 2, LANES), jnp.float32),
            jax.ShapeDtypeStruct((padded, cols), jnp.bfloat16),
            jax.ShapeDtypeStruct((padded, cols), jnp.bfloat16),
        ),
        in_specs=[VMEM] * 3,
        out_specs=(VMEM,) * 3,
        scratch_shapes=[pltpu.VMEM((cols // LANES, 2 * NF * NB, LANES), jnp.float32)],
        compiler_params=pltpu.CompilerParams(vmem_limit_bytes=VMEM_LIMIT),
        cost_estimate=pl.CostEstimate(
            flops=5_000_000_000, bytes_accessed=8_000_000, transcendentals=0
        ),
        name="gram_parts",
    )(snapshots, weight_row, jnp.asarray(dft_operand()))


def hermitian_pair(packed):
    square = jnp.concatenate([packed, pltpu.roll(packed, LANES // 2, 1)], axis=0)
    tall = jnp.concatenate([square] * (LANES // NB), axis=0).T
    row = lax.broadcasted_iota(jnp.int32, (NB, LANES), 0)
    lane = lax.broadcasted_iota(jnp.int32, (NB, LANES), 1)
    flipped = jnp.where(lane // NB == 0, tall[:NB], tall[NB : 2 * NB])
    col = lane % NB
    real = jnp.where(row <= col, square, flipped)
    imag = jnp.where(row > col, square, jnp.where(row < col, -flipped, 0.0))
    return real, imag, lane


def sum_kernel(n_copies, parts_ref, start_ref, response_ref, copies_ref):
    packed = jnp.sum(parts_ref[...], axis=0)
    for i in range(n_copies):
        copies_ref[i] = packed
    real, imag, lane = hermitian_pair(packed)
    start_real = start_ref[0]
    start_imag = start_ref[1]
    resp_real = jnp.sum(real * start_real + imag * start_imag, axis=0, keepdims=True)
    resp_imag = jnp.sum(real * start_imag - imag * start_real, axis=0, keepdims=True)
    power = resp_real * resp_real + resp_imag * resp_imag
    lane = lane[:1]
    first = jnp.sum(jnp.where(lane < NB, power, 0.0), axis=1, keepdims=True) / NB
    second = (
        jnp.sum(jnp.where((lane >= NB) & (lane < 2 * NB), power, 0.0), axis=1, keepdims=True) / NB
    )
    scaling = 1.0 / jnp.sqrt(jnp.where(lane < NB, first, second) + 1e-06)
    resp = jnp.where(
        lane < LANES // 2, resp_real * scaling, pltpu.roll(resp_imag * scaling, LANES // 2, 1)
    )
    response_ref[...] = jnp.broadcast_to(resp.reshape(1, 1, LANES), response_ref.shape)


def sum_parts(parts, start_pair, n_copies):
    n = parts.shape[0]
    return pl.pallas_call(
        functools.partial(sum_kernel, n_copies),
        out_shape=(
            jax.ShapeDtypeStruct((n, 1, LANES), jnp.float32),
            jax.ShapeDtypeStruct((n_copies,) + parts.shape[1:], jnp.float32),
        ),
        in_specs=[VMEM] * 2,
        out_specs=(VMEM,) * 2,
        compiler_params=pltpu.CompilerParams(vmem_limit_bytes=VMEM_LIMIT),
        name="sum_parts",
    )(parts, start_pair)


def unpack_kernel(packed_ref, out_ref):
    for i in range(packed_ref.shape[0]):
        real, imag, _ = hermitian_pair(packed_ref[i])
        for q in range(2):
            out_ref[2 * i + q, 0] = real[:, q * NB : (q + 1) * NB]
            out_ref[2 * i + q, 1] = imag[:, q * NB : (q + 1) * NB]


def unpack_gram(packed):
    pairs = packed.shape[0]
    return pl.pallas_call(
        unpack_kernel,
        out_shape=jax.ShapeDtypeStruct((2 * pairs, 2, NB, NB), jnp.float32),
        in_specs=[VMEM],
        out_specs=VMEM,
        compiler_params=pltpu.CompilerParams(vmem_limit_bytes=VMEM_LIMIT),
        name="unpack_gram",
    )(packed)


def modes_kernel(total_rows, times, high_ref, low_ref, w_ref, resp_ref, table_ref, out_ref, resp_t, a_ref):
    cols = high_ref.shape[1]
    padded = high_ref.shape[0]
    halves = times // HALF
    pairs = NF // 2
    tall = jnp.concatenate([resp_ref[...].reshape(pairs, LANES)] * (LANES // pairs), axis=0).T
    lane = lax.broadcasted_iota(jnp.int32, (NB, LANES), 1)
    turned = tall[:NB]
    for q in range(1, PACK):
        turned = jnp.where(lane // pairs == q, tall[q * NB : (q + 1) * NB], turned)
    swapped = pltpu.roll(turned, LANES // 2, 1)
    left = lane < LANES // 2
    resp_t[0] = jnp.where(left, turned, swapped)
    resp_t[1] = jnp.where(left, swapped, turned)
    for j in range(padded // HALF):
        value = jnp.zeros((HALF, LANES), jnp.float32)
        for block, start in ((j, 0), (j - 1, HALF)):
            if 0 <= block < NB:
                for part in range(2):
                    value += resp_t[part, pl.ds(block, 1), :] * table_ref[part, pl.ds(start, HALF), :]
        high, low = split(value)
        a_ref[0, pl.ds(j * HALF, HALF), :] = high
        a_ref[1, pl.ds(j * HALF, HALF), :] = low
    contract = (((0,), (0,)), ((), ()))
    dot = functools.partial(
        lax.dot_general, dimension_numbers=contract, preferred_element_type=jnp.float32
    )
    modes = (
        dot(a_ref[0], high_ref[...]) + dot(a_ref[0], low_ref[...]) + dot(a_ref[1], high_ref[...])
    )
    modes = modes * jnp.sqrt(total_rows / w_ref[...])
    for part in range(2):
        for parity in range(2):
            first = (2 * part + parity) * pairs
            for c in range(cols // LANES):
                out_ref[c, pl.ds(2 * parity + part, pairs, stride=4), :] = modes[
                    first : first + pairs, c * LANES : (c + 1) * LANES
                ]


def local_modes(high, low, weight_row, response, total_rows, times):
    padded, cols = high.shape
    return pl.pallas_call(
        functools.partial(modes_kernel, total_rows, times),
        out_shape=jax.ShapeDtypeStruct((cols // LANES, 2 * NF, LANES), jnp.float32),
        in_specs=[VMEM] * 5,
        out_specs=VMEM,
        scratch_shapes=[
            pltpu.VMEM((2, NB, LANES), jnp.float32),
            pltpu.VMEM((2, padded, LANES), jnp.bfloat16),
        ],
        compiler_params=pltpu.CompilerParams(vmem_limit_bytes=VMEM_LIMIT),
        name="local_modes",
    )(high, low, weight_row, response, jnp.asarray(mode_tables()))


def response_of(gram, start_vec):
    matvec = functools.partial(jnp.einsum, "fjk,fk->fj", precision=lax.Precision.HIGHEST)
    resp_real = matvec(gram[:, 0], start_vec[:, 0]) - matvec(gram[:, 1], start_vec[:, 1])
    resp_imag = matvec(gram[:, 0], start_vec[:, 1]) + matvec(gram[:, 1], start_vec[:, 0])
    scaling = 1.0 / jnp.sqrt(
        jnp.mean(resp_real * resp_real + resp_imag * resp_imag, axis=1, keepdims=True) + 1e-06
    )
    return jnp.stack([resp_real * scaling, resp_imag * scaling], axis=1)


def shards(n_pts, n_freq, snapshots, weight, start_vec):
    times, cols = snapshots.shape
    total_rows = weight.shape[0] * n_pts
    n_devices = n_pts * n_freq
    mine_count = NF // n_freq
    group = lax.axis_index("freq")
    place = lax.axis_index("pts")
    axes = ("freq", "pts")
    weight_row = lax.dynamic_slice_in_dim(weight, group * cols, cols, 0).reshape(1, cols)
    parts, high, low = gram_parts(snapshots, weight_row, float(total_rows))

    if n_devices * 2 == NF:
        first = (group * n_pts + place) * 2
        start_pair = lax.dynamic_slice_in_dim(start_vec, first, 2, 0)
        start_pair = jnp.transpose(start_pair, (1, 2, 0))[:, :, :, None]
        start_pair = jnp.broadcast_to(start_pair, (2, NB, 2, NB)).reshape(2, NB, 2 * NB)
        start_pair = jnp.concatenate([start_pair, start_pair], axis=2)
        got = lax.all_to_all(parts, axes, 0, 0, tiled=True)
        resp_copies, gram_copies = sum_parts(got, start_pair, n_pts)
        response = lax.all_to_all(resp_copies, axes, 0, 0, tiled=True)
        packed = lax.all_to_all(gram_copies, "pts", 0, 0, tiled=True)
        gram_mine = unpack_gram(packed)
    else:
        share = parts.reshape(n_devices, -1)
        share = jnp.sum(lax.all_to_all(share, axes, 0, 0, tiled=True), axis=0)
        packed = lax.all_gather(share, "pts", axis=0, tiled=True)
        gram_mine = unpack_gram(packed.reshape(mine_count // 2, NB // 2, LANES))
        start_mine = lax.dynamic_slice_in_dim(start_vec, group * mine_count, mine_count, 0)
        response = lax.all_gather(response_of(gram_mine, start_mine), "freq", axis=0, tiled=True)
        response = jnp.transpose(response.reshape(NF // 2, 2, 2, NB), (0, 2, 1, 3))
        response = response.reshape(NF // 2, 1, LANES)

    modes = local_modes(high, low, weight_row, response, float(total_rows), times)
    modes = modes.reshape(cols // LANES, n_freq, mine_count, 2, LANES)
    modes = lax.all_to_all(modes, "freq", 1, 1, tiled=True)
    modes = jnp.transpose(modes, (2, 3, 1, 0, 4)).reshape(mine_count, 2, n_freq * cols)
    return gram_mine, modes


def solution(mesh):
    placed = (P(None, ("pts", "freq")), P("pts"), P())
    return jax.shard_map(
        functools.partial(shards, mesh.shape["pts"], mesh.shape["freq"]),
        mesh=mesh,
        in_specs=placed,
        out_specs=(P("freq", None, None, None), P("freq", None, "pts")),
        check_vma=False,
    )
```

```python
import functools
import math

import jax
import jax.numpy as jnp
import numpy as np
from jax import lax
from jax.experimental import pallas as pl
from jax.experimental.pallas import tpu as pltpu
from jax.sharding import PartitionSpec as P

NFFT = 128
HALF = NFFT // 2
NF = 64
NB = 32
LANES = 128
PACK = 4
VMEM_LIMIT = 32 * 1024 * 1024
SMALL_LIMIT = 16 * 1024 * 1024
VMEM = pl.BlockSpec(memory_space=pltpu.VMEM)


def dft_values():
    times = np.arange(NFFT)
    freqs = np.arange(NF)
    phases = (freqs[:, None] * times[None, :] % NFFT) * (2.0 * math.pi / NFFT)
    window = 0.5 - 0.5 * np.cos(times * (2.0 * math.pi / NFFT))
    weighted = window / np.sqrt(np.sum(window * window))
    return np.cos(phases) * weighted, -np.sin(phases) * weighted


def split_table(table):
    high = table.astype(jnp.bfloat16)
    low = (table - high.astype(np.float64)).astype(jnp.bfloat16)
    return high, low


def dft_operand():
    real, imag = dft_values()
    high, low = split_table(np.concatenate([real, imag], axis=0))
    return np.block([[high, high], [low, np.zeros_like(low)]])


def mode_tables():
    real, imag = dft_values()
    order = np.concatenate([np.arange(0, NF, 2), np.arange(1, NF, 2)])
    real, imag = real[order].T, imag[order].T
    first = np.concatenate([real, imag], axis=1)
    second = np.concatenate([-imag, real], axis=1)
    return np.stack([first, second]).astype(np.float32)


def split(value):
    high = value.astype(jnp.bfloat16)
    low = (value - high.astype(jnp.float32)).astype(jnp.bfloat16)
    return high, low


def my_weights(w_ref, col_tiles):
    first = lax.axis_index("freq") * col_tiles
    return jnp.concatenate([w_ref[pl.ds(first + c, 1), :] for c in range(col_tiles)], axis=1)


def gram_kernel(
    total_rows, x_ref, w_ref, dft_ref, out_ref, high_ref, low_ref, spec_ref, z_ref, pack_ref, sems
):
    times, cols = x_ref.shape
    halves = times // HALF
    col_tiles = cols // LANES

    def add_half(i, acc):
        return acc + x_ref[pl.ds(pl.multiple_of(i * HALF, HALF), HALF), :]

    acc = lax.fori_loop(0, halves, add_half, jnp.zeros((HALF, cols), jnp.float32), unroll=3)
    mean = jnp.sum(acc, axis=0, keepdims=True) / times
    scale = jnp.sqrt(my_weights(w_ref, col_tiles) / total_rows)

    def center(i, carry):
        rows = pl.ds(pl.multiple_of(i * HALF, HALF), HALF)
        high, low = split((x_ref[rows, :] - mean) * scale)
        high_ref[rows, :] = high
        low_ref[rows, :] = low
        return carry

    lax.fori_loop(0, halves, center, 0, unroll=3)
    pad = high_ref.shape[0] - times
    if pad:
        high_ref[pl.ds(times, pad), :] = jnp.zeros((pad, cols), jnp.bfloat16)
        low_ref[pl.ds(times, pad), :] = jnp.zeros((pad, cols), jnp.bfloat16)

    def transform(b, carry):
        rows = pl.ds(pl.multiple_of(b * HALF, HALF), NFFT)
        block = jnp.concatenate([high_ref[rows, :], low_ref[rows, :]], axis=0)
        both = jnp.dot(dft_ref[...], block, preferred_element_type=jnp.float32)
        spectrum = both[: 2 * NF] + both[2 * NF :]
        for o in range(2 * NF // 8):
            for c in range(col_tiles):
                spec_ref[c, o, pl.ds(b, 8, stride=NB + 1), :] = spectrum[
                    8 * o : 8 * o + 8, c * LANES : (c + 1) * LANES
                ]
        return carry

    lax.fori_loop(0, NB, transform, 0, unroll=2)

    row = lax.broadcasted_iota(jnp.int32, (NB, LANES), 0)
    lane = lax.broadcasted_iota(jnp.int32, (NB, LANES), 1)
    upper = row <= lane % NB
    left = lane[: NB // 2] < LANES // 2
    octets = NF // 8
    contract = (((1,), (1,)), ((), ()))

    def copy_out(o):
        return pltpu.make_async_copy(
            pack_ref.at[pl.ds(4 * o, 4)], out_ref.at[pl.ds(4 * o, 4)], sems.at[o]
        )

    def correlate(o, carry):
        for half in range(2):
            for part in range(2):
                for q in range(PACK):
                    first = (NB + 1) * (PACK * half + q)
                    for c in range(col_tiles):
                        value = spec_ref[c, o + octets * part, pl.ds(first, NB), :]
                        high, low = split(value)
                        rows = pl.ds(part * LANES + q * NB, NB)
                        lanes = pl.ds(c * LANES, LANES)
                        z_ref[half, 0, rows, lanes] = high
                        z_ref[half, 1, rows, lanes] = low
            high = z_ref[half, 0]
            low = z_ref[half, 1]
            product = lax.dot_general(
                jnp.concatenate([high, high, low], axis=1),
                jnp.concatenate([high, low, high], axis=1),
                contract,
                preferred_element_type=jnp.float32,
            )
            gram_real = jnp.zeros((NB, LANES), jnp.float32)
            gram_imag = jnp.zeros((NB, LANES), jnp.float32)
            for q in range(PACK):
                mine = lane // NB == q
                real = product[q * NB : (q + 1) * NB]
                imag = product[LANES + q * NB : LANES + (q + 1) * NB]
                gram_real = jnp.where(mine, real[:, :LANES] + imag[:, LANES:], gram_real)
                gram_imag = jnp.where(mine, real[:, LANES:] - imag[:, :LANES], gram_imag)
            packed = jnp.where(upper, gram_real, gram_imag)
            top = packed[: NB // 2]
            bottom = packed[NB // 2 :]
            pair = 4 * o + 2 * half
            pack_ref[pair] = jnp.where(left, top, pltpu.roll(bottom, LANES // 2, 1))
            pack_ref[pair + 1] = jnp.where(left, pltpu.roll(top, LANES // 2, 1), bottom)
        copy_out(o).start()
        return carry

    lax.fori_loop(0, octets, correlate, 0)
    for o in range(octets):
        copy_out(o).wait()


def gram_parts(snapshots, weight_rows, total_rows):
    times, cols = snapshots.shape
    padded = -(-times // 256) * 256
    return pl.pallas_call(
        functools.partial(gram_kernel, total_rows),
        out_shape=(
            jax.ShapeDtypeStruct((NF // 2, NB // 2, LANES), jnp.float32),
            jax.ShapeDtypeStruct((padded, cols), jnp.bfloat16),
            jax.ShapeDtypeStruct((padded, cols), jnp.bfloat16),
        ),
        in_specs=[VMEM] * 3,
        out_specs=(pl.BlockSpec(memory_space=pl.ANY), VMEM, VMEM),
        scratch_shapes=[
            pltpu.VMEM((cols // LANES, 2 * NF // 8, 8 * (NB + 1), LANES), jnp.float32),
            pltpu.VMEM((2, 2, 2 * LANES, cols), jnp.bfloat16),
            pltpu.VMEM((NF // 2, NB // 2, LANES), jnp.float32),
            pltpu.SemaphoreType.DMA((NF // 8,)),
        ],
        compiler_params=pltpu.CompilerParams(vmem_limit_bytes=VMEM_LIMIT),
        cost_estimate=pl.CostEstimate(
            flops=5_000_000_000, bytes_accessed=8_000_000, transcendentals=0
        ),
        name="gram_parts",
    )(snapshots, weight_rows, jnp.asarray(dft_operand()))


def hermitian_pair(packed):
    square = jnp.concatenate([packed, pltpu.roll(packed, LANES // 2, 1)], axis=0)
    tall = jnp.concatenate([square] * (LANES // NB), axis=0).T
    row = lax.broadcasted_iota(jnp.int32, (NB, LANES), 0)
    lane = lax.broadcasted_iota(jnp.int32, (NB, LANES), 1)
    flipped = jnp.where(lane // NB == 0, tall[:NB], tall[NB : 2 * NB])
    col = lane % NB
    real = jnp.where(row <= col, square, flipped)
    imag = jnp.where(row > col, square, jnp.where(row < col, -flipped, 0.0))
    return real, imag, lane


def sum_kernel(parts_ref, start_ref, response_ref, packed_ref):
    packed = jnp.sum(parts_ref[...], axis=0)
    packed_ref[...] = packed
    real, imag, lane = hermitian_pair(packed)
    start_real = start_ref[0]
    start_imag = start_ref[1]
    resp_real = jnp.sum(real * start_real + imag * start_imag, axis=0, keepdims=True)
    resp_imag = jnp.sum(real * start_imag - imag * start_real, axis=0, keepdims=True)
    power = resp_real * resp_real + resp_imag * resp_imag
    lane = lane[:1]
    first = jnp.sum(jnp.where(lane < NB, power, 0.0), axis=1, keepdims=True) / NB
    second = (
        jnp.sum(jnp.where((lane >= NB) & (lane < 2 * NB), power, 0.0), axis=1, keepdims=True) / NB
    )
    scaling = 1.0 / jnp.sqrt(jnp.where(lane < NB, first, second) + 1e-06)
    resp = jnp.where(
        lane < LANES // 2, resp_real * scaling, pltpu.roll(resp_imag * scaling, LANES // 2, 1)
    )
    response_ref[...] = resp


def sum_parts(parts, start_pair):
    return pl.pallas_call(
        sum_kernel,
        out_shape=(
            jax.ShapeDtypeStruct((1, LANES), jnp.float32),
            jax.ShapeDtypeStruct(parts.shape[1:], jnp.float32),
        ),
        in_specs=[VMEM] * 2,
        out_specs=(VMEM,) * 2,
        compiler_params=pltpu.CompilerParams(vmem_limit_bytes=SMALL_LIMIT),
        name="sum_parts",
    )(parts, start_pair)


def unpack_kernel(packed_ref, out_ref):
    for i in range(packed_ref.shape[0]):
        real, imag, _ = hermitian_pair(packed_ref[i])
        for q in range(2):
            out_ref[2 * i + q, 0] = real[:, q * NB : (q + 1) * NB]
            out_ref[2 * i + q, 1] = imag[:, q * NB : (q + 1) * NB]


def unpack_gram(packed):
    pairs = packed.shape[0]
    return pl.pallas_call(
        unpack_kernel,
        out_shape=jax.ShapeDtypeStruct((2 * pairs, 2, NB, NB), jnp.float32),
        in_specs=[VMEM],
        out_specs=VMEM,
        compiler_params=pltpu.CompilerParams(vmem_limit_bytes=SMALL_LIMIT),
        name="unpack_gram",
    )(packed)


def modes_kernel(total_rows, times, relative, high_ref, low_ref, w_ref, resp_ref, table_ref, out_ref, resp_t, a_ref):
    cols = high_ref.shape[1]
    padded = high_ref.shape[0]
    halves = times // HALF
    pairs = NF // 2
    tall = jnp.concatenate([resp_ref[...]] * (LANES // pairs), axis=0).T
    lane = lax.broadcasted_iota(jnp.int32, (NB, LANES), 1)
    turned = tall[:NB]
    for q in range(1, PACK):
        turned = jnp.where(lane // pairs == q, tall[q * NB : (q + 1) * NB], turned)
    swapped = pltpu.roll(turned, LANES // 2, 1)
    left = lane < LANES // 2
    resp_t[0] = jnp.where(left, turned, swapped)
    resp_t[1] = jnp.where(left, swapped, turned)
    for j in range(padded // HALF):
        value = jnp.zeros((HALF, LANES), jnp.float32)
        for block, start in ((j, 0), (j - 1, HALF)):
            if 0 <= block < NB:
                for part in range(2):
                    value += resp_t[part, pl.ds(block, 1), :] * table_ref[part, pl.ds(start, HALF), :]
        high, low = split(value)
        a_ref[0, pl.ds(j * HALF, HALF), :] = high
        a_ref[1, pl.ds(j * HALF, HALF), :] = low
    contract = (((0,), (0,)), ((), ()))
    dot = functools.partial(
        lax.dot_general, dimension_numbers=contract, preferred_element_type=jnp.float32
    )
    modes = (
        dot(a_ref[0], high_ref[...]) + dot(a_ref[0], low_ref[...]) + dot(a_ref[1], high_ref[...])
    )
    modes = modes * jnp.sqrt(total_rows / my_weights(w_ref, cols // LANES))
    n_freq = out_ref.shape[0]
    mine = pairs // n_freq
    group = lax.axis_index("freq")
    for part in range(2):
        for parity in range(2):
            for f in range(n_freq):
                first = (2 * part + parity) * pairs + f * mine
                slot = lax.rem(f + n_freq - group, n_freq) if relative else f
                for c in range(cols // LANES):
                    out_ref[slot, c, pl.ds(2 * parity + part, mine, stride=4), :] = modes[
                        first : first + mine, c * LANES : (c + 1) * LANES
                    ]


def local_modes(high, low, weight_rows, response, total_rows, times, n_freq, relative):
    padded, cols = high.shape
    return pl.pallas_call(
        functools.partial(modes_kernel, total_rows, times, relative),
        out_shape=jax.ShapeDtypeStruct(
            (n_freq, cols // LANES, 2 * NF // n_freq, LANES), jnp.float32
        ),
        in_specs=[VMEM] * 5,
        out_specs=VMEM,
        scratch_shapes=[
            pltpu.VMEM((2, NB, LANES), jnp.float32),
            pltpu.VMEM((2, padded, LANES), jnp.bfloat16),
        ],
        compiler_params=pltpu.CompilerParams(vmem_limit_bytes=SMALL_LIMIT),
        name="local_modes",
    )(high, low, weight_rows, response, jnp.asarray(mode_tables()))


def response_of(gram, start_vec):
    matvec = functools.partial(jnp.einsum, "fjk,fk->fj", precision=lax.Precision.HIGHEST)
    resp_real = matvec(gram[:, 0], start_vec[:, 0]) - matvec(gram[:, 1], start_vec[:, 1])
    resp_imag = matvec(gram[:, 0], start_vec[:, 1]) + matvec(gram[:, 1], start_vec[:, 0])
    scaling = 1.0 / jnp.sqrt(
        jnp.mean(resp_real * resp_real + resp_imag * resp_imag, axis=1, keepdims=True) + 1e-06
    )
    return jnp.stack([resp_real * scaling, resp_imag * scaling], axis=1)


def shards(n_pts, n_freq, snapshots, weight, start_vec):
    times, cols = snapshots.shape
    total_rows = weight.shape[0] * n_pts
    n_devices = n_pts * n_freq
    mine_count = NF // n_freq
    group = lax.axis_index("freq")
    place = lax.axis_index("pts")
    axes = ("freq", "pts")
    weight_rows = weight.reshape(-1, LANES)
    parts, high, low = gram_parts(snapshots, weight_rows, float(total_rows))

    if n_devices * 2 == NF:
        first = (group * n_pts + place) * 2
        start_pair = lax.dynamic_slice_in_dim(start_vec, first, 2, 0)
        start_pair = jnp.transpose(start_pair, (1, 2, 0))[:, :, :, None]
        start_pair = jnp.broadcast_to(start_pair, (2, NB, 2, NB)).reshape(2, NB, 2 * NB)
        start_pair = jnp.concatenate([start_pair, start_pair], axis=2)
        got = lax.all_to_all(parts, axes, 0, 0, tiled=True)
        response, packed = sum_parts(got, start_pair)
        response = lax.all_gather(response, axes, axis=0, tiled=True)
        packed = lax.all_gather(packed, "pts", axis=0)
        gram_mine = unpack_gram(packed)
    else:
        share = parts.reshape(n_devices, -1)
        share = jnp.sum(lax.all_to_all(share, axes, 0, 0, tiled=True), axis=0)
        packed = lax.all_gather(share, "pts", axis=0, tiled=True)
        gram_mine = unpack_gram(packed.reshape(mine_count // 2, NB // 2, LANES))
        start_mine = lax.dynamic_slice_in_dim(start_vec, group * mine_count, mine_count, 0)
        response = lax.all_gather(response_of(gram_mine, start_mine), "freq", axis=0, tiled=True)
        response = jnp.transpose(response.reshape(NF // 2, 2, 2, NB), (0, 2, 1, 3))
        response = response.reshape(NF // 2, LANES)

    modes = local_modes(
        high, low, weight_rows, response, float(total_rows), times, n_freq, n_freq == 2
    )
    if n_freq == 2:
        kept = modes[0]
        got = lax.ppermute(modes[1], "freq", [(0, 1), (1, 0)])
        modes = jnp.stack(
            [jnp.where(group == 0, kept, got), jnp.where(group == 0, got, kept)]
        )
    else:
        modes = lax.all_to_all(modes, "freq", 0, 0, tiled=True)
    modes = modes.reshape(n_freq, cols // LANES, mine_count, 2, LANES)
    modes = jnp.transpose(modes, (2, 3, 0, 1, 4)).reshape(mine_count, 2, n_freq * cols)
    return gram_mine, modes


def solution(mesh):
    placed = (P(None, ("pts", "freq")), P("pts"), P())
    return jax.shard_map(
        functools.partial(shards, mesh.shape["pts"], mesh.shape["freq"]),
        mesh=mesh,
        in_specs=placed,
        out_specs=(P("freq", None, None, None), P("freq", None, "pts")),
        check_vma=False,
    )
```

```python
import functools
import math

import jax
import jax.numpy as jnp
import numpy as np
from jax import lax
from jax.experimental import pallas as pl
from jax.experimental.pallas import tpu as pltpu
from jax.sharding import PartitionSpec as P

NFFT = 128
HALF = NFFT // 2
NF = 64
NB = 32
LANES = 128
PACK = 4
VMEM_LIMIT = 56 * 1024 * 1024
SMALL_LIMIT = 16 * 1024 * 1024
VMEM = pl.BlockSpec(memory_space=pltpu.VMEM)


def dft_values():
    times = np.arange(NFFT)
    freqs = np.arange(NF)
    phases = (freqs[:, None] * times[None, :] % NFFT) * (2.0 * math.pi / NFFT)
    window = 0.5 - 0.5 * np.cos(times * (2.0 * math.pi / NFFT))
    weighted = window / np.sqrt(np.sum(window * window))
    return np.cos(phases) * weighted, -np.sin(phases) * weighted


def split_table(table):
    high = table.astype(jnp.bfloat16)
    low = (table - high.astype(np.float64)).astype(jnp.bfloat16)
    return high, low


def dft_operand():
    real, imag = dft_values()
    high, low = split_table(np.concatenate([real, imag], axis=0))
    return np.block([[high, high], [low, np.zeros_like(low)]])


def mode_tables():
    real, imag = dft_values()
    order = np.concatenate([np.arange(0, NF, 2), np.arange(1, NF, 2)])
    real, imag = real[order].T, imag[order].T
    first = np.concatenate([real, imag], axis=1)
    second = np.concatenate([-imag, real], axis=1)
    return np.stack([first, second]).astype(np.float32)


def split(value):
    high = value.astype(jnp.bfloat16)
    low = (value - high.astype(jnp.float32)).astype(jnp.bfloat16)
    return high, low


def load_weights(w_ref, col_tiles):
    first = lax.axis_index("freq") * col_tiles
    return jnp.concatenate([w_ref[pl.ds(first + c, 1), :] for c in range(col_tiles)], axis=1)


def near_index():
    return lax.axis_index("freq") * 2 + lax.rem(lax.axis_index("pts"), 2)


def far_index():
    return lax.div(lax.axis_index("pts"), 2)


def gram_kernel(
    total_rows,
    chunks,
    x_hbm,
    w_hbm,
    dft_hbm,
    *refs,
):
    out_refs = refs[:chunks]
    (high_hbm, low_hbm, x_ref, w_ref, dft_ref, high_ref, low_ref, spec_ref, z_ref, pack_ref) = refs[
        chunks:-2
    ]
    in_sems, out_sems = refs[-2:]
    times, cols = x_ref.shape
    halves = times // HALF
    col_tiles = cols // LANES
    pieces = in_sems.shape[0] - 2
    piece = times // pieces

    def fetch(i):
        rows = pl.ds(i * piece, piece)
        return pltpu.make_async_copy(x_hbm.at[rows], x_ref.at[rows], in_sems.at[i])

    fetch_w = pltpu.make_async_copy(w_hbm, w_ref, in_sems.at[pieces])
    fetch_dft = pltpu.make_async_copy(dft_hbm, dft_ref, in_sems.at[pieces + 1])
    for i in range(pieces):
        fetch(i).start()
    fetch_w.start()
    fetch_dft.start()

    acc = jnp.zeros((HALF, cols), jnp.float32)
    for i in range(pieces):
        fetch(i).wait()
        for h in range(piece // HALF):
            acc = acc + x_ref[pl.ds(i * piece + h * HALF, HALF), :]
    mean = jnp.sum(acc, axis=0, keepdims=True) / times
    fetch_w.wait()
    scale = jnp.sqrt(load_weights(w_ref, col_tiles) / (2.0 * total_rows))

    def center(i, carry):
        rows = pl.ds(pl.multiple_of(i * HALF, HALF), HALF)
        high, low = split((x_ref[rows, :] - mean) * scale)
        high_ref[rows, :] = high
        low_ref[rows, :] = low
        return carry

    lax.fori_loop(0, halves, center, 0, unroll=3)
    save_high = pltpu.make_async_copy(high_ref, high_hbm, out_sems.at[0])
    save_low = pltpu.make_async_copy(low_ref, low_hbm, out_sems.at[1])
    save_high.start()
    save_low.start()
    fetch_dft.wait()

    def transform(i, carry):
        blocks = []
        for s in range(2):
            rows = pl.ds(pl.multiple_of((2 * i + s) * HALF, HALF), NFFT)
            blocks.append(jnp.concatenate([high_ref[rows, :], low_ref[rows, :]], axis=0))
        both = jnp.dot(
            dft_ref[...], jnp.concatenate(blocks, axis=1), preferred_element_type=jnp.float32
        )
        spectrum = both[: 2 * NF] + both[2 * NF :]
        for s in range(2):
            for o in range(2 * NF // 8):
                for c in range(col_tiles):
                    first = s * cols + c * LANES
                    spec_ref[c, o, pl.ds(2 * i + s, 8, stride=NB + 1), :] = spectrum[
                        8 * o : 8 * o + 8, first : first + LANES
                    ]
        return carry

    lax.fori_loop(0, NB // 2, transform, 0, unroll=2)

    row = lax.broadcasted_iota(jnp.int32, (NB, LANES), 0)
    lane = lax.broadcasted_iota(jnp.int32, (NB, LANES), 1)
    upper = row <= lane % NB
    lower = row >= lane % NB
    left = lane[: NB // 2] < LANES // 2
    octets = NF // 8
    contract = (((1,), (1,)), ((), ()))

    def correlate(o, carry):
        direct = []
        flipped = []
        for half in range(2):
            for part in range(2):
                for q in range(PACK):
                    first = (NB + 1) * (PACK * half + q)
                    for c in range(col_tiles):
                        value = spec_ref[c, o + octets * part, pl.ds(first, NB), :]
                        high = value.astype(jnp.bfloat16)
                        low = (2.0 * (value - high.astype(jnp.float32))).astype(jnp.bfloat16)
                        rows = pl.ds(part * LANES + q * NB, NB)
                        z_ref[half, rows, pl.ds(c * LANES, LANES)] = high
                        z_ref[half, rows, pl.ds(cols + c * LANES, LANES)] = low
            high = z_ref[half, :, pl.ds(0, cols)]
            product = lax.dot_general(
                jnp.concatenate([high, high], axis=1),
                z_ref[half],
                contract,
                preferred_element_type=jnp.float32,
            )
            gram_real = jnp.zeros((NB, LANES), jnp.float32)
            gram_imag = jnp.zeros((NB, LANES), jnp.float32)
            for q in range(PACK):
                mine = lane // NB == q
                real = product[q * NB : (q + 1) * NB]
                imag = product[LANES + q * NB : LANES + (q + 1) * NB]
                gram_real = jnp.where(mine, real[:, :LANES] + imag[:, LANES:], gram_real)
                gram_imag = jnp.where(mine, real[:, LANES:] - imag[:, :LANES], gram_imag)
            direct.append(jnp.where(upper, gram_real, gram_imag))
            flipped.append(jnp.where(lower, gram_real, -gram_imag))
        turned = jnp.concatenate(flipped + flipped, axis=0).T
        for half in range(2):
            packed = direct[half]
            for q in range(PACK):
                block = turned[q * NB : (q + 1) * NB]
                shift = (q - half) % PACK
                if shift:
                    block = pltpu.roll(block, shift * NB, 1)
                packed = packed + jnp.where(lane // NB == q, block, 0.0)
            top = packed[: NB // 2]
            bottom = packed[NB // 2 :]
            pair = 4 * o + 2 * half
            pack_ref[pair] = jnp.where(left, top, pltpu.roll(bottom, LANES // 2, 1))
            pack_ref[pair + 1] = jnp.where(left, pltpu.roll(top, LANES // 2, 1), bottom)
        return carry

    lax.fori_loop(0, octets, correlate, 0)
    length = NF // 2 // chunks
    for m in range(chunks):
        source = near_index() ^ m if chunks > 1 else 0
        out_refs[m][...] = pack_ref[pl.ds(source * length, length)]
    save_high.wait()
    save_low.wait()


def gram_parts(snapshots, weight_rows, total_rows, chunks):
    times, cols = snapshots.shape
    dft = dft_operand()
    pieces = 11
    any_space = pl.BlockSpec(memory_space=pltpu.HBM)
    part = jax.ShapeDtypeStruct((NF // 2 // chunks, NB // 2, LANES), jnp.float32)
    saved = jax.ShapeDtypeStruct((times, cols), jnp.bfloat16)
    results = pl.pallas_call(
        functools.partial(gram_kernel, total_rows, chunks),
        out_shape=(part,) * chunks + (saved,) * 2,
        in_specs=[any_space] * 3,
        out_specs=(VMEM,) * chunks + (any_space,) * 2,
        scratch_shapes=[
            pltpu.VMEM((times, cols), jnp.float32),
            pltpu.VMEM(weight_rows.shape, jnp.float32),
            pltpu.VMEM(dft.shape, jnp.bfloat16),
            pltpu.VMEM((times, cols), jnp.bfloat16),
            pltpu.VMEM((times, cols), jnp.bfloat16),
            pltpu.VMEM((cols // LANES, 2 * NF // 8, 8 * (NB + 1), LANES), jnp.float32),
            pltpu.VMEM((2, 2 * LANES, 2 * cols), jnp.bfloat16),
            pltpu.VMEM((NF // 2, NB // 2, LANES), jnp.float32),
            pltpu.SemaphoreType.DMA((pieces + 2,)),
            pltpu.SemaphoreType.DMA((2,)),
        ],
        compiler_params=pltpu.CompilerParams(vmem_limit_bytes=VMEM_LIMIT),
        cost_estimate=pl.CostEstimate(
            flops=5_000_000_000, bytes_accessed=8_000_000, transcendentals=0
        ),
        name="gram_parts",
    )(snapshots, weight_rows, jnp.asarray(dft))
    return results[:chunks], results[chunks], results[chunks + 1]


def hermitian_pair(packed):
    square = jnp.concatenate([packed, pltpu.roll(packed, LANES // 2, 1)], axis=0)
    tall = jnp.concatenate([square] * (LANES // NB), axis=0).T
    row = lax.broadcasted_iota(jnp.int32, (NB, LANES), 0)
    lane = lax.broadcasted_iota(jnp.int32, (NB, LANES), 1)
    flipped = jnp.where(lane // NB == 0, tall[:NB], tall[NB : 2 * NB])
    col = lane % NB
    real = jnp.where(row <= col, square, flipped)
    imag = jnp.where(row > col, square, jnp.where(row < col, -flipped, 0.0))
    return real, imag, lane


def small_call(kernel, name, out_shape, scratch_shapes=(), limit=SMALL_LIMIT):
    def call(*args):
        return pl.pallas_call(
            kernel,
            out_shape=out_shape,
            in_specs=[VMEM] * len(args),
            out_specs=VMEM if isinstance(out_shape, jax.ShapeDtypeStruct) else (VMEM,) * len(out_shape),
            scratch_shapes=list(scratch_shapes),
            compiler_params=pltpu.CompilerParams(vmem_limit_bytes=limit),
            name=name,
        )(*args)

    return call


def floats(*shape):
    return jax.ShapeDtypeStruct(shape, jnp.float32)


def near_sum_kernel(*refs):
    parts, outs, sum_ref = refs[:4], refs[4:-1], refs[-1]
    sum_ref[...] = (parts[0][...] + parts[1][...]) + (parts[2][...] + parts[3][...])
    for n, out in enumerate(outs):
        out[...] = sum_ref[far_index() ^ n]


def far_sum_kernel(*refs):
    parts, start_ref, out_ref = refs[:-2], refs[-2], refs[-1]
    packed = parts[0][...]
    for part in parts[1:]:
        packed = packed + part[...]
    out_ref[pl.ds(0, NB // 2), :] = packed
    real, imag, lane = hermitian_pair(packed)
    start_real = start_ref[0]
    start_imag = start_ref[1]
    resp_real = jnp.sum(real * start_real + imag * start_imag, axis=0, keepdims=True)
    resp_imag = jnp.sum(real * start_imag - imag * start_real, axis=0, keepdims=True)
    power = resp_real * resp_real + resp_imag * resp_imag
    lane = lane[:1]
    first = jnp.sum(jnp.where(lane < NB, power, 0.0), axis=1, keepdims=True) / NB
    second = (
        jnp.sum(jnp.where((lane >= NB) & (lane < 2 * NB), power, 0.0), axis=1, keepdims=True) / NB
    )
    scaling = 1.0 / jnp.sqrt(jnp.where(lane < NB, first, second) + 1e-06)
    resp = jnp.where(
        lane < LANES // 2, resp_real * scaling, pltpu.roll(resp_imag * scaling, LANES // 2, 1)
    )
    out_ref[pl.ds(NB // 2, 8), :] = jnp.broadcast_to(resp, (8, LANES))


def far_join_kernel(*refs):
    parts, resp_ref, packed_ref = refs[:-2], refs[-2], refs[-1]
    for n, part in enumerate(parts):
        place = far_index() ^ n
        resp_ref[pl.ds(place, 1), :] = part[pl.ds(NB // 2, 1), :]
        packed_ref[place] = part[pl.ds(0, NB // 2), :]


def unpack_kernel(*refs):
    parts, out_ref = refs[:-1], refs[-1]
    own = lax.rem(lax.axis_index("pts"), 2)
    count = parts[0].shape[0]
    for m, part in enumerate(parts):
        first = (own ^ m) * 2 * count if len(parts) > 1 else 0
        for i in range(count):
            real, imag, _ = hermitian_pair(part[i])
            for q in range(2):
                out_ref[first + 2 * i + q, 0] = real[:, q * NB : (q + 1) * NB]
                out_ref[first + 2 * i + q, 1] = imag[:, q * NB : (q + 1) * NB]


def unpack_gram(*parts):
    pairs = sum(part.shape[0] for part in parts)
    return small_call(unpack_kernel, "unpack_gram", floats(2 * pairs, 2, NB, NB))(*parts)


def modes_kernel(total_rows, n_resp, *refs):
    high_hbm, low_hbm, w_ref, table_ref = refs[:4]
    resp_refs = refs[4 : 4 + n_resp]
    out_ref, resp_ref, resp_t, a_ref, x_ref, sems = refs[4 + n_resp :]
    times, cols = high_hbm.shape
    padded = x_ref.shape[1]
    pairs = NF // 2
    fetches = [
        pltpu.make_async_copy(source, x_ref.at[i, pl.ds(0, times)], sems.at[i])
        for i, source in enumerate((high_hbm, low_hbm))
    ]
    for fetch in fetches:
        fetch.start()
    if padded > times:
        pad = pl.ds(times, padded - times)
        x_ref[0, pad, :] = jnp.zeros((padded - times, cols), jnp.bfloat16)
        x_ref[1, pad, :] = jnp.zeros((padded - times, cols), jnp.bfloat16)
    count = pairs // n_resp
    for m, part in enumerate(resp_refs):
        place = (near_index() ^ m) * count if n_resp > 1 else 0
        resp_ref[pl.ds(place, count), :] = part[...]
    tall = jnp.concatenate([resp_ref[...]] * (LANES // pairs), axis=0).T
    lane = lax.broadcasted_iota(jnp.int32, (NB, LANES), 1)
    turned = tall[:NB]
    for q in range(1, PACK):
        turned = jnp.where(lane // pairs == q, tall[q * NB : (q + 1) * NB], turned)
    swapped = pltpu.roll(turned, LANES // 2, 1)
    left = lane < LANES // 2
    resp_t[0] = jnp.where(left, turned, swapped)
    resp_t[1] = jnp.where(left, swapped, turned)
    for j in range(padded // HALF):
        value = jnp.zeros((HALF, LANES), jnp.float32)
        for block, start in ((j, 0), (j - 1, HALF)):
            if 0 <= block < NB:
                for part in range(2):
                    value += resp_t[part, pl.ds(block, 1), :] * table_ref[part, pl.ds(start, HALF), :]
        high, low = split(value)
        a_ref[0, pl.ds(j * HALF, HALF), :] = high
        a_ref[1, pl.ds(j * HALF, HALF), :] = low
    dot = functools.partial(
        lax.dot_general,
        dimension_numbers=(((0,), (0,)), ((), ())),
        preferred_element_type=jnp.float32,
    )
    for fetch in fetches:
        fetch.wait()
    modes = dot(a_ref[0], x_ref[0]) + dot(a_ref[0], x_ref[1]) + dot(a_ref[1], x_ref[0])
    modes = modes * jnp.sqrt(2.0 * total_rows / load_weights(w_ref, cols // LANES))
    n_freq = out_ref.shape[0]
    mine = pairs // n_freq
    group = lax.axis_index("freq")
    for part in range(2):
        for parity in range(2):
            for f in range(n_freq):
                first = (2 * part + parity) * pairs + f * mine
                slot = f ^ group if n_freq == 2 else f
                for c in range(cols // LANES):
                    out_ref[slot, 2 * c + part, pl.ds(parity, mine, stride=2), :] = modes[
                        first : first + mine, c * LANES : (c + 1) * LANES
                    ]


def local_modes(high, low, weight_rows, responses, total_rows, n_freq):
    times, cols = high.shape
    padded = -(-times // 256) * 256
    any_space = pl.BlockSpec(memory_space=pltpu.HBM)
    n_resp = len(responses)
    return pl.pallas_call(
        functools.partial(modes_kernel, total_rows, n_resp),
        out_shape=floats(n_freq, 2 * cols // LANES, NF // n_freq, LANES),
        in_specs=[any_space] * 2 + [VMEM] * (2 + n_resp),
        out_specs=VMEM,
        scratch_shapes=[
            pltpu.VMEM((NF // 2, LANES), jnp.float32),
            pltpu.VMEM((2, NB, LANES), jnp.float32),
            pltpu.VMEM((2, padded, LANES), jnp.bfloat16),
            pltpu.VMEM((2, padded, cols), jnp.bfloat16),
            pltpu.SemaphoreType.DMA((2,)),
        ],
        compiler_params=pltpu.CompilerParams(vmem_limit_bytes=SMALL_LIMIT),
        name="local_modes",
    )(high, low, weight_rows, jnp.asarray(mode_tables()), *responses)


def join_kernel(kept_ref, got_ref, out_ref):
    tiles = got_ref.shape[0] // 2
    group = lax.axis_index("freq")
    for slot, ref in enumerate((kept_ref.at[0], got_ref)):
        for c in range(tiles):
            lanes = pl.ds(pl.multiple_of(((group ^ slot) * tiles + c) * LANES, LANES), LANES)
            for part in range(2):
                out_ref[:, part, lanes] = ref[2 * c + part]


def join_modes(kept, got):
    tiles, count, _ = got.shape
    return small_call(join_kernel, "join_modes", floats(count, 2, tiles * LANES))(kept, got)


def response_of(gram, start_vec):
    matvec = functools.partial(jnp.einsum, "fjk,fk->fj", precision=lax.Precision.HIGHEST)
    resp_real = matvec(gram[:, 0], start_vec[:, 0]) - matvec(gram[:, 1], start_vec[:, 1])
    resp_imag = matvec(gram[:, 0], start_vec[:, 1]) + matvec(gram[:, 1], start_vec[:, 0])
    scaling = 1.0 / jnp.sqrt(
        jnp.mean(resp_real * resp_real + resp_imag * resp_imag, axis=1, keepdims=True) + 1e-06
    )
    return jnp.stack([resp_real * scaling, resp_imag * scaling], axis=1)


def swap(value, mask, n_devices):
    return lax.ppermute(value, ("pts", "freq"), [(i, i ^ mask) for i in range(n_devices)])


def two_level_shards(n_devices, snapshots, weight, start_vec):
    total_rows = float(weight.shape[0] * 16)
    weight_rows = weight.reshape(-1, LANES)
    parts, high, low = gram_parts(snapshots, weight_rows, total_rows, 4)
    near = (0, 2, 1, 3)
    far = tuple(4 * n for n in range(8))

    first = (near_index() * 8 + far_index()) * 2
    start_pair = lax.dynamic_slice_in_dim(start_vec, first, 2, 0)
    start_pair = jnp.transpose(start_pair, (1, 2, 0))[:, :, :, None]
    start_pair = jnp.broadcast_to(start_pair, (2, NB, 2, NB)).reshape(2, NB, 2 * NB)
    start_pair = jnp.concatenate([start_pair, start_pair], axis=2)

    got = [parts[0]] + [swap(parts[m], near[m], n_devices) for m in range(1, 4)]
    parts = small_call(
        near_sum_kernel,
        "near_sum",
        (floats(NB // 2, LANES),) * 8,
        [pltpu.VMEM((8, NB // 2, LANES), jnp.float32)],
    )(*got)
    got = [parts[0]] + [swap(parts[n], far[n], n_devices) for n in range(1, 8)]
    own = small_call(far_sum_kernel, "far_sum", floats(NB // 2 + 8, LANES))(*got, start_pair)
    got = [own] + [swap(own, far[n], n_devices) for n in range(1, 8)]
    response, packed = small_call(
        far_join_kernel, "far_join", (floats(8, LANES), floats(8, NB // 2, LANES))
    )(*got)
    responses = [response] + [swap(response, near[m], n_devices) for m in range(1, 4)]
    gram_mine = unpack_gram(packed, swap(packed, near[1], n_devices))
    modes = local_modes(high, low, weight_rows, responses, total_rows, 2)
    modes = join_modes(modes, swap(modes[1], 1, n_devices))
    return gram_mine, modes


def shards(n_pts, n_freq, snapshots, weight, start_vec):
    cols = snapshots.shape[1]
    total_rows = float(weight.shape[0] * n_pts)
    n_devices = n_pts * n_freq
    mine_count = NF // n_freq
    group = lax.axis_index("freq")
    weight_rows = weight.reshape(-1, LANES)
    (parts,), high, low = gram_parts(snapshots, weight_rows, total_rows, 1)
    share = parts.reshape(n_devices, -1)
    share = jnp.sum(lax.all_to_all(share, ("freq", "pts"), 0, 0, tiled=True), axis=0)
    packed = lax.all_gather(share, "pts", axis=0, tiled=True)
    gram_mine = unpack_gram(packed.reshape(mine_count // 2, NB // 2, LANES))
    start_mine = lax.dynamic_slice_in_dim(start_vec, group * mine_count, mine_count, 0)
    response = lax.all_gather(response_of(gram_mine, start_mine), "freq", axis=0, tiled=True)
    response = jnp.transpose(response.reshape(NF // 2, 2, 2, NB), (0, 2, 1, 3))
    response = response.reshape(NF // 2, LANES)
    modes = local_modes(high, low, weight_rows, (response,), total_rows, n_freq)
    modes = lax.all_to_all(modes, "freq", 0, 0, tiled=True)
    modes = modes.reshape(n_freq, cols // LANES, 2, mine_count, LANES)
    modes = jnp.transpose(modes, (3, 2, 0, 1, 4)).reshape(mine_count, 2, n_freq * cols)
    return gram_mine, modes


def solution(mesh):
    n_pts, n_freq = mesh.shape["pts"], mesh.shape["freq"]
    if (n_pts, n_freq) == (16, 2):
        body = functools.partial(two_level_shards, n_pts * n_freq)
    else:
        body = functools.partial(shards, n_pts, n_freq)
    placed = (P(None, ("pts", "freq")), P("pts"), P())
    return jax.shard_map(
        body,
        mesh=mesh,
        in_specs=placed,
        out_specs=(P("freq", None, None, None), P("freq", None, "pts")),
        check_vma=False,
    )
```

```python
import functools
import math

import jax
import jax.numpy as jnp
import numpy as np
from jax import lax
from jax.experimental import pallas as pl
from jax.experimental.pallas import tpu as pltpu
from jax.sharding import PartitionSpec as P

NFFT = 128
HALF = NFFT // 2
NF = 64
NB = 32
LANES = 128
PACK = 4
VMEM_LIMIT = 56 * 1024 * 1024
SMALL_LIMIT = 16 * 1024 * 1024
VMEM = pl.BlockSpec(memory_space=pltpu.VMEM)


def dft_values():
    times = np.arange(NFFT)
    freqs = np.arange(NF)
    phases = (freqs[:, None] * times[None, :] % NFFT) * (2.0 * math.pi / NFFT)
    window = 0.5 - 0.5 * np.cos(times * (2.0 * math.pi / NFFT))
    weighted = window / np.sqrt(np.sum(window * window))
    return np.cos(phases) * weighted, -np.sin(phases) * weighted


def split_table(table):
    high = table.astype(jnp.bfloat16)
    low = (table - high.astype(np.float64)).astype(jnp.bfloat16)
    return high, low


def dft_operand():
    real, imag = dft_values()
    high, low = split_table(np.concatenate([real, imag], axis=0))
    return np.block([[high, high], [low, np.zeros_like(low)]])


def mode_tables():
    real, imag = dft_values()
    order = np.concatenate([np.arange(0, NF, 2), np.arange(1, NF, 2)])
    real, imag = real[order].T, imag[order].T
    first = np.concatenate([real, imag], axis=1)
    second = np.concatenate([-imag, real], axis=1)
    return np.stack([first, second]).astype(np.float32)


def split(value):
    high = value.astype(jnp.bfloat16)
    low = (value - high.astype(jnp.float32)).astype(jnp.bfloat16)
    return high, low


def load_weights(w_ref, col_tiles):
    first = lax.axis_index("freq") * col_tiles
    return jnp.concatenate([w_ref[pl.ds(first + c, 1), :] for c in range(col_tiles)], axis=1)


def flip_groups(groups, flipped):
    turned = flipped.T
    lane = lax.broadcasted_iota(jnp.int32, (NB, LANES), 1)
    out = []
    for g in range(PACK):
        total = groups[g]
        for q in range(PACK):
            block = turned[q * NB : (q + 1) * NB]
            if q != g:
                block = pltpu.roll(block, ((q - g) % PACK) * NB, 1)
            total = total + jnp.where(lane // NB == q, block, 0.0)
        out.append(total)
    return out


ROW_STEP = 3
FREQ_STEP = ROW_STEP * NB + 1


def gram_kernel(
    total_rows,
    places,
    x_hbm,
    w_hbm,
    dft_hbm,
    out_ref,
    high_hbm,
    low_hbm,
    x_ref,
    w_ref,
    dft_ref,
    high_ref,
    low_ref,
    spec_ref,
    z_even,
    z_odd,
    direct_ref,
    flipped_ref,
    in_sems,
    out_sems,
):
    times, cols = x_ref.shape
    halves = times // HALF
    col_tiles = cols // LANES
    pieces = in_sems.shape[0] - 2
    piece = times // pieces

    def fetch(i):
        rows = pl.ds(i * piece, piece)
        return pltpu.make_async_copy(x_hbm.at[rows], x_ref.at[rows], in_sems.at[i])

    fetch_w = pltpu.make_async_copy(w_hbm, w_ref, in_sems.at[pieces])
    fetch_dft = pltpu.make_async_copy(dft_hbm, dft_ref, in_sems.at[pieces + 1])
    for i in range(pieces):
        fetch(i).start()
    fetch_w.start()
    fetch_dft.start()

    acc = jnp.zeros((HALF, cols), jnp.float32)
    for i in range(pieces):
        fetch(i).wait()
        for h in range(piece // HALF):
            acc = acc + x_ref[pl.ds(i * piece + h * HALF, HALF), :]
    mean = jnp.sum(acc, axis=0, keepdims=True) / times
    fetch_w.wait()
    scale = jnp.sqrt(load_weights(w_ref, col_tiles) / (2.0 * total_rows))

    def center(i, carry):
        rows = pl.ds(pl.multiple_of(i * HALF, HALF), HALF)
        high, low = split((x_ref[rows, :] - mean) * scale)
        high_ref[rows, :] = high
        low_ref[rows, :] = low
        return carry

    lax.fori_loop(0, halves, center, 0, unroll=3)
    save_high = pltpu.make_async_copy(high_ref, high_hbm, out_sems.at[0])
    save_low = pltpu.make_async_copy(low_ref, low_hbm, out_sems.at[1])
    save_high.start()
    save_low.start()
    fetch_dft.wait()

    def transform(i, carry):
        blocks = []
        for s in range(2):
            rows = pl.ds(pl.multiple_of((2 * i + s) * HALF, HALF), NFFT)
            blocks.append(jnp.concatenate([high_ref[rows, :], low_ref[rows, :]], axis=0))
        both = jnp.dot(
            dft_ref[...], jnp.concatenate(blocks, axis=1), preferred_element_type=jnp.float32
        )
        spectrum = both[: 2 * NF] + both[2 * NF :]
        for s in range(2):
            for o in range(2 * NF // 8):
                for c in range(col_tiles):
                    first = s * cols + c * LANES
                    rows = pl.ds(ROW_STEP * (2 * i + s), 8, stride=FREQ_STEP)
                    spec_ref[c, o, rows, :] = spectrum[8 * o : 8 * o + 8, first : first + LANES]
        return carry

    lax.fori_loop(0, NB // 2, transform, 0, unroll=2)

    row = lax.broadcasted_iota(jnp.int32, (NB, LANES), 0)
    lane = lax.broadcasted_iota(jnp.int32, (NB, LANES), 1)
    upper = row <= lane % NB
    lower = row >= lane % NB
    octets = NF // 8

    def prepare(z_ref, octet, half):
        for part in range(2):
            for q in range(PACK):
                rows = pl.ds(FREQ_STEP * (PACK * half + q), NB, stride=ROW_STEP)
                own = pl.ds(part * LANES + q * NB, NB)
                for c in range(col_tiles):
                    value = spec_ref[c, octet + octets * part, rows, :]
                    high = value.astype(jnp.bfloat16)
                    low = (2.0 * (value - high.astype(jnp.float32))).astype(jnp.bfloat16)
                    z_ref[own, pl.ds(c * LANES, LANES)] = high
                    z_ref[own, pl.ds(cols + c * LANES, LANES)] = low

    def correlate(z_ref, group):
        high = z_ref[:, pl.ds(0, cols)]
        product = lax.dot_general(
            jnp.concatenate([high, high], axis=1),
            z_ref[...],
            (((1,), (1,)), ((), ())),
            preferred_element_type=jnp.float32,
        )
        gram_real = jnp.zeros((NB, LANES), jnp.float32)
        gram_imag = jnp.zeros((NB, LANES), jnp.float32)
        for q in range(PACK):
            mine = lane // NB == q
            real = product[q * NB : (q + 1) * NB]
            imag = product[LANES + q * NB : LANES + (q + 1) * NB]
            gram_real = jnp.where(mine, real[:, :LANES] + imag[:, LANES:], gram_real)
            gram_imag = jnp.where(mine, real[:, LANES:] - imag[:, :LANES], gram_imag)
        direct_ref[group] = jnp.where(upper, gram_real, gram_imag)
        flipped_ref[group] = jnp.where(lower, gram_real, -gram_imag)

    prepare(z_even, 0, 0)

    def step(o, carry):
        prepare(z_odd, o, 1)
        correlate(z_even, 2 * o)
        prepare(z_even, jnp.minimum(o + 1, octets - 1), 0)
        correlate(z_odd, 2 * o + 1)
        return carry

    lax.fori_loop(0, octets, step, 0)
    left = lane[: NB // 2] < LANES // 2
    for quad in range(NF // PACK // PACK):
        groups = [direct_ref[quad * PACK + g] for g in range(PACK)]
        flipped = flipped_ref[pl.ds(quad * PACK, PACK)].reshape(PACK * NB, LANES)
        for g, packed in enumerate(flip_groups(groups, flipped)):
            top = packed[: NB // 2]
            bottom = packed[NB // 2 :]
            pair = 2 * (quad * PACK + g)
            out_ref[places[pair]] = jnp.where(left, top, pltpu.roll(bottom, LANES // 2, 1))
            out_ref[places[pair + 1]] = jnp.where(left, pltpu.roll(top, LANES // 2, 1), bottom)
    save_high.wait()
    save_low.wait()


def gram_parts(snapshots, weight_rows, total_rows, places):
    times, cols = snapshots.shape
    dft = dft_operand()
    pieces = 11
    any_space = pl.BlockSpec(memory_space=pl.ANY)
    saved = jax.ShapeDtypeStruct((times, cols), jnp.bfloat16)
    return pl.pallas_call(
        functools.partial(gram_kernel, total_rows, places),
        out_shape=(jax.ShapeDtypeStruct((NF // 2, NB // 2, LANES), jnp.float32), saved, saved),
        in_specs=[any_space] * 3,
        out_specs=(VMEM, any_space, any_space),
        scratch_shapes=[
            pltpu.VMEM((times, cols), jnp.float32),
            pltpu.VMEM(weight_rows.shape, jnp.float32),
            pltpu.VMEM(dft.shape, jnp.bfloat16),
            pltpu.VMEM((times, cols), jnp.bfloat16),
            pltpu.VMEM((times, cols), jnp.bfloat16),
            pltpu.VMEM((cols // LANES, 2 * NF // 8, 8 * FREQ_STEP, LANES), jnp.float32),
            pltpu.VMEM((2 * LANES, 2 * cols), jnp.bfloat16),
            pltpu.VMEM((2 * LANES, 2 * cols), jnp.bfloat16),
            pltpu.VMEM((NF // PACK, NB, LANES), jnp.float32),
            pltpu.VMEM((NF // PACK, NB, LANES), jnp.float32),
            pltpu.SemaphoreType.DMA((pieces + 2,)),
            pltpu.SemaphoreType.DMA((2,)),
        ],
        compiler_params=pltpu.CompilerParams(vmem_limit_bytes=VMEM_LIMIT),
        cost_estimate=pl.CostEstimate(
            flops=5_000_000_000, bytes_accessed=8_000_000, transcendentals=0
        ),
        name="gram_parts",
    )(snapshots, weight_rows, jnp.asarray(dft))


def hermitian_pair(packed):
    square = jnp.concatenate([packed, pltpu.roll(packed, LANES // 2, 1)], axis=0)
    tall = jnp.concatenate([square] * (LANES // NB), axis=0).T
    row = lax.broadcasted_iota(jnp.int32, (NB, LANES), 0)
    lane = lax.broadcasted_iota(jnp.int32, (NB, LANES), 1)
    flipped = jnp.where(lane // NB == 0, tall[:NB], tall[NB : 2 * NB])
    col = lane % NB
    real = jnp.where(row <= col, square, flipped)
    imag = jnp.where(row > col, square, jnp.where(row < col, -flipped, 0.0))
    return real, imag, lane


def small_call(kernel, name, out_shape, scratch_shapes=(), limit=SMALL_LIMIT):
    def call(*args):
        return pl.pallas_call(
            kernel,
            out_shape=out_shape,
            in_specs=[VMEM] * len(args),
            out_specs=VMEM if isinstance(out_shape, jax.ShapeDtypeStruct) else (VMEM,) * len(out_shape),
            scratch_shapes=list(scratch_shapes),
            compiler_params=pltpu.CompilerParams(vmem_limit_bytes=limit),
            name=name,
        )(*args)

    return call


def floats(*shape):
    return jax.ShapeDtypeStruct(shape, jnp.float32)


def near_sum_kernel(parts_ref, out_ref):
    out_ref[...] = (parts_ref[0] + parts_ref[1]) + (parts_ref[2] + parts_ref[3])


def far_sum_kernel(parts_ref, start_ref, out_ref):
    packed = jnp.sum(parts_ref[...], axis=0)
    real, imag, lane = hermitian_pair(packed)
    start_real = start_ref[0]
    start_imag = start_ref[1]
    resp_real = jnp.sum(real * start_real + imag * start_imag, axis=0, keepdims=True)
    resp_imag = jnp.sum(real * start_imag - imag * start_real, axis=0, keepdims=True)
    power = resp_real * resp_real + resp_imag * resp_imag
    lane = lane[:1]
    first = jnp.sum(jnp.where(lane < NB, power, 0.0), axis=1, keepdims=True) / NB
    second = (
        jnp.sum(jnp.where((lane >= NB) & (lane < 2 * NB), power, 0.0), axis=1, keepdims=True) / NB
    )
    scaling = 1.0 / jnp.sqrt(jnp.where(lane < NB, first, second) + 1e-06)
    resp = jnp.where(
        lane < LANES // 2, resp_real * scaling, pltpu.roll(resp_imag * scaling, LANES // 2, 1)
    )
    resp = jnp.broadcast_to(resp, (8, LANES))
    for n in range(out_ref.shape[0]):
        out_ref[n, pl.ds(0, NB // 2), :] = packed
        out_ref[n, pl.ds(NB // 2, 8), :] = resp


def far_join_kernel(parts_ref, resp_ref, packed_ref):
    for n in range(parts_ref.shape[0]):
        row = parts_ref[n, pl.ds(NB // 2, 1), :]
        for m in range(resp_ref.shape[0]):
            resp_ref[m, pl.ds(n, 1), :] = row
        packed_ref[n] = parts_ref[n, pl.ds(0, NB // 2), :]


def unpack_kernel(*refs):
    parts, out_ref = refs[:-1], refs[-1]
    own = lax.rem(lax.axis_index("pts"), 2)
    row = lax.broadcasted_iota(jnp.int32, (NB, LANES), 0)
    lane = lax.broadcasted_iota(jnp.int32, (NB, LANES), 1)
    left = lane[: NB // 2] < LANES // 2
    col = lane % NB
    zero = jnp.zeros((NB, LANES), jnp.float32)
    for m, part in enumerate(parts):
        count = part.shape[0]
        place = (own ^ m) * 2 * count if len(parts) > 1 else 0
        for first in range(0, count, 2 * PACK):
            squares = []
            for i in range(first, min(first + 2 * PACK, count), 2):
                even, odd = part[i], part[i + 1]
                top = jnp.where(left, even, pltpu.roll(odd, LANES // 2, 1))
                bottom = jnp.where(left, pltpu.roll(even, LANES // 2, 1), odd)
                squares.append(jnp.concatenate([top, bottom], axis=0))
            full = squares + [zero] * (PACK - len(squares))
            turned = flip_groups([zero] * PACK, jnp.concatenate(full, axis=0))
            for g, square in enumerate(squares):
                real = jnp.where(row <= col, square, turned[g])
                imag = jnp.where(row > col, square, jnp.where(row < col, -turned[g], 0.0))
                for q in range(PACK):
                    freq = place + 2 * first + PACK * g + q
                    out_ref[freq, 0] = real[:, q * NB : (q + 1) * NB]
                    out_ref[freq, 1] = imag[:, q * NB : (q + 1) * NB]


def unpack_gram(*parts):
    pairs = sum(part.shape[0] for part in parts)
    return small_call(unpack_kernel, "unpack_gram", floats(2 * pairs, 2, NB, NB))(*parts)


def modes_kernel(
    total_rows, starts, high_hbm, low_hbm, w_hbm, table_hbm, resp_hbm,
    out_ref, resp_ref, w_ref, table_ref, resp_t, a_ref, x_ref, sems,
):
    times, cols = high_hbm.shape
    padded = x_ref.shape[1]
    pairs = NF // 2
    count = pairs // len(starts)
    fetch_resp = [
        pltpu.make_async_copy(
            resp_hbm.at[m], resp_ref.at[pl.ds(start, count)], sems.at[4 + m]
        )
        for m, start in enumerate(starts)
    ]
    fetches = [
        pltpu.make_async_copy(table_hbm, table_ref, sems.at[0]),
        pltpu.make_async_copy(w_hbm, w_ref, sems.at[1]),
        pltpu.make_async_copy(high_hbm, x_ref.at[0, pl.ds(0, times)], sems.at[2]),
        pltpu.make_async_copy(low_hbm, x_ref.at[1, pl.ds(0, times)], sems.at[3]),
    ]
    for fetch in fetch_resp + fetches:
        fetch.start()
    if padded > times:
        pad = pl.ds(times, padded - times)
        x_ref[0, pad, :] = jnp.zeros((padded - times, cols), jnp.bfloat16)
        x_ref[1, pad, :] = jnp.zeros((padded - times, cols), jnp.bfloat16)
    for fetch in fetch_resp + fetches[:2]:
        fetch.wait()
    tall = jnp.concatenate([resp_ref[...]] * (LANES // pairs), axis=0).T
    lane = lax.broadcasted_iota(jnp.int32, (NB, LANES), 1)
    turned = tall[:NB]
    for q in range(1, PACK):
        turned = jnp.where(lane // pairs == q, tall[q * NB : (q + 1) * NB], turned)
    swapped = pltpu.roll(turned, LANES // 2, 1)
    left = lane < LANES // 2
    resp_t[0] = jnp.where(left, turned, swapped)
    resp_t[1] = jnp.where(left, swapped, turned)
    for j in range(padded // HALF):
        value = jnp.zeros((HALF, LANES), jnp.float32)
        for block, start in ((j, 0), (j - 1, HALF)):
            if 0 <= block < NB:
                for part in range(2):
                    value += resp_t[part, pl.ds(block, 1), :] * table_ref[part, pl.ds(start, HALF), :]
        high, low = split(value)
        a_ref[0, pl.ds(j * HALF, HALF), :] = high
        a_ref[1, pl.ds(j * HALF, HALF), :] = low
    dot = functools.partial(
        lax.dot_general,
        dimension_numbers=(((0,), (0,)), ((), ())),
        preferred_element_type=jnp.float32,
    )
    for fetch in fetches[2:]:
        fetch.wait()
    modes = dot(a_ref[0], x_ref[0]) + dot(a_ref[0], x_ref[1]) + dot(a_ref[1], x_ref[0])
    modes = modes * jnp.sqrt(2.0 * total_rows / load_weights(w_ref, cols // LANES))
    n_freq = out_ref.shape[0]
    mine = pairs // n_freq
    group = lax.axis_index("freq")
    for part in range(2):
        for parity in range(2):
            for f in range(n_freq):
                first = (2 * part + parity) * pairs + f * mine
                slot = f ^ group if n_freq == 2 else f
                for c in range(cols // LANES):
                    out_ref[slot, 2 * c + part, pl.ds(parity, mine, stride=2), :] = modes[
                        first : first + mine, c * LANES : (c + 1) * LANES
                    ]


def local_modes(high, low, weight_rows, response, starts, total_rows, n_freq):
    times, cols = high.shape
    padded = -(-times // 256) * 256
    tables = mode_tables()
    any_space = pl.BlockSpec(memory_space=pl.ANY)
    return pl.pallas_call(
        functools.partial(modes_kernel, total_rows, starts),
        out_shape=floats(n_freq, 2 * cols // LANES, NF // n_freq, LANES),
        in_specs=[any_space] * 5,
        out_specs=VMEM,
        scratch_shapes=[
            pltpu.VMEM((NF // 2, LANES), jnp.float32),
            pltpu.VMEM(weight_rows.shape, jnp.float32),
            pltpu.VMEM(tables.shape, jnp.float32),
            pltpu.VMEM((2, NB, LANES), jnp.float32),
            pltpu.VMEM((2, padded, LANES), jnp.bfloat16),
            pltpu.VMEM((2, padded, cols), jnp.bfloat16),
            pltpu.SemaphoreType.DMA((4 + len(starts),)),
        ],
        compiler_params=pltpu.CompilerParams(vmem_limit_bytes=VMEM_LIMIT),
        name="local_modes",
    )(high, low, weight_rows, jnp.asarray(tables), response)


def join_kernel(kept_ref, got_ref, out_ref):
    tiles = got_ref.shape[0] // 2
    group = lax.axis_index("freq")
    for slot, ref in enumerate((kept_ref.at[0], got_ref)):
        for c in range(tiles):
            lanes = pl.ds(pl.multiple_of(((group ^ slot) * tiles + c) * LANES, LANES), LANES)
            for part in range(2):
                out_ref[:, part, lanes] = ref[2 * c + part]


def join_modes(kept, got):
    tiles, count, _ = got.shape
    return small_call(join_kernel, "join_modes", floats(count, 2, tiles * LANES))(kept, got)


def response_of(gram, start_vec):
    matvec = functools.partial(jnp.einsum, "fjk,fk->fj", precision=lax.Precision.HIGHEST)
    resp_real = matvec(gram[:, 0], start_vec[:, 0]) - matvec(gram[:, 1], start_vec[:, 1])
    resp_imag = matvec(gram[:, 0], start_vec[:, 1]) + matvec(gram[:, 1], start_vec[:, 0])
    scaling = 1.0 / jnp.sqrt(
        jnp.mean(resp_real * resp_real + resp_imag * resp_imag, axis=1, keepdims=True) + 1e-06
    )
    return jnp.stack([resp_real * scaling, resp_imag * scaling], axis=1)


def two_level_shards(n_devices, snapshots, weight, start_vec):
    both = ("pts", "freq")
    near = [[4 * i + j for j in range(4)] for i in range(n_devices // 4)]
    far = [[i + 4 * j for j in range(n_devices // 4)] for i in range(4)]
    exchange = functools.partial(
        lax.all_to_all, axis_name=both, split_axis=0, concat_axis=0, tiled=True
    )
    total_rows = float(weight.shape[0] * 16)
    weight_rows = weight.reshape(-1, LANES)
    starts = (0, 16, 8, 24)
    places = [8 * starts.index(i // 8 * 8) + i % 8 for i in range(NF // 2)]
    parts, high, low = gram_parts(snapshots, weight_rows, total_rows, places)

    group = lax.axis_index("freq")
    place = lax.axis_index("pts")
    first = (group * 16 + lax.rem(place, 2) * 8 + lax.div(place, 2)) * 2
    start_pair = lax.dynamic_slice_in_dim(start_vec, first, 2, 0)
    start_pair = jnp.transpose(start_pair, (1, 2, 0))[:, :, :, None]
    start_pair = jnp.broadcast_to(start_pair, (2, NB, 2, NB)).reshape(2, NB, 2 * NB)
    start_pair = jnp.concatenate([start_pair, start_pair], axis=2)

    parts = exchange(parts, axis_index_groups=near).reshape(4, 8, NB // 2, LANES)
    parts = small_call(near_sum_kernel, "near_sum", floats(8, NB // 2, LANES))(parts)
    parts = exchange(parts, axis_index_groups=far)
    own = small_call(far_sum_kernel, "far_sum", floats(8, NB // 2 + 8, LANES))(parts, start_pair)
    own = exchange(own, axis_index_groups=far)
    response, packed = small_call(
        far_join_kernel, "far_join", (floats(4, 8, LANES), floats(8, NB // 2, LANES))
    )(own)
    response = exchange(response, axis_index_groups=near)
    other = lax.ppermute(packed, both, [(i, i ^ 2) for i in range(n_devices)])
    gram_mine = unpack_gram(packed, other)
    modes = local_modes(high, low, weight_rows, response, starts, total_rows, 2)
    got = lax.ppermute(modes[1], "freq", [(0, 1), (1, 0)])
    return gram_mine, join_modes(modes, got)


def shards(n_pts, n_freq, snapshots, weight, start_vec):
    cols = snapshots.shape[1]
    total_rows = float(weight.shape[0] * n_pts)
    n_devices = n_pts * n_freq
    mine_count = NF // n_freq
    group = lax.axis_index("freq")
    weight_rows = weight.reshape(-1, LANES)
    parts, high, low = gram_parts(snapshots, weight_rows, total_rows, list(range(NF // 2)))
    share = parts.reshape(n_devices, -1)
    share = jnp.sum(lax.all_to_all(share, ("freq", "pts"), 0, 0, tiled=True), axis=0)
    packed = lax.all_gather(share, "pts", axis=0, tiled=True)
    gram_mine = unpack_gram(packed.reshape(mine_count // 2, NB // 2, LANES))
    start_mine = lax.dynamic_slice_in_dim(start_vec, group * mine_count, mine_count, 0)
    response = lax.all_gather(response_of(gram_mine, start_mine), "freq", axis=0, tiled=True)
    response = jnp.transpose(response.reshape(NF // 2, 2, 2, NB), (0, 2, 1, 3))
    response = response.reshape(1, NF // 2, LANES)
    modes = local_modes(high, low, weight_rows, response, (0,), total_rows, n_freq)
    modes = lax.all_to_all(modes, "freq", 0, 0, tiled=True)
    modes = modes.reshape(n_freq, cols // LANES, 2, mine_count, LANES)
    modes = jnp.transpose(modes, (3, 2, 0, 1, 4)).reshape(mine_count, 2, n_freq * cols)
    return gram_mine, modes


def solution(mesh):
    n_pts, n_freq = mesh.shape["pts"], mesh.shape["freq"]
    if (n_pts, n_freq) == (16, 2):
        body = functools.partial(two_level_shards, n_pts * n_freq)
    else:
        body = functools.partial(shards, n_pts, n_freq)
    placed = (P(None, ("pts", "freq")), P("pts"), P())
    return jax.shard_map(
        body,
        mesh=mesh,
        in_specs=placed,
        out_specs=(P("freq", None, None, None), P("freq", None, "pts")),
        check_vma=False,
    )
```

```python
import functools
import math

import jax
import jax.numpy as jnp
import numpy as np
from jax import lax
from jax.experimental import pallas as pl
from jax.experimental.pallas import tpu as pltpu
from jax.sharding import PartitionSpec as P

NFFT = 128
HALF = NFFT // 2
NF = 64
NB = 32
LANES = 128
PACK = 4
VMEM_LIMIT = 53 * 1024 * 1024
SMALL_LIMIT = 8 * 1024 * 1024
VMEM = pl.BlockSpec(memory_space=pltpu.VMEM)


def dft_values():
    times = np.arange(NFFT)
    freqs = np.arange(NF)
    phases = (freqs[:, None] * times[None, :] % NFFT) * (2.0 * math.pi / NFFT)
    window = 0.5 - 0.5 * np.cos(times * (2.0 * math.pi / NFFT))
    weighted = window / np.sqrt(np.sum(window * window))
    return np.cos(phases) * weighted, -np.sin(phases) * weighted


def split_table(table):
    high = table.astype(jnp.bfloat16)
    low = (table - high.astype(np.float64)).astype(jnp.bfloat16)
    return high, low


def dft_operand():
    real, imag = dft_values()
    high, low = split_table(np.concatenate([real, imag], axis=0))
    return np.block([[high, high], [low, np.zeros_like(low)]])


def mode_tables():
    real, imag = dft_values()
    order = np.concatenate([np.arange(0, NF, 2), np.arange(1, NF, 2)])
    real, imag = real[order].T, imag[order].T
    first = np.concatenate([real, imag], axis=1)
    second = np.concatenate([-imag, real], axis=1)
    return np.stack([first, second]).astype(np.float32)


def split(value):
    high = value.astype(jnp.bfloat16)
    low = (value - high.astype(jnp.float32)).astype(jnp.bfloat16)
    return high, low


def load_weights(w_ref, col_tiles):
    first = lax.axis_index("freq") * col_tiles
    return jnp.concatenate([w_ref[pl.ds(first + c, 1), :] for c in range(col_tiles)], axis=1)


def flip_groups(groups, flipped):
    turned = flipped.T
    lane = lax.broadcasted_iota(jnp.int32, (NB, LANES), 1)
    out = []
    for g in range(PACK):
        total = groups[g]
        for q in range(PACK):
            block = turned[q * NB : (q + 1) * NB]
            if q != g:
                block = pltpu.roll(block, ((q - g) % PACK) * NB, 1)
            total = total + jnp.where(lane // NB == q, block, 0.0)
        out.append(total)
    return out


ROW_STEP = 3
FREQ_STEP = ROW_STEP * NB + 1


def core_bit():
    return lax.rem(lax.axis_index("pts"), 2)


def y_bit():
    return lax.rem(lax.div(lax.axis_index("pts"), 2), 2)


def give_half(value_ref, bit, keep_ref, send_ref):
    half = keep_ref.shape[0]
    keep_ref[...] = value_ref[pl.ds(bit * half, half)]
    send_ref[...] = value_ref[pl.ds((1 - bit) * half, half)]


def gram_kernel(
    total_rows,
    places,
    by_core,
    x_hbm,
    w_hbm,
    dft_hbm,
    keep_ref,
    send_ref,
    high_hbm,
    low_hbm,
    x_ref,
    w_ref,
    dft_ref,
    high_ref,
    low_ref,
    spec_ref,
    z_even,
    z_odd,
    direct_ref,
    flipped_ref,
    pack_ref,
    in_sems,
    out_sems,
):
    times, cols = x_ref.shape
    halves = times // HALF
    col_tiles = cols // LANES
    pieces = in_sems.shape[0] - 2
    piece = times // pieces

    def fetch(i):
        rows = pl.ds(i * piece, piece)
        return pltpu.make_async_copy(x_hbm.at[rows], x_ref.at[rows], in_sems.at[i])

    fetch_w = pltpu.make_async_copy(w_hbm, w_ref, in_sems.at[pieces])
    fetch_dft = pltpu.make_async_copy(dft_hbm, dft_ref, in_sems.at[pieces + 1])
    for i in range(pieces):
        fetch(i).start()
    fetch_w.start()
    fetch_dft.start()

    acc = jnp.zeros((HALF, cols), jnp.float32)
    for i in range(pieces):
        fetch(i).wait()
        for h in range(piece // HALF):
            acc = acc + x_ref[pl.ds(i * piece + h * HALF, HALF), :]
    mean = jnp.sum(acc, axis=0, keepdims=True) / times
    fetch_w.wait()
    scale = jnp.sqrt(load_weights(w_ref, col_tiles) / (2.0 * total_rows))

    def center(i, carry):
        rows = pl.ds(pl.multiple_of(i * HALF, HALF), HALF)
        high, low = split((x_ref[rows, :] - mean) * scale)
        high_ref[rows, :] = high
        low_ref[rows, :] = low
        return carry

    lax.fori_loop(0, halves, center, 0, unroll=3)
    save_high = pltpu.make_async_copy(high_ref, high_hbm, out_sems.at[0])
    save_low = pltpu.make_async_copy(low_ref, low_hbm, out_sems.at[1])
    save_high.start()
    save_low.start()
    fetch_dft.wait()

    def transform(i, carry):
        blocks = []
        for s in range(2):
            rows = pl.ds(pl.multiple_of((2 * i + s) * HALF, HALF), NFFT)
            blocks.append(jnp.concatenate([high_ref[rows, :], low_ref[rows, :]], axis=0))
        both = jnp.dot(
            dft_ref[...], jnp.concatenate(blocks, axis=1), preferred_element_type=jnp.float32
        )
        spectrum = both[: 2 * NF] + both[2 * NF :]
        for s in range(2):
            for o in range(2 * NF // 8):
                for c in range(col_tiles):
                    first = s * cols + c * LANES
                    rows = pl.ds(ROW_STEP * (2 * i + s), 8, stride=FREQ_STEP)
                    spec_ref[c, o, rows, :] = spectrum[8 * o : 8 * o + 8, first : first + LANES]
        return carry

    lax.fori_loop(0, NB // 2, transform, 0, unroll=2)

    row = lax.broadcasted_iota(jnp.int32, (NB, LANES), 0)
    lane = lax.broadcasted_iota(jnp.int32, (NB, LANES), 1)
    upper = row <= lane % NB
    lower = row >= lane % NB
    octets = NF // 8

    def prepare(z_ref, octet, half):
        for part in range(2):
            for q in range(PACK):
                rows = pl.ds(FREQ_STEP * (PACK * half + q), NB, stride=ROW_STEP)
                own = pl.ds(part * LANES + q * NB, NB)
                for c in range(col_tiles):
                    value = spec_ref[c, octet + octets * part, rows, :]
                    high = value.astype(jnp.bfloat16)
                    low = (2.0 * (value - high.astype(jnp.float32))).astype(jnp.bfloat16)
                    z_ref[own, pl.ds(c * LANES, LANES)] = high
                    z_ref[own, pl.ds(cols + c * LANES, LANES)] = low

    def correlate(z_ref, group):
        high = z_ref[:, pl.ds(0, cols)]
        product = lax.dot_general(
            jnp.concatenate([high, high], axis=1),
            z_ref[...],
            (((1,), (1,)), ((), ())),
            preferred_element_type=jnp.float32,
        )
        gram_real = jnp.zeros((NB, LANES), jnp.float32)
        gram_imag = jnp.zeros((NB, LANES), jnp.float32)
        for q in range(PACK):
            mine = lane // NB == q
            real = product[q * NB : (q + 1) * NB]
            imag = product[LANES + q * NB : LANES + (q + 1) * NB]
            gram_real = jnp.where(mine, real[:, :LANES] + imag[:, LANES:], gram_real)
            gram_imag = jnp.where(mine, real[:, LANES:] - imag[:, :LANES], gram_imag)
        direct_ref[group] = jnp.where(upper, gram_real, gram_imag)
        flipped_ref[group] = jnp.where(lower, gram_real, -gram_imag)

    prepare(z_even, 0, 0)

    def step(o, carry):
        prepare(z_odd, o, 1)
        correlate(z_even, 2 * o)
        prepare(z_even, jnp.minimum(o + 1, octets - 1), 0)
        correlate(z_odd, 2 * o + 1)
        return carry

    lax.fori_loop(0, octets, step, 0)
    left = lane[: NB // 2] < LANES // 2
    for quad in range(NF // PACK // PACK):
        groups = [direct_ref[quad * PACK + g] for g in range(PACK)]
        flipped = flipped_ref[pl.ds(quad * PACK, PACK)].reshape(PACK * NB, LANES)
        for g, packed in enumerate(flip_groups(groups, flipped)):
            top = packed[: NB // 2]
            bottom = packed[NB // 2 :]
            pair = 2 * (quad * PACK + g)
            pack_ref[places[pair]] = jnp.where(left, top, pltpu.roll(bottom, LANES // 2, 1))
            pack_ref[places[pair + 1]] = jnp.where(left, pltpu.roll(top, LANES // 2, 1), bottom)
    give_half(pack_ref, core_bit() if by_core else 0, keep_ref, send_ref)
    save_high.wait()
    save_low.wait()


def gram_parts(snapshots, weight_rows, total_rows, places, by_core):
    times, cols = snapshots.shape
    dft = dft_operand()
    pieces = 11
    any_space = pl.BlockSpec(memory_space=pl.ANY)
    saved = jax.ShapeDtypeStruct((times, cols), jnp.bfloat16)
    half = floats(NF // 4, NB // 2, LANES)
    return pl.pallas_call(
        functools.partial(gram_kernel, total_rows, places, by_core),
        out_shape=(half, half, saved, saved),
        in_specs=[any_space] * 3,
        out_specs=(VMEM, VMEM, any_space, any_space),
        scratch_shapes=[
            pltpu.VMEM((times, cols), jnp.float32),
            pltpu.VMEM(weight_rows.shape, jnp.float32),
            pltpu.VMEM(dft.shape, jnp.bfloat16),
            pltpu.VMEM((times, cols), jnp.bfloat16),
            pltpu.VMEM((times, cols), jnp.bfloat16),
            pltpu.VMEM((cols // LANES, 2 * NF // 8, 8 * FREQ_STEP, LANES), jnp.float32),
            pltpu.VMEM((2 * LANES, 2 * cols), jnp.bfloat16),
            pltpu.VMEM((2 * LANES, 2 * cols), jnp.bfloat16),
            pltpu.VMEM((NF // PACK, NB, LANES), jnp.float32),
            pltpu.VMEM((NF // PACK, NB, LANES), jnp.float32),
            pltpu.VMEM((NF // 2, NB // 2, LANES), jnp.float32),
            pltpu.SemaphoreType.DMA((pieces + 2,)),
            pltpu.SemaphoreType.DMA((2,)),
        ],
        compiler_params=pltpu.CompilerParams(vmem_limit_bytes=VMEM_LIMIT),
        cost_estimate=pl.CostEstimate(
            flops=5_000_000_000, bytes_accessed=8_000_000, transcendentals=0
        ),
        name="gram_parts",
    )(snapshots, weight_rows, jnp.asarray(dft))


def pair_square(even, odd):
    left = lax.broadcasted_iota(jnp.int32, (NB // 2, LANES), 1) < LANES // 2
    top = jnp.where(left, even, pltpu.roll(odd, LANES // 2, 1))
    bottom = jnp.where(left, pltpu.roll(even, LANES // 2, 1), odd)
    return jnp.concatenate([top, bottom], axis=0)


def hermitian(squares):
    row = lax.broadcasted_iota(jnp.int32, (NB, LANES), 0)
    col = lax.broadcasted_iota(jnp.int32, (NB, LANES), 1) % NB
    zero = jnp.zeros((NB, LANES), jnp.float32)
    full = squares + [zero] * (PACK - len(squares))
    turned = flip_groups([zero] * PACK, jnp.concatenate(full, axis=0))
    for square, flipped in zip(squares, turned):
        real = jnp.where(row <= col, square, flipped)
        imag = jnp.where(row > col, square, jnp.where(row < col, -flipped, 0.0))
        yield real, imag


def small_call(kernel, name, out_shape, scratch_shapes=(), limit=SMALL_LIMIT):
    def call(*args):
        return pl.pallas_call(
            kernel,
            out_shape=out_shape,
            in_specs=[VMEM] * len(args),
            out_specs=VMEM if isinstance(out_shape, jax.ShapeDtypeStruct) else (VMEM,) * len(out_shape),
            scratch_shapes=list(scratch_shapes),
            compiler_params=pltpu.CompilerParams(vmem_limit_bytes=limit),
            name=name,
        )(*args)

    return call


def floats(*shape):
    return jax.ShapeDtypeStruct(shape, jnp.float32)


def add_split_kernel(bit, kept_ref, got_ref, keep_ref, send_ref, sum_ref):
    sum_ref[...] = kept_ref[...] + got_ref[...]
    give_half(sum_ref, bit(), keep_ref, send_ref)


def add_split(bit, name, kept, got):
    half = floats(kept.shape[0] // 2, *kept.shape[1:])
    scratch = [pltpu.VMEM(kept.shape, jnp.float32)]
    return small_call(functools.partial(add_split_kernel, bit), name, (half, half), scratch)(
        kept, got
    )


def add_kernel(kept_ref, got_ref, out_ref):
    out_ref[...] = kept_ref[...] + got_ref[...]


def add(name, kept, got):
    return small_call(add_kernel, name, floats(*kept.shape))(kept, got)


def respond_kernel(kept_ref, got_ref, start_ref, out_ref):
    pairs, rows = kept_ref.shape[:2]
    packed = kept_ref[...] + got_ref[...]
    out_ref[pl.ds(0, pairs * rows), :] = packed.reshape(pairs * rows, LANES)
    squares = [pair_square(packed[i], packed[i + 1]) for i in range(0, pairs, 2)]
    lane = lax.broadcasted_iota(jnp.int32, (1, LANES), 1)
    left = lane < LANES // 2
    lines = []
    for i, (real, imag) in enumerate(hermitian(squares)):
        start_real = start_ref[i, 0]
        start_imag = start_ref[i, 1]
        resp_real = jnp.sum(real * start_real + imag * start_imag, axis=0, keepdims=True)
        resp_imag = jnp.sum(real * start_imag - imag * start_real, axis=0, keepdims=True)
        power = resp_real * resp_real + resp_imag * resp_imag
        mean = jnp.zeros((1, LANES), jnp.float32)
        for q in range(PACK):
            mine = lane // NB == q
            part = jnp.sum(jnp.where(mine, power, 0.0), axis=1, keepdims=True) / NB
            mean = jnp.where(mine, part, mean)
        scaling = 1.0 / jnp.sqrt(mean + 1e-06)
        resp_real = resp_real * scaling
        resp_imag = resp_imag * scaling
        lines.append(jnp.where(left, resp_real, pltpu.roll(resp_imag, LANES // 2, 1)))
        lines.append(jnp.where(left, pltpu.roll(resp_real, LANES // 2, 1), resp_imag))
    lines += [jnp.zeros((1, LANES), jnp.float32)] * (8 - len(lines))
    out_ref[pl.ds(pairs * rows, 8), :] = jnp.concatenate(lines, axis=0)


def respond(kept, got, start):
    pairs, rows, _ = kept.shape
    return small_call(respond_kernel, "respond", floats(pairs * rows + 8, LANES))(kept, got, start)


def join_y_kernel(own_ref, got_ref, resp_ref, packed_ref):
    pairs = packed_ref.shape[0] // 2
    rows = NB // 2
    for m, ref in enumerate((own_ref, got_ref)):
        first = (y_bit() ^ m) * pairs
        resp_ref[pl.ds(first, pairs), :] = ref[pl.ds(pairs * rows, pairs), :]
        packed_ref[pl.ds(first, pairs)] = ref[pl.ds(0, pairs * rows), :].reshape(pairs, rows, LANES)


def join_core_kernel(own_ref, got_ref, out_ref):
    pairs = own_ref.shape[0]
    for m, ref in enumerate((own_ref, got_ref)):
        out_ref[pl.ds((core_bit() ^ m) * pairs, pairs), :] = ref[...]


def unpack_kernel(*refs):
    parts, out_ref = refs[:-1], refs[-1]
    for m, part in enumerate(parts):
        count = part.shape[0]
        place = (core_bit() ^ m) * 2 * count if len(parts) > 1 else 0
        for first in range(0, count, 2 * PACK):
            last = min(first + 2 * PACK, count)
            squares = [pair_square(part[i], part[i + 1]) for i in range(first, last, 2)]
            for g, both in enumerate(hermitian(squares)):
                for q in range(PACK):
                    freq = place + 2 * first + PACK * g + q
                    for c in range(2):
                        out_ref[freq, c] = both[c][:, q * NB : (q + 1) * NB]


def unpack_gram(*parts):
    pairs = sum(part.shape[0] for part in parts)
    return small_call(unpack_kernel, "unpack_gram", floats(2 * pairs, 2, NB, NB))(*parts)


def modes_kernel(total_rows, n_resp, high_hbm, low_hbm, w_hbm, table_hbm, *refs):
    resp_refs = refs[:n_resp]
    (out_ref, resp_ref, w_ref, table_ref, resp_t, a_ref, x_ref, sems) = refs[n_resp:]
    times, cols = high_hbm.shape
    padded = x_ref.shape[0] // 2
    chunk = 256
    pairs = NF // 2

    def fetch(i, source):
        first = i * chunk
        count = min(chunk, times - first)
        place = 2 * first + source * chunk
        return pltpu.make_async_copy(
            (high_hbm, low_hbm)[source].at[pl.ds(first, count)],
            x_ref.at[pl.ds(place, count)],
            sems.at[2 + 2 * i + source],
        )

    fetch_table = pltpu.make_async_copy(table_hbm, table_ref, sems.at[0])
    fetch_w = pltpu.make_async_copy(w_hbm, w_ref, sems.at[1])
    fetch_table.start()
    chunks = padded // chunk
    for i in range(chunks):
        for source in range(2):
            fetch(i, source).start()
    fetch_w.start()
    pad = padded - times
    if pad:
        for source in range(2):
            first = 2 * (padded - chunk) + source * chunk + chunk - pad
            x_ref[pl.ds(first, pad), :] = jnp.zeros((pad, cols), jnp.bfloat16)
    if n_resp == 1:
        resp_ref[...] = resp_refs[0][...]
    else:
        for m, part in enumerate(resp_refs):
            place = (lax.axis_index("freq") ^ m) * (pairs // 2)
            resp_ref[pl.ds(place, pairs // 2), :] = part[...]
    tall = jnp.concatenate([resp_ref[...]] * (LANES // pairs), axis=0).T
    lane = lax.broadcasted_iota(jnp.int32, (NB, LANES), 1)
    turned = tall[:NB]
    for q in range(1, PACK):
        turned = jnp.where(lane // pairs == q, tall[q * NB : (q + 1) * NB], turned)
    swapped = pltpu.roll(turned, LANES // 2, 1)
    left = lane < LANES // 2
    resp_t[0] = jnp.where(left, turned, swapped)
    resp_t[1] = jnp.where(left, swapped, turned)
    fetch_table.wait()
    modes = jnp.zeros((2 * NF, cols), jnp.float32)
    for i in range(chunks):
        for h in range(chunk // HALF):
            j = i * (chunk // HALF) + h
            value = jnp.zeros((HALF, LANES), jnp.float32)
            for block, start in ((j, 0), (j - 1, HALF)):
                if 0 <= block < NB:
                    for part in range(2):
                        rows = pl.ds(start, HALF)
                        value += resp_t[part, pl.ds(block, 1), :] * table_ref[part, rows, :]
            high, low = split(value)
            a_ref[i, pl.ds(h * HALF, HALF), :] = high
            a_ref[i, pl.ds(chunk + h * HALF, HALF), :] = high
            a_ref[i, pl.ds(2 * chunk + h * HALF, HALF), :] = low
        for source in range(2):
            fetch(i, source).wait()
        x_high = x_ref[pl.ds(2 * i * chunk, chunk), :]
        x_low = x_ref[pl.ds((2 * i + 1) * chunk, chunk), :]
        modes += lax.dot_general(
            a_ref[i],
            jnp.concatenate([x_high, x_low, x_high], axis=0),
            (((0,), (0,)), ((), ())),
            preferred_element_type=jnp.float32,
        )
    fetch_w.wait()
    modes = modes * jnp.sqrt(2.0 * total_rows / load_weights(w_ref, cols // LANES))
    n_freq = out_ref.shape[0]
    mine = pairs // n_freq
    group = lax.axis_index("freq")
    for part in range(2):
        for parity in range(2):
            for f in range(n_freq):
                first = (2 * part + parity) * pairs + f * mine
                slot = f ^ group if n_freq == 2 else f
                for c in range(cols // LANES):
                    out_ref[slot, 2 * c + part, pl.ds(parity, mine, stride=2), :] = modes[
                        first : first + mine, c * LANES : (c + 1) * LANES
                    ]


def local_modes(high, low, weight_rows, responses, total_rows, n_freq):
    times, cols = high.shape
    padded = -(-times // 256) * 256
    tables = mode_tables()
    any_space = pl.BlockSpec(memory_space=pl.ANY)
    return pl.pallas_call(
        functools.partial(modes_kernel, total_rows, len(responses)),
        out_shape=floats(n_freq, 2 * cols // LANES, NF // n_freq, LANES),
        in_specs=[any_space] * 4 + [VMEM] * len(responses),
        out_specs=VMEM,
        scratch_shapes=[
            pltpu.VMEM((NF // 2, LANES), jnp.float32),
            pltpu.VMEM(weight_rows.shape, jnp.float32),
            pltpu.VMEM(tables.shape, jnp.float32),
            pltpu.VMEM((2, NB, LANES), jnp.float32),
            pltpu.VMEM((padded // 256, 3 * 256, LANES), jnp.bfloat16),
            pltpu.VMEM((2 * padded, cols), jnp.bfloat16),
            pltpu.SemaphoreType.DMA((2 + 2 * (padded // 256),)),
        ],
        compiler_params=pltpu.CompilerParams(vmem_limit_bytes=VMEM_LIMIT),
        name="local_modes",
    )(high, low, weight_rows, jnp.asarray(tables), *responses)


def join_kernel(kept_ref, got_ref, out_ref):
    tiles = got_ref.shape[0] // 2
    group = lax.axis_index("freq")
    for slot, ref in enumerate((kept_ref.at[0], got_ref)):
        for c in range(tiles):
            lanes = pl.ds(pl.multiple_of(((group ^ slot) * tiles + c) * LANES, LANES), LANES)
            for part in range(2):
                out_ref[:, part, lanes] = ref[2 * c + part]


def join_modes(kept, got):
    tiles, count, _ = got.shape
    return small_call(join_kernel, "join_modes", floats(count, 2, tiles * LANES))(kept, got)


def response_of(gram, start_vec):
    matvec = functools.partial(jnp.einsum, "fjk,fk->fj", precision=lax.Precision.HIGHEST)
    resp_real = matvec(gram[:, 0], start_vec[:, 0]) - matvec(gram[:, 1], start_vec[:, 1])
    resp_imag = matvec(gram[:, 0], start_vec[:, 1]) + matvec(gram[:, 1], start_vec[:, 0])
    scaling = 1.0 / jnp.sqrt(
        jnp.mean(resp_real * resp_real + resp_imag * resp_imag, axis=1, keepdims=True) + 1e-06
    )
    return jnp.stack([resp_real * scaling, resp_imag * scaling], axis=1)


def direction_shards(n_devices, snapshots, weight, start_vec):
    def swap(value, mask):
        return lax.ppermute(value, ("pts", "freq"), [(i, i ^ mask) for i in range(n_devices)])

    x, core, y, z_near, z_far = 1, 2, 4, 8, 16
    total_rows = float(weight.shape[0] * 16)
    weight_rows = weight.reshape(-1, LANES)
    places = [(i // 8 % 2) * 16 + (i // 16) * 8 + i % 8 for i in range(NF // 2)]
    keep, send, high, low = gram_parts(snapshots, weight_rows, total_rows, places, True)

    group = lax.axis_index("freq")
    first = group * 32 + core_bit() * 16 + y_bit() * 8
    start = lax.dynamic_slice_in_dim(start_vec, first, 8, 0).reshape(2, PACK, 2, NB)
    start = jnp.transpose(start, (0, 2, 3, 1))[..., None]
    start = jnp.broadcast_to(start, (2, 2, NB, PACK, NB)).reshape(2, 2, NB, LANES)

    keep, send = add_split(lambda: lax.axis_index("freq"), "add_core", keep, swap(send, core))
    keep, send = add_split(y_bit, "add_x", keep, swap(send, x))
    part = add("add_y", keep, swap(send, y))
    part = add("add_z", part, swap(part, z_near))
    own = respond(part, swap(part, z_far), start)
    response, packed = small_call(
        join_y_kernel, "join_y", (floats(8, LANES), floats(8, NB // 2, LANES))
    )(own, swap(own, y))
    response = small_call(join_core_kernel, "join_core", floats(16, LANES))(
        response, swap(response, core)
    )
    gram_mine = unpack_gram(packed, swap(packed, core))
    modes = local_modes(high, low, weight_rows, (response, swap(response, x)), total_rows, 2)
    return gram_mine, join_modes(modes, swap(modes[1], x))


def shards(n_pts, n_freq, snapshots, weight, start_vec):
    cols = snapshots.shape[1]
    total_rows = float(weight.shape[0] * n_pts)
    n_devices = n_pts * n_freq
    mine_count = NF // n_freq
    group = lax.axis_index("freq")
    weight_rows = weight.reshape(-1, LANES)
    places = list(range(NF // 2))
    first, second, high, low = gram_parts(snapshots, weight_rows, total_rows, places, False)
    share = jnp.concatenate([first, second], axis=0).reshape(n_devices, -1)
    share = jnp.sum(lax.all_to_all(share, ("freq", "pts"), 0, 0, tiled=True), axis=0)
    packed = lax.all_gather(share, "pts", axis=0, tiled=True)
    gram_mine = unpack_gram(packed.reshape(mine_count // 2, NB // 2, LANES))
    start_mine = lax.dynamic_slice_in_dim(start_vec, group * mine_count, mine_count, 0)
    response = lax.all_gather(response_of(gram_mine, start_mine), "freq", axis=0, tiled=True)
    response = jnp.transpose(response.reshape(NF // 2, 2, 2, NB), (0, 2, 1, 3))
    response = response.reshape(NF // 2, LANES)
    modes = local_modes(high, low, weight_rows, (response,), total_rows, n_freq)
    modes = lax.all_to_all(modes, "freq", 0, 0, tiled=True)
    modes = modes.reshape(n_freq, cols // LANES, 2, mine_count, LANES)
    modes = jnp.transpose(modes, (3, 2, 0, 1, 4)).reshape(mine_count, 2, n_freq * cols)
    return gram_mine, modes


def solution(mesh):
    n_pts, n_freq = mesh.shape["pts"], mesh.shape["freq"]
    if (n_pts, n_freq) == (16, 2):
        body = functools.partial(direction_shards, n_pts * n_freq)
    else:
        body = functools.partial(shards, n_pts, n_freq)
    placed = (P(None, ("pts", "freq")), P("pts"), P())
    return jax.shard_map(
        body,
        mesh=mesh,
        in_specs=placed,
        out_specs=(P("freq", None, None, None), P("freq", None, "pts")),
        check_vma=False,
    )
```

```python
import functools
import math

import jax
import jax.numpy as jnp
import numpy as np
from jax import lax
from jax.experimental import pallas as pl
from jax.experimental.pallas import tpu as pltpu
from jax.sharding import PartitionSpec as P

NFFT = 128
HALF = NFFT // 2
NF = 64
NB = 32
LANES = 128
PACK = 4
VMEM_LIMIT = 51 * 1024 * 1024
SMALL_LIMIT = 8 * 1024 * 1024
VMEM = pl.BlockSpec(memory_space=pltpu.VMEM)


def dft_values():
    times = np.arange(NFFT)
    freqs = np.arange(NF)
    phases = (freqs[:, None] * times[None, :] % NFFT) * (2.0 * math.pi / NFFT)
    window = 0.5 - 0.5 * np.cos(times * (2.0 * math.pi / NFFT))
    weighted = window / np.sqrt(np.sum(window * window))
    return np.cos(phases) * weighted, -np.sin(phases) * weighted


def split_table(table):
    high = table.astype(jnp.bfloat16)
    low = (table - high.astype(np.float64)).astype(jnp.bfloat16)
    return high, low


def mode_tables():
    real, imag = dft_values()
    order = np.arange(NF).reshape(NF // PACK, PACK).T
    real, imag = (np.moveaxis(part[order], -1, 0) for part in (real, imag))
    first = np.stack([real, imag], axis=2).reshape(NFFT, 2 * NF)
    second = np.stack([-imag, real], axis=2).reshape(NFFT, 2 * NF)
    return np.stack([first, second]).astype(np.float32)


def cosine_of_turns(count):
    folded = jnp.minimum(count, NFFT - count)
    angle = (NFFT // 4 - folded).astype(jnp.float32) * (2.0 * math.pi / NFFT)
    square = angle * angle
    series = 1.0
    for n in (10, 8, 6, 4, 2):
        series = 1.0 - square * series * (1.0 / (n * (n + 1)))
    return angle * series


def fill_dft(dft_ref):
    row = lax.broadcasted_iota(jnp.int32, (2 * NF, NFFT), 0)
    time = lax.broadcasted_iota(jnp.int32, (2 * NF, NFFT), 1)
    quarter = jnp.where(row < NF, 0, NFFT // 4)
    wave = cosine_of_turns((row % NF * time + quarter) % NFFT)
    window = 0.5 - 0.5 * np.cos(np.arange(NFFT) * (2.0 * math.pi / NFFT))
    norm = float(np.sqrt(np.sum(window * window)))
    high, low = split(wave * ((0.5 - 0.5 * cosine_of_turns(time)) / norm))
    dft_ref[pl.ds(0, 2 * NF), pl.ds(0, NFFT)] = high
    dft_ref[pl.ds(0, 2 * NF), pl.ds(NFFT, NFFT)] = high
    dft_ref[pl.ds(2 * NF, 2 * NF), pl.ds(0, NFFT)] = low
    dft_ref[pl.ds(2 * NF, 2 * NF), pl.ds(NFFT, NFFT)] = jnp.zeros((2 * NF, NFFT), jnp.bfloat16)


def spread_start(start_ref, spread_ref):
    row = lax.broadcasted_iota(jnp.int32, (NF, LANES), 0)
    lane = lax.broadcasted_iota(jnp.int32, (NF, LANES), 1)
    for g in range(NF // PACK):
        pick = (row == PACK * g + lane // NB).astype(jnp.float32)
        spread_ref[g] = jnp.dot(
            start_ref[...],
            pick,
            precision=lax.Precision.HIGHEST,
            preferred_element_type=jnp.float32,
        )


def split(value):
    high = value.astype(jnp.bfloat16)
    low = (value - high.astype(jnp.float32)).astype(jnp.bfloat16)
    return high, low


def load_weights(w_ref, col_tiles):
    first = lax.axis_index("freq") * col_tiles
    return jnp.concatenate([w_ref[pl.ds(first + c, 1), :] for c in range(col_tiles)], axis=1)


def flip_groups(groups, flipped):
    turned = flipped.T
    lane = lax.broadcasted_iota(jnp.int32, (NB, LANES), 1)
    out = []
    for g in range(PACK):
        total = groups[g]
        for q in range(PACK):
            block = turned[q * NB : (q + 1) * NB]
            if q != g:
                block = pltpu.roll(block, ((q - g) % PACK) * NB, 1)
            total = total + jnp.where(lane // NB == q, block, 0.0)
        out.append(total)
    return out


ROW_STEP = 3
FREQ_STEP = ROW_STEP * NB + 1


def core_bit():
    return lax.rem(lax.axis_index("pts"), 2)


def y_bit():
    return lax.rem(lax.div(lax.axis_index("pts"), 2), 2)


RESP_ROWS = 2 * NF // PACK


def give_half(value_ref, bit, keep_ref, send_ref):
    half = keep_ref.shape[0] - RESP_ROWS
    keep_ref[pl.ds(0, half), :] = value_ref[pl.ds(bit * half, half), :]
    send_ref[pl.ds(0, half), :] = value_ref[pl.ds((1 - bit) * half, half), :]
    resp = value_ref[pl.ds(2 * half, RESP_ROWS), :]
    keep_ref[pl.ds(half, RESP_ROWS), :] = resp
    send_ref[pl.ds(half, RESP_ROWS), :] = resp


def gram_kernel(
    total_rows,
    places,
    by_core,
    x_hbm,
    w_hbm,
    start_ref,
    keep_ref,
    send_ref,
    high_ref,
    low_hbm,
    x_ref,
    w_ref,
    dft_ref,
    low_ref,
    spec_ref,
    z_even,
    z_odd,
    real_ref,
    imag_ref,
    spread_ref,
    pack_ref,
    in_sems,
    out_sem,
):
    times, cols = x_ref.shape
    halves = times // HALF
    col_tiles = cols // LANES
    pieces = in_sems.shape[0] - 1
    piece = times // pieces

    def fetch(i):
        rows = pl.ds(i * piece, piece)
        return pltpu.make_async_copy(x_hbm.at[rows], x_ref.at[rows], in_sems.at[i])

    fetch_w = pltpu.make_async_copy(w_hbm, w_ref, in_sems.at[pieces])
    for i in range(pieces):
        fetch(i).start()
    fetch_w.start()
    fill_dft(dft_ref)
    spread_start(start_ref, spread_ref)

    acc = jnp.zeros((HALF, cols), jnp.float32)
    for i in range(pieces):
        fetch(i).wait()
        for h in range(piece // HALF):
            acc = acc + x_ref[pl.ds(i * piece + h * HALF, HALF), :]
    mean = jnp.sum(acc, axis=0, keepdims=True) / times
    fetch_w.wait()
    scale = jnp.sqrt(load_weights(w_ref, col_tiles) / (2.0 * total_rows))

    def center(i, carry):
        rows = pl.ds(pl.multiple_of(i * HALF, HALF), HALF)
        high, low = split((x_ref[rows, :] - mean) * scale)
        high_ref[rows, :] = high
        low_ref[rows, :] = low
        return carry

    lax.fori_loop(0, halves, center, 0, unroll=3)
    pad = high_ref.shape[0] - times
    if pad:
        high_ref[pl.ds(times, pad), :] = jnp.zeros((pad, cols), jnp.bfloat16)
        low_ref[pl.ds(times, pad), :] = jnp.zeros((pad, cols), jnp.bfloat16)
    save_low = pltpu.make_async_copy(low_ref, low_hbm, out_sem)
    save_low.start()

    def transform(i, carry):
        blocks = []
        for s in range(2):
            rows = pl.ds(pl.multiple_of((2 * i + s) * HALF, HALF), NFFT)
            blocks.append(jnp.concatenate([high_ref[rows, :], low_ref[rows, :]], axis=0))
        both = jnp.dot(
            dft_ref[...], jnp.concatenate(blocks, axis=1), preferred_element_type=jnp.float32
        )
        spectrum = both[: 2 * NF] + both[2 * NF :]
        for s in range(2):
            for o in range(2 * NF // 8):
                for c in range(col_tiles):
                    first = s * cols + c * LANES
                    rows = pl.ds(ROW_STEP * (2 * i + s), 8, stride=FREQ_STEP)
                    spec_ref[c, o, rows, :] = spectrum[8 * o : 8 * o + 8, first : first + LANES]
        return carry

    lax.fori_loop(0, NB // 2, transform, 0, unroll=2)

    row = lax.broadcasted_iota(jnp.int32, (NB, LANES), 0)
    lane = lax.broadcasted_iota(jnp.int32, (NB, LANES), 1)
    upper = row <= lane % NB
    octets = NF // 8

    def prepare(z_ref, octet, half):
        for part in range(2):
            for q in range(PACK):
                rows = pl.ds(FREQ_STEP * (PACK * half + q), NB, stride=ROW_STEP)
                own = pl.ds(part * LANES + q * NB, NB)
                for c in range(col_tiles):
                    value = spec_ref[c, octet + octets * part, rows, :]
                    high = value.astype(jnp.bfloat16)
                    low = (2.0 * (value - high.astype(jnp.float32))).astype(jnp.bfloat16)
                    z_ref[own, pl.ds(c * LANES, LANES)] = high
                    z_ref[own, pl.ds(cols + c * LANES, LANES)] = low

    def correlate(z_ref, group):
        high = z_ref[:, pl.ds(0, cols)]
        product = lax.dot_general(
            jnp.concatenate([high, high], axis=1),
            z_ref[...],
            (((1,), (1,)), ((), ())),
            preferred_element_type=jnp.float32,
        )
        gram_real = jnp.zeros((NB, LANES), jnp.float32)
        gram_imag = jnp.zeros((NB, LANES), jnp.float32)
        for q in range(PACK):
            mine = lane // NB == q
            real = product[q * NB : (q + 1) * NB]
            imag = product[LANES + q * NB : LANES + (q + 1) * NB]
            gram_real = jnp.where(mine, real[:, :LANES] + imag[:, LANES:], gram_real)
            gram_imag = jnp.where(mine, real[:, LANES:] - imag[:, :LANES], gram_imag)
        real_ref[group] = gram_real
        imag_ref[group] = gram_imag

    prepare(z_even, 0, 0)

    def step(o, carry):
        prepare(z_odd, o, 1)
        correlate(z_even, 2 * o)
        prepare(z_even, jnp.minimum(o + 1, octets - 1), 0)
        correlate(z_odd, 2 * o + 1)
        return carry

    lax.fori_loop(0, octets, step, 0)
    left = lane[: NB // 2] < LANES // 2
    half = NB // 2
    resp_real = []
    resp_imag = []
    for quad in range(NF // PACK // PACK):
        own = pl.ds(quad * PACK, PACK)
        reals = [real_ref[quad * PACK + g] for g in range(PACK)]
        imags = [imag_ref[quad * PACK + g] for g in range(PACK)]
        reals = flip_groups(reals, real_ref[own].reshape(PACK * NB, LANES))
        imags = flip_groups(imags, -imag_ref[own].reshape(PACK * NB, LANES))
        for g, (real, imag) in enumerate(zip(reals, imags)):
            group = quad * PACK + g
            start_real = spread_ref[group, pl.ds(0, NB), :]
            start_imag = spread_ref[group, pl.ds(NB, NB), :]
            resp_real.append(
                jnp.sum(real * start_real + imag * start_imag, axis=0, keepdims=True)
            )
            resp_imag.append(
                jnp.sum(real * start_imag - imag * start_real, axis=0, keepdims=True)
            )
            packed = jnp.where(upper, real, imag)
            top = packed[:half]
            bottom = packed[half:]
            even = jnp.where(left, top, pltpu.roll(bottom, LANES // 2, 1))
            odd = jnp.where(left, pltpu.roll(top, LANES // 2, 1), bottom)
            pack_ref[pl.ds(places[2 * group] * half, half), :] = even
            pack_ref[pl.ds(places[2 * group + 1] * half, half), :] = odd
    resp = jnp.concatenate(resp_real + resp_imag, axis=0)
    pack_ref[pl.ds(NF // 2 * half, RESP_ROWS), :] = resp
    give_half(pack_ref, core_bit() if by_core else 0, keep_ref, send_ref)
    save_low.wait()


def gram_parts(snapshots, weight_rows, start_vec, total_rows, places, by_core):
    times, cols = snapshots.shape
    start = jnp.transpose(start_vec, (1, 2, 0)).reshape(2 * NB, NF)
    pieces = 11
    any_space = pl.BlockSpec(memory_space=pl.ANY)
    saved = jax.ShapeDtypeStruct((-(-times // 256) * 256, cols), jnp.bfloat16)
    half = floats(NF // 4 * NB // 2 + RESP_ROWS, LANES)
    return pl.pallas_call(
        functools.partial(gram_kernel, total_rows, places, by_core),
        out_shape=(half, half, saved, saved),
        in_specs=[any_space] * 2 + [VMEM],
        out_specs=(VMEM, VMEM, VMEM, any_space),
        scratch_shapes=[
            pltpu.VMEM((times, cols), jnp.float32),
            pltpu.VMEM(weight_rows.shape, jnp.float32),
            pltpu.VMEM((4 * NF, 2 * NFFT), jnp.bfloat16),
            pltpu.VMEM(saved.shape, jnp.bfloat16),
            pltpu.VMEM((cols // LANES, 2 * NF // 8, 8 * FREQ_STEP, LANES), jnp.float32),
            pltpu.VMEM((2 * LANES, 2 * cols), jnp.bfloat16),
            pltpu.VMEM((2 * LANES, 2 * cols), jnp.bfloat16),
            pltpu.VMEM((NF // PACK, NB, LANES), jnp.float32),
            pltpu.VMEM((NF // PACK, NB, LANES), jnp.float32),
            pltpu.VMEM((NF // PACK, 2 * NB, LANES), jnp.float32),
            pltpu.VMEM((NF // 2 * NB // 2 + RESP_ROWS, LANES), jnp.float32),
            pltpu.SemaphoreType.DMA((pieces + 1,)),
            pltpu.SemaphoreType.DMA(()),
        ],
        compiler_params=pltpu.CompilerParams(vmem_limit_bytes=VMEM_LIMIT),
        cost_estimate=pl.CostEstimate(
            flops=5_000_000_000, bytes_accessed=8_000_000, transcendentals=0
        ),
        name="gram_parts",
    )(snapshots, weight_rows, start)


def pair_square(even, odd):
    left = lax.broadcasted_iota(jnp.int32, (NB // 2, LANES), 1) < LANES // 2
    top = jnp.where(left, even, pltpu.roll(odd, LANES // 2, 1))
    bottom = jnp.where(left, pltpu.roll(even, LANES // 2, 1), odd)
    return jnp.concatenate([top, bottom], axis=0)


def hermitian(squares):
    row = lax.broadcasted_iota(jnp.int32, (NB, LANES), 0)
    col = lax.broadcasted_iota(jnp.int32, (NB, LANES), 1) % NB
    zero = jnp.zeros((NB, LANES), jnp.float32)
    full = squares + [zero] * (PACK - len(squares))
    turned = flip_groups([zero] * PACK, jnp.concatenate(full, axis=0))
    for square, flipped in zip(squares, turned):
        real = jnp.where(row <= col, square, flipped)
        imag = jnp.where(row > col, square, jnp.where(row < col, -flipped, 0.0))
        yield real, imag


def small_call(kernel, name, out_shape, scratch_shapes=(), limit=SMALL_LIMIT):
    def call(*args):
        return pl.pallas_call(
            kernel,
            out_shape=out_shape,
            in_specs=[VMEM] * len(args),
            out_specs=VMEM if isinstance(out_shape, jax.ShapeDtypeStruct) else (VMEM,) * len(out_shape),
            scratch_shapes=list(scratch_shapes),
            compiler_params=pltpu.CompilerParams(vmem_limit_bytes=limit),
            name=name,
        )(*args)

    return call


def floats(*shape):
    return jax.ShapeDtypeStruct(shape, jnp.float32)


def add_split_kernel(bit, kept_ref, got_ref, keep_ref, send_ref, sum_ref):
    sum_ref[...] = kept_ref[...] + got_ref[...]
    give_half(sum_ref, bit(), keep_ref, send_ref)


def add_split(bit, name, kept, got):
    half = floats((kept.shape[0] - RESP_ROWS) // 2 + RESP_ROWS, LANES)
    scratch = [pltpu.VMEM(kept.shape, jnp.float32)]
    return small_call(functools.partial(add_split_kernel, bit), name, (half, half), scratch)(
        kept, got
    )


def add_kernel(kept_ref, got_ref, out_ref):
    out_ref[...] = kept_ref[...] + got_ref[...]


def add(name, kept, got):
    return small_call(add_kernel, name, floats(*kept.shape))(kept, got)


def finish_kernel(kept_ref, got_ref, packed_ref, resp_ref):
    rows = packed_ref.shape[0]
    packed_ref[...] = kept_ref[pl.ds(0, rows), :] + got_ref[pl.ds(0, rows), :]
    tail = pl.ds(rows, RESP_ROWS)
    resp = kept_ref[tail, :] + got_ref[tail, :]
    real = resp[: RESP_ROWS // 2]
    imag = resp[RESP_ROWS // 2 :]
    power = real * real + imag * imag
    lane = lax.broadcasted_iota(jnp.int32, power.shape, 1)
    mean = jnp.zeros(power.shape, jnp.float32)
    for q in range(PACK):
        mine = lane // NB == q
        part = jnp.sum(jnp.where(mine, power, 0.0), axis=1, keepdims=True) / NB
        mean = jnp.where(mine, part, mean)
    scaling = 1.0 / jnp.sqrt(mean + 1e-06)
    resp_ref[pl.ds(0, RESP_ROWS // 2), :] = real * scaling
    resp_ref[pl.ds(RESP_ROWS // 2, RESP_ROWS // 2), :] = imag * scaling


def finish(kept, got):
    rows = kept.shape[0] - RESP_ROWS
    return small_call(finish_kernel, "finish", (floats(rows, LANES), floats(RESP_ROWS, LANES)))(
        kept, got
    )


def join_y_kernel(own_ref, got_ref, packed_ref):
    rows = own_ref.shape[0]
    for m, ref in enumerate((own_ref, got_ref)):
        packed_ref[pl.ds((y_bit() ^ m) * rows, rows), :] = ref[...]


def unpack_kernel(*refs):
    parts, out_ref = refs[:-1], refs[-1]
    half = NB // 2
    for m, part in enumerate(parts):
        count = part.shape[0] // half
        place = (core_bit() ^ m) * 2 * count if len(parts) > 1 else 0
        for first in range(0, count, 2 * PACK):
            last = min(first + 2 * PACK, count)
            pairs = [part[pl.ds(i * half, half), :] for i in range(first, last)]
            squares = [pair_square(*pairs[i : i + 2]) for i in range(0, len(pairs), 2)]
            for g, both in enumerate(hermitian(squares)):
                for q in range(PACK):
                    freq = place + 2 * first + PACK * g + q
                    for c in range(2):
                        out_ref[freq, c] = both[c][:, q * NB : (q + 1) * NB]


def unpack_gram(*parts):
    count = sum(part.shape[0] for part in parts) * 4 // NB
    return small_call(unpack_kernel, "unpack_gram", floats(count, 2, NB, NB))(*parts)


def modes_kernel(
    total_rows,
    high_ref,
    low_hbm,
    w_ref,
    table_ref,
    resp_ref,
    out_ref,
    low_ref,
    resp_t,
    a_ref,
    sem,
):
    padded, cols = high_ref.shape
    fetch_low = pltpu.make_async_copy(low_hbm, low_ref, sem)
    fetch_low.start()
    tall = jnp.concatenate([resp_ref[...]] * (LANES // RESP_ROWS), axis=0).T
    lane = lax.broadcasted_iota(jnp.int32, (NB, LANES), 1)
    turned = tall[:NB]
    for q in range(1, PACK):
        turned = jnp.where(lane // RESP_ROWS == q, tall[q * NB : (q + 1) * NB], turned)
    groups = RESP_ROWS // 2
    first_part = lane // groups % 2 == 0
    resp_t[0] = jnp.where(first_part, turned, pltpu.roll(turned, groups, 1))
    resp_t[1] = jnp.where(first_part, pltpu.roll(turned, LANES - groups, 1), turned)
    for j in range(padded // HALF):
        value = jnp.zeros((HALF, LANES), jnp.float32)
        for block, start in ((j, 0), (j - 1, HALF)):
            if 0 <= block < NB:
                for part in range(2):
                    value += resp_t[part, pl.ds(block, 1), :] * table_ref[part, pl.ds(start, HALF), :]
        high, low = split(value)
        a_ref[0, pl.ds(j * HALF, HALF), :] = high
        a_ref[1, pl.ds(j * HALF, HALF), :] = low
    dot = functools.partial(
        lax.dot_general,
        dimension_numbers=(((0,), (0,)), ((), ())),
        preferred_element_type=jnp.float32,
    )
    modes = dot(a_ref[0], high_ref[...]) + dot(a_ref[1], high_ref[...])
    fetch_low.wait()
    modes = modes + dot(a_ref[0], low_ref[...])
    modes = modes * jnp.sqrt(2.0 * total_rows / load_weights(w_ref, cols // LANES))
    n_freq = out_ref.shape[0]
    mine = groups // n_freq
    group = lax.axis_index("freq")
    for q in range(PACK):
        for part in range(2):
            for f in range(n_freq):
                first = q * RESP_ROWS + part * groups + f * mine
                slot = f ^ group if n_freq == 2 else f
                for c in range(cols // LANES):
                    out_ref[slot, 2 * c + part, pl.ds(q, mine, stride=PACK), :] = modes[
                        first : first + mine, c * LANES : (c + 1) * LANES
                    ]


def local_modes(high, low, weight_rows, response, total_rows, n_freq):
    padded, cols = high.shape
    return pl.pallas_call(
        functools.partial(modes_kernel, total_rows),
        out_shape=floats(n_freq, 2 * cols // LANES, NF // n_freq, LANES),
        in_specs=[VMEM, pl.BlockSpec(memory_space=pl.ANY)] + [VMEM] * 3,
        out_specs=VMEM,
        scratch_shapes=[
            pltpu.VMEM((padded, cols), jnp.bfloat16),
            pltpu.VMEM((2, NB, LANES), jnp.float32),
            pltpu.VMEM((2, padded, LANES), jnp.bfloat16),
            pltpu.SemaphoreType.DMA(()),
        ],
        compiler_params=pltpu.CompilerParams(vmem_limit_bytes=VMEM_LIMIT),
        name="local_modes",
    )(high, low, weight_rows, jnp.asarray(mode_tables()), response)


def join_kernel(kept_ref, got_ref, out_ref):
    tiles = got_ref.shape[0] // 2
    group = lax.axis_index("freq")
    for slot, ref in enumerate((kept_ref.at[0], got_ref)):
        for c in range(tiles):
            lanes = pl.ds(pl.multiple_of(((group ^ slot) * tiles + c) * LANES, LANES), LANES)
            for part in range(2):
                out_ref[:, part, lanes] = ref[2 * c + part]


def join_modes(kept, got):
    tiles, count, _ = got.shape
    return small_call(join_kernel, "join_modes", floats(count, 2, tiles * LANES))(kept, got)


def response_of(gram, start_vec):
    matvec = functools.partial(jnp.einsum, "fjk,fk->fj", precision=lax.Precision.HIGHEST)
    resp_real = matvec(gram[:, 0], start_vec[:, 0]) - matvec(gram[:, 1], start_vec[:, 1])
    resp_imag = matvec(gram[:, 0], start_vec[:, 1]) + matvec(gram[:, 1], start_vec[:, 0])
    scaling = 1.0 / jnp.sqrt(
        jnp.mean(resp_real * resp_real + resp_imag * resp_imag, axis=1, keepdims=True) + 1e-06
    )
    return jnp.stack([resp_real * scaling, resp_imag * scaling], axis=1)


def direction_shards(n_devices, snapshots, weight, start_vec):
    def swap(value, mask):
        return lax.ppermute(value, ("pts", "freq"), [(i, i ^ mask) for i in range(n_devices)])

    x, core, y, z_near, z_far = 1, 2, 4, 8, 16
    total_rows = float(weight.shape[0] * 16)
    weight_rows = weight.reshape(-1, LANES)
    places = [(i // 8 % 2) * 16 + (i // 16) * 8 + i % 8 for i in range(NF // 2)]
    keep, send, high, low = gram_parts(
        snapshots, weight_rows, start_vec, total_rows, places, True
    )
    keep, send = add_split(lambda: lax.axis_index("freq"), "add_core", keep, swap(send, core))
    keep, send = add_split(y_bit, "add_x", keep, swap(send, x))
    part = add("add_y", keep, swap(send, y))
    part = add("add_z", part, swap(part, z_near))
    packed, response = finish(part, swap(part, z_far))
    other = swap(packed, y)
    modes = local_modes(high, low, weight_rows, response, total_rows, 2)
    packed = small_call(join_y_kernel, "join_y", floats(2 * packed.shape[0], LANES))(packed, other)
    gram_mine = unpack_gram(packed, swap(packed, core))
    return gram_mine, join_modes(modes, swap(modes[1], x))


def shards(n_pts, n_freq, snapshots, weight, start_vec):
    cols = snapshots.shape[1]
    total_rows = float(weight.shape[0] * n_pts)
    n_devices = n_pts * n_freq
    mine_count = NF // n_freq
    group = lax.axis_index("freq")
    weight_rows = weight.reshape(-1, LANES)
    places = list(range(NF // 2))
    first, second, high, low = gram_parts(
        snapshots, weight_rows, start_vec, total_rows, places, False
    )
    parts = jnp.concatenate([first[:-RESP_ROWS], second[:-RESP_ROWS]], axis=0)
    share = parts.reshape(n_devices, -1)
    share = jnp.sum(lax.all_to_all(share, ("freq", "pts"), 0, 0, tiled=True), axis=0)
    packed = lax.all_gather(share, "pts", axis=0, tiled=True)
    gram_mine = unpack_gram(packed.reshape(-1, LANES))
    start_mine = lax.dynamic_slice_in_dim(start_vec, group * mine_count, mine_count, 0)
    response = lax.all_gather(response_of(gram_mine, start_mine), "freq", axis=0, tiled=True)
    response = jnp.transpose(response.reshape(NF // PACK, PACK, 2, NB), (2, 0, 1, 3))
    response = response.reshape(RESP_ROWS, LANES)
    modes = local_modes(high, low, weight_rows, response, total_rows, n_freq)
    modes = lax.all_to_all(modes, "freq", 0, 0, tiled=True)
    modes = modes.reshape(n_freq, cols // LANES, 2, mine_count, LANES)
    modes = jnp.transpose(modes, (3, 2, 0, 1, 4)).reshape(mine_count, 2, n_freq * cols)
    return gram_mine, modes


def solution(mesh):
    n_pts, n_freq = mesh.shape["pts"], mesh.shape["freq"]
    if (n_pts, n_freq) == (16, 2):
        body = functools.partial(direction_shards, n_pts * n_freq)
    else:
        body = functools.partial(shards, n_pts, n_freq)
    placed = (P(None, ("pts", "freq")), P("pts"), P())
    return jax.shard_map(
        body,
        mesh=mesh,
        in_specs=placed,
        out_specs=(P("freq", None, None, None), P("freq", None, "pts")),
        check_vma=False,
    )
```

```python
import functools
import math

import jax
import jax.numpy as jnp
import numpy as np
from jax import lax
from jax.experimental import pallas as pl
from jax.experimental.pallas import tpu as pltpu
from jax.sharding import PartitionSpec as P

NFFT = 128
HALF = NFFT // 2
NF = 64
NB = 32
LANES = 128
PACK = 4
VMEM_LIMIT = 51 * 1024 * 1024
SMALL_LIMIT = 8 * 1024 * 1024
VMEM = pl.BlockSpec(memory_space=pltpu.VMEM)


def dft_values():
    times = np.arange(NFFT)
    freqs = np.arange(NF)
    phases = (freqs[:, None] * times[None, :] % NFFT) * (2.0 * math.pi / NFFT)
    window = 0.5 - 0.5 * np.cos(times * (2.0 * math.pi / NFFT))
    weighted = window / np.sqrt(np.sum(window * window))
    return np.cos(phases) * weighted, -np.sin(phases) * weighted


def split_table(table):
    high = table.astype(jnp.bfloat16)
    low = (table - high.astype(np.float64)).astype(jnp.bfloat16)
    return high, low


def mode_tables():
    real, imag = dft_values()
    order = np.arange(NF).reshape(NF // PACK, PACK).T
    real, imag = real[order], imag[order]
    first = np.stack([real, imag], axis=1).reshape(2 * NF, NFFT)
    second = np.stack([-imag, real], axis=1).reshape(2 * NF, NFFT)
    return np.stack([first, second]).astype(np.float32)


def cosine_of_turns(count):
    folded = jnp.minimum(count, NFFT - count)
    angle = (NFFT // 4 - folded).astype(jnp.float32) * (2.0 * math.pi / NFFT)
    square = angle * angle
    series = 1.0
    for n in (10, 8, 6, 4, 2):
        series = 1.0 - square * series * (1.0 / (n * (n + 1)))
    return angle * series


def fill_dft(dft_ref):
    row = lax.broadcasted_iota(jnp.int32, (2 * NF, NFFT), 0)
    time = lax.broadcasted_iota(jnp.int32, (2 * NF, NFFT), 1)
    quarter = jnp.where(row < NF, 0, NFFT // 4)
    wave = cosine_of_turns((row % NF * time + quarter) % NFFT)
    window = 0.5 - 0.5 * np.cos(np.arange(NFFT) * (2.0 * math.pi / NFFT))
    norm = float(np.sqrt(np.sum(window * window)))
    high, low = split(wave * ((0.5 - 0.5 * cosine_of_turns(time)) / norm))
    dft_ref[pl.ds(0, 2 * NF), pl.ds(0, NFFT)] = high
    dft_ref[pl.ds(0, 2 * NF), pl.ds(NFFT, NFFT)] = high
    dft_ref[pl.ds(2 * NF, 2 * NF), pl.ds(0, NFFT)] = low
    dft_ref[pl.ds(2 * NF, 2 * NF), pl.ds(NFFT, NFFT)] = jnp.zeros((2 * NF, NFFT), jnp.bfloat16)


def spread_start(start_ref, spread_ref):
    row = lax.broadcasted_iota(jnp.int32, (NF, LANES), 0)
    lane = lax.broadcasted_iota(jnp.int32, (NF, LANES), 1)
    start = start_ref[pl.ds(0, 2 * NB), pl.ds(0, NF)]
    for g in range(NF // PACK):
        pick = (row == PACK * g + lane // NB).astype(jnp.float32)
        spread_ref[g] = jnp.dot(
            start,
            pick,
            precision=lax.Precision.HIGHEST,
            preferred_element_type=jnp.float32,
        )


def split(value):
    high = value.astype(jnp.bfloat16)
    low = (value - high.astype(jnp.float32)).astype(jnp.bfloat16)
    return high, low


def load_weights(w_ref, col_tiles):
    first = lax.axis_index("freq") * col_tiles
    return jnp.concatenate([w_ref[pl.ds(first + c, 1), :] for c in range(col_tiles)], axis=1)


def flip_groups(groups, flipped):
    turned = flipped.T
    lane = lax.broadcasted_iota(jnp.int32, (NB, LANES), 1)
    out = []
    for g in range(PACK):
        total = groups[g]
        for q in range(PACK):
            block = turned[q * NB : (q + 1) * NB]
            if q != g:
                block = pltpu.roll(block, ((q - g) % PACK) * NB, 1)
            total = total + jnp.where(lane // NB == q, block, 0.0)
        out.append(total)
    return out


ROW_STEP = 3
FREQ_STEP = ROW_STEP * NB + 1


def core_bit():
    return lax.rem(lax.axis_index("pts"), 2)


def y_bit():
    return lax.rem(lax.div(lax.axis_index("pts"), 2), 2)


RESP_ROWS = 2 * NF // PACK


def give_half(value_ref, bit, keep_ref, send_ref):
    half = keep_ref.shape[0] - RESP_ROWS
    keep_ref[pl.ds(0, half), :] = value_ref[pl.ds(bit * half, half), :]
    send_ref[pl.ds(0, half), :] = value_ref[pl.ds((1 - bit) * half, half), :]
    resp = value_ref[pl.ds(2 * half, RESP_ROWS), :]
    keep_ref[pl.ds(half, RESP_ROWS), :] = resp
    send_ref[pl.ds(half, RESP_ROWS), :] = resp


def gram_kernel(
    total_rows,
    places,
    by_core,
    x_hbm,
    aux_ref,
    keep_ref,
    send_ref,
    high_ref,
    low_hbm,
    x_ref,
    dft_ref,
    low_ref,
    spec_ref,
    z_even,
    z_odd,
    real_ref,
    imag_ref,
    spread_ref,
    pack_ref,
    in_sems,
    out_sem,
):
    times, cols = x_ref.shape
    halves = times // HALF
    col_tiles = cols // LANES
    pieces = in_sems.shape[0]
    piece = times // pieces

    def fetch(i):
        rows = pl.ds(i * piece, piece)
        return pltpu.make_async_copy(x_hbm.at[rows], x_ref.at[rows], in_sems.at[i])

    for i in range(pieces):
        fetch(i).start()
    fill_dft(dft_ref)
    spread_start(aux_ref, spread_ref)

    acc = jnp.zeros((HALF, cols), jnp.float32)
    for i in range(pieces):
        fetch(i).wait()
        for h in range(piece // HALF):
            acc = acc + x_ref[pl.ds(i * piece + h * HALF, HALF), :]
    mean = jnp.sum(acc, axis=0, keepdims=True) / times
    weights = load_weights(aux_ref.at[pl.ds(2 * NB, aux_ref.shape[0] - 2 * NB)], col_tiles)
    scale = jnp.sqrt(weights / (2.0 * total_rows))

    def center(i, carry):
        rows = pl.ds(pl.multiple_of(i * HALF, HALF), HALF)
        high, low = split((x_ref[rows, :] - mean) * scale)
        high_ref[rows, :] = high
        low_ref[rows, :] = low
        return carry

    lax.fori_loop(0, halves, center, 0, unroll=3)
    pad = high_ref.shape[0] - times
    if pad:
        high_ref[pl.ds(times, pad), :] = jnp.zeros((pad, cols), jnp.bfloat16)
        low_ref[pl.ds(times, pad), :] = jnp.zeros((pad, cols), jnp.bfloat16)
    save_low = pltpu.make_async_copy(low_ref, low_hbm, out_sem)
    save_low.start()

    def transform(i, carry):
        blocks = []
        for s in range(2):
            rows = pl.ds(pl.multiple_of((2 * i + s) * HALF, HALF), NFFT)
            blocks.append(jnp.concatenate([high_ref[rows, :], low_ref[rows, :]], axis=0))
        both = jnp.dot(
            dft_ref[...], jnp.concatenate(blocks, axis=1), preferred_element_type=jnp.float32
        )
        spectrum = both[: 2 * NF] + both[2 * NF :]
        for s in range(2):
            for o in range(2 * NF // 8):
                for c in range(col_tiles):
                    first = s * cols + c * LANES
                    rows = pl.ds(ROW_STEP * (2 * i + s), 8, stride=FREQ_STEP)
                    spec_ref[c, o, rows, :] = spectrum[8 * o : 8 * o + 8, first : first + LANES]
        return carry

    lax.fori_loop(0, NB // 2, transform, 0, unroll=2)

    row = lax.broadcasted_iota(jnp.int32, (NB, LANES), 0)
    lane = lax.broadcasted_iota(jnp.int32, (NB, LANES), 1)
    upper = row <= lane % NB
    octets = NF // 8

    def prepare(z_ref, octet, half):
        for part in range(2):
            for q in range(PACK):
                rows = pl.ds(FREQ_STEP * (PACK * half + q), NB, stride=ROW_STEP)
                own = pl.ds(part * LANES + q * NB, NB)
                for c in range(col_tiles):
                    value = spec_ref[c, octet + octets * part, rows, :]
                    high = value.astype(jnp.bfloat16)
                    low = (2.0 * (value - high.astype(jnp.float32))).astype(jnp.bfloat16)
                    z_ref[own, pl.ds(c * LANES, LANES)] = high
                    z_ref[own, pl.ds(cols + c * LANES, LANES)] = low

    def correlate(z_ref, group):
        high = z_ref[:, pl.ds(0, cols)]
        product = lax.dot_general(
            jnp.concatenate([high, high], axis=1),
            z_ref[...],
            (((1,), (1,)), ((), ())),
            preferred_element_type=jnp.float32,
        )
        gram_real = jnp.zeros((NB, LANES), jnp.float32)
        gram_imag = jnp.zeros((NB, LANES), jnp.float32)
        for q in range(PACK):
            mine = lane // NB == q
            real = product[q * NB : (q + 1) * NB]
            imag = product[LANES + q * NB : LANES + (q + 1) * NB]
            gram_real = jnp.where(mine, real[:, :LANES] + imag[:, LANES:], gram_real)
            gram_imag = jnp.where(mine, real[:, LANES:] - imag[:, :LANES], gram_imag)
        real_ref[group] = gram_real
        imag_ref[group] = gram_imag

    prepare(z_even, 0, 0)

    def step(o, carry):
        prepare(z_odd, o, 1)
        correlate(z_even, 2 * o)
        prepare(z_even, jnp.minimum(o + 1, octets - 1), 0)
        correlate(z_odd, 2 * o + 1)
        return carry

    lax.fori_loop(0, octets, step, 0)
    left = lane[: NB // 2] < LANES // 2
    half = NB // 2
    resp_real = []
    resp_imag = []
    for quad in range(NF // PACK // PACK):
        own = pl.ds(quad * PACK, PACK)
        reals = [real_ref[quad * PACK + g] for g in range(PACK)]
        imags = [imag_ref[quad * PACK + g] for g in range(PACK)]
        reals = flip_groups(reals, real_ref[own].reshape(PACK * NB, LANES))
        imags = flip_groups(imags, -imag_ref[own].reshape(PACK * NB, LANES))
        for g, (real, imag) in enumerate(zip(reals, imags)):
            group = quad * PACK + g
            start_real = spread_ref[group, pl.ds(0, NB), :]
            start_imag = spread_ref[group, pl.ds(NB, NB), :]
            resp_real.append(
                jnp.sum(real * start_real + imag * start_imag, axis=0, keepdims=True)
            )
            resp_imag.append(
                jnp.sum(real * start_imag - imag * start_real, axis=0, keepdims=True)
            )
            packed = jnp.where(upper, real, imag)
            top = packed[:half]
            bottom = packed[half:]
            even = jnp.where(left, top, pltpu.roll(bottom, LANES // 2, 1))
            odd = jnp.where(left, pltpu.roll(top, LANES // 2, 1), bottom)
            pack_ref[pl.ds(places[2 * group] * half, half), :] = even
            pack_ref[pl.ds(places[2 * group + 1] * half, half), :] = odd
    resp = jnp.concatenate(resp_real + resp_imag, axis=0)
    pack_ref[pl.ds(NF // 2 * half, RESP_ROWS), :] = resp
    give_half(pack_ref, core_bit() if by_core else 0, keep_ref, send_ref)
    save_low.wait()


def gram_parts(snapshots, weight_rows, start_vec, total_rows, places, by_core):
    times, cols = snapshots.shape
    start = jnp.transpose(start_vec, (1, 2, 0)).reshape(2 * NB, NF)
    start = jnp.pad(start, ((0, 0), (0, LANES - NF)))
    aux = jnp.concatenate([start, weight_rows], axis=0)
    pieces = 11
    any_space = pl.BlockSpec(memory_space=pl.ANY)
    saved = jax.ShapeDtypeStruct((-(-times // LANES) * LANES, cols), jnp.bfloat16)
    half = floats(NF // 4 * NB // 2 + RESP_ROWS, LANES)
    return pl.pallas_call(
        functools.partial(gram_kernel, total_rows, places, by_core),
        out_shape=(half, half, saved, saved),
        in_specs=[any_space, VMEM],
        out_specs=(VMEM, VMEM, VMEM, any_space),
        scratch_shapes=[
            pltpu.VMEM((times, cols), jnp.float32),
            pltpu.VMEM((4 * NF, 2 * NFFT), jnp.bfloat16),
            pltpu.VMEM(saved.shape, jnp.bfloat16),
            pltpu.VMEM((cols // LANES, 2 * NF // 8, 8 * FREQ_STEP, LANES), jnp.float32),
            pltpu.VMEM((2 * LANES, 2 * cols), jnp.bfloat16),
            pltpu.VMEM((2 * LANES, 2 * cols), jnp.bfloat16),
            pltpu.VMEM((NF // PACK, NB, LANES), jnp.float32),
            pltpu.VMEM((NF // PACK, NB, LANES), jnp.float32),
            pltpu.VMEM((NF // PACK, 2 * NB, LANES), jnp.float32),
            pltpu.VMEM((NF // 2 * NB // 2 + RESP_ROWS, LANES), jnp.float32),
            pltpu.SemaphoreType.DMA((pieces,)),
            pltpu.SemaphoreType.DMA(()),
        ],
        compiler_params=pltpu.CompilerParams(vmem_limit_bytes=VMEM_LIMIT),
        cost_estimate=pl.CostEstimate(
            flops=5_000_000_000, bytes_accessed=8_000_000, transcendentals=0
        ),
        name="gram_parts",
    )(snapshots, aux)


def pair_square(even, odd):
    left = lax.broadcasted_iota(jnp.int32, (NB // 2, LANES), 1) < LANES // 2
    top = jnp.where(left, even, pltpu.roll(odd, LANES // 2, 1))
    bottom = jnp.where(left, pltpu.roll(even, LANES // 2, 1), odd)
    return jnp.concatenate([top, bottom], axis=0)


def hermitian(squares):
    row = lax.broadcasted_iota(jnp.int32, (NB, LANES), 0)
    col = lax.broadcasted_iota(jnp.int32, (NB, LANES), 1) % NB
    zero = jnp.zeros((NB, LANES), jnp.float32)
    full = squares + [zero] * (PACK - len(squares))
    turned = flip_groups([zero] * PACK, jnp.concatenate(full, axis=0))
    for square, flipped in zip(squares, turned):
        real = jnp.where(row <= col, square, flipped)
        imag = jnp.where(row > col, square, jnp.where(row < col, -flipped, 0.0))
        yield real, imag


def small_call(kernel, name, out_shape, scratch_shapes=(), limit=SMALL_LIMIT):
    def call(*args):
        return pl.pallas_call(
            kernel,
            out_shape=out_shape,
            in_specs=[VMEM] * len(args),
            out_specs=VMEM if isinstance(out_shape, jax.ShapeDtypeStruct) else (VMEM,) * len(out_shape),
            scratch_shapes=list(scratch_shapes),
            compiler_params=pltpu.CompilerParams(vmem_limit_bytes=limit),
            name=name,
        )(*args)

    return call


def floats(*shape):
    return jax.ShapeDtypeStruct(shape, jnp.float32)


def add_core_kernel(kept_ref, got_ref, out_ref):
    quarter = out_ref.shape[1] - RESP_ROWS
    tail = pl.ds(4 * quarter, RESP_ROWS)
    resp = kept_ref[tail, :] + got_ref[tail, :]
    for m in range(4):
        rows = pl.ds(m * quarter, quarter)
        out_ref[m, pl.ds(0, quarter), :] = kept_ref[rows, :] + got_ref[rows, :]
        out_ref[m, pl.ds(quarter, RESP_ROWS), :] = resp


def add_core(kept, got):
    quarter = (kept.shape[0] - RESP_ROWS) // 4
    return small_call(add_core_kernel, "add_core", floats(4, quarter + RESP_ROWS, LANES))(kept, got)


def add_near_kernel(parts_ref, out_ref):
    out_ref[...] = (parts_ref[0] + parts_ref[1]) + (parts_ref[2] + parts_ref[3])


def add_kernel(kept_ref, got_ref, out_ref):
    out_ref[...] = kept_ref[...] + got_ref[...]


def add(name, kept, got):
    return small_call(add_kernel, name, floats(*kept.shape))(kept, got)


def finish_kernel(kept_ref, got_ref, packed_ref, resp_ref):
    rows = packed_ref.shape[0]
    packed_ref[...] = kept_ref[pl.ds(0, rows), :] + got_ref[pl.ds(0, rows), :]
    tail = pl.ds(rows, RESP_ROWS)
    resp = kept_ref[tail, :] + got_ref[tail, :]
    real = resp[: RESP_ROWS // 2]
    imag = resp[RESP_ROWS // 2 :]
    power = real * real + imag * imag
    lane = lax.broadcasted_iota(jnp.int32, power.shape, 1)
    mean = jnp.zeros(power.shape, jnp.float32)
    for q in range(PACK):
        mine = lane // NB == q
        part = jnp.sum(jnp.where(mine, power, 0.0), axis=1, keepdims=True) / NB
        mean = jnp.where(mine, part, mean)
    scaling = 1.0 / jnp.sqrt(mean + 1e-06)
    resp_ref[pl.ds(0, RESP_ROWS // 2), :] = real * scaling
    resp_ref[pl.ds(RESP_ROWS // 2, RESP_ROWS // 2), :] = imag * scaling


def finish(kept, got):
    rows = kept.shape[0] - RESP_ROWS
    return small_call(finish_kernel, "finish", (floats(rows, LANES), floats(RESP_ROWS, LANES)))(
        kept, got
    )


def join_y_kernel(own_ref, got_ref, packed_ref):
    rows = own_ref.shape[0]
    for m, ref in enumerate((own_ref, got_ref)):
        packed_ref[pl.ds((y_bit() ^ m) * rows, rows), :] = ref[...]


def unpack_kernel(*refs):
    parts, out_ref = refs[:-1], refs[-1]
    half = NB // 2
    for m, part in enumerate(parts):
        count = part.shape[0] // half
        place = (core_bit() ^ m) * 2 * count if len(parts) > 1 else 0
        for first in range(0, count, 2 * PACK):
            last = min(first + 2 * PACK, count)
            pairs = [part[pl.ds(i * half, half), :] for i in range(first, last)]
            squares = [pair_square(*pairs[i : i + 2]) for i in range(0, len(pairs), 2)]
            for g, both in enumerate(hermitian(squares)):
                for q in range(PACK):
                    freq = place + 2 * first + PACK * g + q
                    for c in range(2):
                        out_ref[freq, c] = both[c][:, q * NB : (q + 1) * NB]


def unpack_gram(*parts):
    count = sum(part.shape[0] for part in parts) * 4 // NB
    return small_call(unpack_kernel, "unpack_gram", floats(count, 2, NB, NB))(*parts)


def modes_kernel(
    total_rows, high_ref, low_hbm, w_ref, table_ref, resp_ref, out_ref, low_ref, a_ref, sem
):
    padded, cols = high_ref.shape
    fetch_low = pltpu.make_async_copy(low_hbm, low_ref, sem)
    fetch_low.start()
    groups = RESP_ROWS // 2
    lane = lax.broadcasted_iota(jnp.int32, (RESP_ROWS, LANES), 1)
    left = lane < HALF
    for q in range(PACK):
        resp = resp_ref[...]
        if q:
            resp = pltpu.roll(resp, LANES - q * NB, 1)
        real = jnp.concatenate([resp[:groups]] * 2, axis=0)
        imag = jnp.concatenate([resp[groups:]] * 2, axis=0)
        rows = pl.ds(q * RESP_ROWS, RESP_ROWS)
        first = table_ref[0, rows, :]
        second = table_ref[1, rows, :]
        first_turned = pltpu.roll(first, HALF, 1)
        second_turned = pltpu.roll(second, HALF, 1)

        def spread(value, block):
            if 0 <= block < NB:
                return jnp.broadcast_to(value[:, block : block + 1], (RESP_ROWS, LANES))
            return jnp.zeros((RESP_ROWS, LANES), jnp.float32)

        for m in range(padded // LANES):
            value = first_turned * jnp.where(left, spread(real, 2 * m - 1), spread(real, 2 * m + 1))
            value += second_turned * jnp.where(
                left, spread(imag, 2 * m - 1), spread(imag, 2 * m + 1)
            )
            if 2 * m < NB:
                value += first * spread(real, 2 * m) + second * spread(imag, 2 * m)
            high, low = split(value)
            own = pl.ds(m * LANES, LANES)
            a_ref[rows, own] = high
            a_ref[pl.ds(2 * NF + q * RESP_ROWS, RESP_ROWS), own] = low
    both = jnp.dot(a_ref[...], high_ref[...], preferred_element_type=jnp.float32)
    modes = both[: 2 * NF] + both[2 * NF :]
    fetch_low.wait()
    modes += jnp.dot(
        a_ref[pl.ds(0, 2 * NF), :], low_ref[...], preferred_element_type=jnp.float32
    )
    modes = modes * jnp.sqrt(2.0 * total_rows / load_weights(w_ref, cols // LANES))
    n_freq = out_ref.shape[0]
    mine = groups // n_freq
    group = lax.axis_index("freq")
    for q in range(PACK):
        for part in range(2):
            for f in range(n_freq):
                first = q * RESP_ROWS + part * groups + f * mine
                slot = f ^ group if n_freq == 2 else f
                for c in range(cols // LANES):
                    out_ref[slot, 2 * c + part, pl.ds(q, mine, stride=PACK), :] = modes[
                        first : first + mine, c * LANES : (c + 1) * LANES
                    ]


def local_modes(high, low, weight_rows, response, total_rows, n_freq):
    padded, cols = high.shape
    return pl.pallas_call(
        functools.partial(modes_kernel, total_rows),
        out_shape=floats(n_freq, 2 * cols // LANES, NF // n_freq, LANES),
        in_specs=[VMEM, pl.BlockSpec(memory_space=pl.ANY)] + [VMEM] * 3,
        out_specs=VMEM,
        scratch_shapes=[
            pltpu.VMEM((padded, cols), jnp.bfloat16),
            pltpu.VMEM((4 * NF, padded), jnp.bfloat16),
            pltpu.SemaphoreType.DMA(()),
        ],
        compiler_params=pltpu.CompilerParams(vmem_limit_bytes=VMEM_LIMIT),
        cost_estimate=pl.CostEstimate(
            flops=3_000_000_000, bytes_accessed=8_000_000, transcendentals=0
        ),
        name="local_modes",
    )(high, low, weight_rows, jnp.asarray(mode_tables()), response)


def join_kernel(kept_ref, got_ref, out_ref):
    tiles = got_ref.shape[0] // 2
    group = lax.axis_index("freq")
    for slot, ref in enumerate((kept_ref.at[0], got_ref)):
        for c in range(tiles):
            lanes = pl.ds(pl.multiple_of(((group ^ slot) * tiles + c) * LANES, LANES), LANES)
            for part in range(2):
                out_ref[:, part, lanes] = ref[2 * c + part]


def join_modes(kept, got):
    tiles, count, _ = got.shape
    return small_call(join_kernel, "join_modes", floats(count, 2, tiles * LANES))(kept, got)


def response_of(gram, start_vec):
    matvec = functools.partial(jnp.einsum, "fjk,fk->fj", precision=lax.Precision.HIGHEST)
    resp_real = matvec(gram[:, 0], start_vec[:, 0]) - matvec(gram[:, 1], start_vec[:, 1])
    resp_imag = matvec(gram[:, 0], start_vec[:, 1]) + matvec(gram[:, 1], start_vec[:, 0])
    scaling = 1.0 / jnp.sqrt(
        jnp.mean(resp_real * resp_real + resp_imag * resp_imag, axis=1, keepdims=True) + 1e-06
    )
    return jnp.stack([resp_real * scaling, resp_imag * scaling], axis=1)


def direction_shards(n_devices, snapshots, weight, start_vec):
    def swap(value, mask):
        return lax.ppermute(value, ("pts", "freq"), [(i, i ^ mask) for i in range(n_devices)])

    x, core, y, z_near, z_far = 1, 2, 4, 8, 16
    near = [
        [first + far, first + far + x, first + far + y, first + far + y + x]
        for far in range(0, n_devices, z_near)
        for first in (0, core)
    ]
    total_rows = float(weight.shape[0] * 16)
    weight_rows = weight.reshape(-1, LANES)
    places = [
        (i // 8 % 2) * 16 + (i // 4 % 2) * 8 + (i // 16) * 4 + i % 4 for i in range(NF // 2)
    ]
    keep, send, high, low = gram_parts(
        snapshots, weight_rows, start_vec, total_rows, places, True
    )
    parts = add_core(keep, swap(send, core))
    parts = lax.all_to_all(
        parts, ("pts", "freq"), 0, 0, axis_index_groups=near, tiled=True
    )
    part = small_call(add_near_kernel, "add_near", floats(*parts.shape[1:]))(parts)
    part = add("add_z", part, swap(part, z_near))
    packed, response = finish(part, swap(part, z_far))
    other = swap(packed, y)
    modes = local_modes(high, low, weight_rows, response, total_rows, 2)
    packed = small_call(join_y_kernel, "join_y", floats(2 * packed.shape[0], LANES))(packed, other)
    gram_mine = unpack_gram(packed, swap(packed, core))
    return gram_mine, join_modes(modes, swap(modes[1], x))


def shards(n_pts, n_freq, snapshots, weight, start_vec):
    cols = snapshots.shape[1]
    total_rows = float(weight.shape[0] * n_pts)
    n_devices = n_pts * n_freq
    mine_count = NF // n_freq
    group = lax.axis_index("freq")
    weight_rows = weight.reshape(-1, LANES)
    places = list(range(NF // 2))
    first, second, high, low = gram_parts(
        snapshots, weight_rows, start_vec, total_rows, places, False
    )
    parts = jnp.concatenate([first[:-RESP_ROWS], second[:-RESP_ROWS]], axis=0)
    share = parts.reshape(n_devices, -1)
    share = jnp.sum(lax.all_to_all(share, ("freq", "pts"), 0, 0, tiled=True), axis=0)
    packed = lax.all_gather(share, "pts", axis=0, tiled=True)
    gram_mine = unpack_gram(packed.reshape(-1, LANES))
    start_mine = lax.dynamic_slice_in_dim(start_vec, group * mine_count, mine_count, 0)
    response = lax.all_gather(response_of(gram_mine, start_mine), "freq", axis=0, tiled=True)
    response = jnp.transpose(response.reshape(NF // PACK, PACK, 2, NB), (2, 0, 1, 3))
    response = response.reshape(RESP_ROWS, LANES)
    modes = local_modes(high, low, weight_rows, response, total_rows, n_freq)
    modes = lax.all_to_all(modes, "freq", 0, 0, tiled=True)
    modes = modes.reshape(n_freq, cols // LANES, 2, mine_count, LANES)
    modes = jnp.transpose(modes, (3, 2, 0, 1, 4)).reshape(mine_count, 2, n_freq * cols)
    return gram_mine, modes


def solution(mesh):
    n_pts, n_freq = mesh.shape["pts"], mesh.shape["freq"]
    if (n_pts, n_freq) == (16, 2):
        body = functools.partial(direction_shards, n_pts * n_freq)
    else:
        body = functools.partial(shards, n_pts, n_freq)
    placed = (P(None, ("pts", "freq")), P("pts"), P())
    return jax.shard_map(
        body,
        mesh=mesh,
        in_specs=placed,
        out_specs=(P("freq", None, None, None), P("freq", None, "pts")),
        check_vma=False,
    )
```

```python
import functools
import math

import jax
import jax.numpy as jnp
import numpy as np
from jax import lax
from jax.experimental import pallas as pl
from jax.experimental.pallas import tpu as pltpu
from jax.sharding import PartitionSpec as P

NFFT = 128
HALF = NFFT // 2
NF = 64
NB = 32
LANES = 128
PACK = 4
VMEM_LIMIT = 51 * 1024 * 1024
SMALL_LIMIT = 8 * 1024 * 1024
VMEM = pl.BlockSpec(memory_space=pltpu.VMEM)


def dft_values():
    times = np.arange(NFFT)
    freqs = np.arange(NF)
    phases = (freqs[:, None] * times[None, :] % NFFT) * (2.0 * math.pi / NFFT)
    window = 0.5 - 0.5 * np.cos(times * (2.0 * math.pi / NFFT))
    weighted = window / np.sqrt(np.sum(window * window))
    return np.cos(phases) * weighted, -np.sin(phases) * weighted


def split_table(table):
    high = table.astype(jnp.bfloat16)
    low = (table - high.astype(np.float64)).astype(jnp.bfloat16)
    return high, low


def window_leaks():
    real, _ = dft_values()
    return [float(np.sum(real[k])) for k in range(2)]


def mode_tables():
    real, imag = dft_values()
    order = np.arange(NF).reshape(NF // PACK, PACK).T
    real, imag = real[order], imag[order]
    first = np.stack([real, imag], axis=1).reshape(2 * NF, NFFT)
    second = np.stack([-imag, real], axis=1).reshape(2 * NF, NFFT)
    return np.stack([first, second]).astype(np.float32)


def cosine_of_turns(count):
    folded = jnp.minimum(count, NFFT - count)
    angle = (NFFT // 4 - folded).astype(jnp.float32) * (2.0 * math.pi / NFFT)
    square = angle * angle
    series = 1.0
    for n in (10, 8, 6, 4, 2):
        series = 1.0 - square * series * (1.0 / (n * (n + 1)))
    return angle * series


def fill_dft(dft_ref):
    row = lax.broadcasted_iota(jnp.int32, (2 * NF, NFFT), 0)
    time = lax.broadcasted_iota(jnp.int32, (2 * NF, NFFT), 1)
    quarter = jnp.where(row < NF, 0, NFFT // 4)
    wave = cosine_of_turns((row % NF * time + quarter) % NFFT)
    window = 0.5 - 0.5 * np.cos(np.arange(NFFT) * (2.0 * math.pi / NFFT))
    norm = float(np.sqrt(np.sum(window * window)))
    high, low = split(wave * ((0.5 - 0.5 * cosine_of_turns(time)) / norm))
    dft_ref[pl.ds(0, 2 * NF), pl.ds(0, NFFT)] = high
    dft_ref[pl.ds(0, 2 * NF), pl.ds(NFFT, NFFT)] = high
    dft_ref[pl.ds(2 * NF, 2 * NF), pl.ds(0, NFFT)] = low
    dft_ref[pl.ds(2 * NF, 2 * NF), pl.ds(NFFT, NFFT)] = jnp.zeros((2 * NF, NFFT), jnp.bfloat16)


def spread_start(start_ref, spread_ref):
    row = lax.broadcasted_iota(jnp.int32, (NF, LANES), 0)
    lane = lax.broadcasted_iota(jnp.int32, (NF, LANES), 1)
    start = start_ref[pl.ds(0, 2 * NB), pl.ds(0, NF)]
    for g in range(NF // PACK):
        pick = (row == PACK * g + lane // NB).astype(jnp.float32)
        spread_ref[g] = jnp.dot(
            start,
            pick,
            precision=lax.Precision.HIGHEST,
            preferred_element_type=jnp.float32,
        )


def split(value):
    high = value.astype(jnp.bfloat16)
    low = (value - high.astype(jnp.float32)).astype(jnp.bfloat16)
    return high, low


def load_weights(w_ref, col_tiles):
    first = lax.axis_index("freq") * col_tiles
    return jnp.concatenate([w_ref[pl.ds(first + c, 1), :] for c in range(col_tiles)], axis=1)


def flip_groups(groups, flipped):
    turned = flipped.T
    lane = lax.broadcasted_iota(jnp.int32, (NB, LANES), 1)
    out = []
    for g in range(PACK):
        total = groups[g]
        for q in range(PACK):
            block = turned[q * NB : (q + 1) * NB]
            if q != g:
                block = pltpu.roll(block, ((q - g) % PACK) * NB, 1)
            total = total + jnp.where(lane // NB == q, block, 0.0)
        out.append(total)
    return out


ROW_STEP = 3
FREQ_STEP = ROW_STEP * NB + 1


def core_bit():
    return lax.rem(lax.axis_index("pts"), 2)


def y_bit():
    return lax.rem(lax.div(lax.axis_index("pts"), 2), 2)


RESP_ROWS = 2 * NF // PACK


def give_half(value_ref, bit, keep_ref, send_ref):
    half = keep_ref.shape[0] - RESP_ROWS
    keep_ref[pl.ds(0, half), :] = value_ref[pl.ds(bit * half, half), :]
    send_ref[pl.ds(0, half), :] = value_ref[pl.ds((1 - bit) * half, half), :]
    resp = value_ref[pl.ds(2 * half, RESP_ROWS), :]
    keep_ref[pl.ds(half, RESP_ROWS), :] = resp
    send_ref[pl.ds(half, RESP_ROWS), :] = resp


def gram_kernel(
    total_rows,
    places,
    by_core,
    x_hbm,
    aux_ref,
    keep_ref,
    send_ref,
    high_ref,
    rest_ref,
    low_hbm,
    x_ref,
    dft_ref,
    low_ref,
    spec_ref,
    z_even,
    z_odd,
    real_ref,
    imag_ref,
    spread_ref,
    pack_ref,
    in_sems,
    out_sem,
):
    times, cols = x_ref.shape
    col_tiles = cols // LANES
    pieces = NB // 2
    tail = times - pieces * NFFT

    def piece_rows(i):
        return pl.ds(i * NFFT, NFFT) if isinstance(i, int) else pl.ds(pl.multiple_of(i * NFFT, NFFT), NFFT)

    def fetch(i):
        rows = piece_rows(i)
        return pltpu.make_async_copy(x_hbm.at[rows], x_ref.at[rows], in_sems.at[i])

    tail_rows = pl.ds(pieces * NFFT, tail)
    fetch_tail = pltpu.make_async_copy(x_hbm.at[tail_rows], x_ref.at[tail_rows], in_sems.at[pieces])
    for i in range(pieces):
        fetch(i).start()
    fetch_tail.start()
    fill_dft(dft_ref)
    spread_start(aux_ref, spread_ref)
    weights = load_weights(aux_ref.at[pl.ds(2 * NB, aux_ref.shape[0] - 2 * NB)], col_tiles)
    scale = jnp.sqrt(weights / (2.0 * total_rows))
    fetch(0).wait()
    first_mean = jnp.mean(x_ref[pl.ds(0, NFFT), :], axis=0, keepdims=True)

    def center(rows, acc):
        value = x_ref[rows, :] - first_mean
        high, low = split(value * scale)
        high_ref[rows, :] = high
        low_ref[rows, :] = low
        for h in range(value.shape[0] // HALF):
            acc = acc + value[h * HALF : (h + 1) * HALF]
        return acc

    def transform(i):
        blocks = []
        for s in range(2):
            start = (2 * i + s) * HALF
            rows = pl.ds(start if isinstance(i, int) else pl.multiple_of(start, HALF), NFFT)
            blocks.append(jnp.concatenate([high_ref[rows, :], low_ref[rows, :]], axis=0))
        both = jnp.dot(
            dft_ref[...], jnp.concatenate(blocks, axis=1), preferred_element_type=jnp.float32
        )
        return both[: 2 * NF] + both[2 * NF :]

    def store(i, spectrum):
        for s in range(2):
            for o in range(2 * NF // 8):
                for c in range(col_tiles):
                    first = s * cols + c * LANES
                    rows = pl.ds(ROW_STEP * (2 * i + s), 8, stride=FREQ_STEP)
                    spec_ref[c, o, rows, :] = spectrum[8 * o : 8 * o + 8, first : first + LANES]

    acc = center(piece_rows(0), jnp.zeros((HALF, cols), jnp.float32))
    fetch(1).wait()
    acc = center(piece_rows(1), acc)

    def stream(i, acc):
        fetch(i + 2).wait()
        spectrum = transform(i)
        acc = center(piece_rows(i + 2), acc)
        store(i, spectrum)
        return acc

    acc = lax.fori_loop(0, pieces - 2, stream, acc, unroll=2)
    fetch_tail.wait()
    spectrum = transform(pieces - 2)
    acc = center(tail_rows, acc)
    store(pieces - 2, spectrum)
    store(pieces - 1, transform(pieces - 1))
    pad = high_ref.shape[0] - times
    if pad:
        high_ref[pl.ds(times, pad), :] = jnp.zeros((pad, cols), jnp.bfloat16)
        low_ref[pl.ds(times, pad), :] = jnp.zeros((pad, cols), jnp.bfloat16)
    save_low = pltpu.make_async_copy(low_ref, low_hbm, out_sem)
    save_low.start()
    rest = jnp.sum(acc, axis=0, keepdims=True) / times * scale
    rest_ref[...] = jnp.broadcast_to(rest, rest_ref.shape)
    for k, leak in enumerate(window_leaks()):
        rows = pl.ds(FREQ_STEP * k, NB, stride=ROW_STEP)
        for c in range(col_tiles):
            part = rest[:, c * LANES : (c + 1) * LANES]
            spec_ref[c, 0, rows, :] = spec_ref[c, 0, rows, :] - leak * part

    row = lax.broadcasted_iota(jnp.int32, (NB, LANES), 0)
    lane = lax.broadcasted_iota(jnp.int32, (NB, LANES), 1)
    upper = row <= lane % NB
    octets = NF // 8

    def prepare(z_ref, octet, half):
        for part in range(2):
            for q in range(PACK):
                rows = pl.ds(FREQ_STEP * (PACK * half + q), NB, stride=ROW_STEP)
                own = pl.ds(part * LANES + q * NB, NB)
                for c in range(col_tiles):
                    value = spec_ref[c, octet + octets * part, rows, :]
                    high = value.astype(jnp.bfloat16)
                    low = (2.0 * (value - high.astype(jnp.float32))).astype(jnp.bfloat16)
                    z_ref[own, pl.ds(c * LANES, LANES)] = high
                    z_ref[own, pl.ds(cols + c * LANES, LANES)] = low

    def correlate(z_ref, group):
        high = z_ref[:, pl.ds(0, cols)]
        product = lax.dot_general(
            jnp.concatenate([high, high], axis=1),
            z_ref[...],
            (((1,), (1,)), ((), ())),
            preferred_element_type=jnp.float32,
        )
        gram_real = jnp.zeros((NB, LANES), jnp.float32)
        gram_imag = jnp.zeros((NB, LANES), jnp.float32)
        for q in range(PACK):
            mine = lane // NB == q
            real = product[q * NB : (q + 1) * NB]
            imag = product[LANES + q * NB : LANES + (q + 1) * NB]
            gram_real = jnp.where(mine, real[:, :LANES] + imag[:, LANES:], gram_real)
            gram_imag = jnp.where(mine, real[:, LANES:] - imag[:, :LANES], gram_imag)
        real_ref[group] = gram_real
        imag_ref[group] = gram_imag

    prepare(z_even, 0, 0)

    def step(o, carry):
        prepare(z_odd, o, 1)
        correlate(z_even, 2 * o)
        prepare(z_even, jnp.minimum(o + 1, octets - 1), 0)
        correlate(z_odd, 2 * o + 1)
        return carry

    lax.fori_loop(0, octets, step, 0)
    left = lane[: NB // 2] < LANES // 2
    half = NB // 2
    resp_real = []
    resp_imag = []
    for quad in range(NF // PACK // PACK):
        own = pl.ds(quad * PACK, PACK)
        reals = [real_ref[quad * PACK + g] for g in range(PACK)]
        imags = [imag_ref[quad * PACK + g] for g in range(PACK)]
        reals = flip_groups(reals, real_ref[own].reshape(PACK * NB, LANES))
        imags = flip_groups(imags, -imag_ref[own].reshape(PACK * NB, LANES))
        for g, (real, imag) in enumerate(zip(reals, imags)):
            group = quad * PACK + g
            start_real = spread_ref[group, pl.ds(0, NB), :]
            start_imag = spread_ref[group, pl.ds(NB, NB), :]
            resp_real.append(
                jnp.sum(real * start_real + imag * start_imag, axis=0, keepdims=True)
            )
            resp_imag.append(
                jnp.sum(real * start_imag - imag * start_real, axis=0, keepdims=True)
            )
            packed = jnp.where(upper, real, imag)
            top = packed[:half]
            bottom = packed[half:]
            even = jnp.where(left, top, pltpu.roll(bottom, LANES // 2, 1))
            odd = jnp.where(left, pltpu.roll(top, LANES // 2, 1), bottom)
            pack_ref[pl.ds(places[2 * group] * half, half), :] = even
            pack_ref[pl.ds(places[2 * group + 1] * half, half), :] = odd
    resp = jnp.concatenate(resp_real + resp_imag, axis=0)
    pack_ref[pl.ds(NF // 2 * half, RESP_ROWS), :] = resp
    give_half(pack_ref, core_bit() if by_core else 0, keep_ref, send_ref)
    save_low.wait()


def gram_parts(snapshots, weight_rows, start_vec, total_rows, places, by_core):
    times, cols = snapshots.shape
    start = jnp.transpose(start_vec, (1, 2, 0)).reshape(2 * NB, NF)
    start = jnp.pad(start, ((0, 0), (0, LANES - NF)))
    aux = jnp.concatenate([start, weight_rows], axis=0)
    any_space = pl.BlockSpec(memory_space=pl.ANY)
    saved = jax.ShapeDtypeStruct((-(-times // LANES) * LANES, cols), jnp.bfloat16)
    half = floats(NF // 4 * NB // 2 + RESP_ROWS, LANES)
    return pl.pallas_call(
        functools.partial(gram_kernel, total_rows, places, by_core),
        out_shape=(half, half, saved, floats(8, cols), saved),
        in_specs=[any_space, VMEM],
        out_specs=(VMEM, VMEM, VMEM, VMEM, any_space),
        scratch_shapes=[
            pltpu.VMEM((times, cols), jnp.float32),
            pltpu.VMEM((4 * NF, 2 * NFFT), jnp.bfloat16),
            pltpu.VMEM(saved.shape, jnp.bfloat16),
            pltpu.VMEM((cols // LANES, 2 * NF // 8, 8 * FREQ_STEP, LANES), jnp.float32),
            pltpu.VMEM((2 * LANES, 2 * cols), jnp.bfloat16),
            pltpu.VMEM((2 * LANES, 2 * cols), jnp.bfloat16),
            pltpu.VMEM((NF // PACK, NB, LANES), jnp.float32),
            pltpu.VMEM((NF // PACK, NB, LANES), jnp.float32),
            pltpu.VMEM((NF // PACK, 2 * NB, LANES), jnp.float32),
            pltpu.VMEM((NF // 2 * NB // 2 + RESP_ROWS, LANES), jnp.float32),
            pltpu.SemaphoreType.DMA((NB // 2 + 1,)),
            pltpu.SemaphoreType.DMA(()),
        ],
        compiler_params=pltpu.CompilerParams(vmem_limit_bytes=VMEM_LIMIT),
        cost_estimate=pl.CostEstimate(
            flops=5_000_000_000, bytes_accessed=8_000_000, transcendentals=0
        ),
        name="gram_parts",
    )(snapshots, aux)


def pair_square(even, odd):
    left = lax.broadcasted_iota(jnp.int32, (NB // 2, LANES), 1) < LANES // 2
    top = jnp.where(left, even, pltpu.roll(odd, LANES // 2, 1))
    bottom = jnp.where(left, pltpu.roll(even, LANES // 2, 1), odd)
    return jnp.concatenate([top, bottom], axis=0)


def hermitian(squares):
    row = lax.broadcasted_iota(jnp.int32, (NB, LANES), 0)
    col = lax.broadcasted_iota(jnp.int32, (NB, LANES), 1) % NB
    zero = jnp.zeros((NB, LANES), jnp.float32)
    full = squares + [zero] * (PACK - len(squares))
    turned = flip_groups([zero] * PACK, jnp.concatenate(full, axis=0))
    for square, flipped in zip(squares, turned):
        real = jnp.where(row <= col, square, flipped)
        imag = jnp.where(row > col, square, jnp.where(row < col, -flipped, 0.0))
        yield real, imag


def small_call(kernel, name, out_shape, scratch_shapes=(), limit=SMALL_LIMIT):
    def call(*args):
        return pl.pallas_call(
            kernel,
            out_shape=out_shape,
            in_specs=[VMEM] * len(args),
            out_specs=VMEM if isinstance(out_shape, jax.ShapeDtypeStruct) else (VMEM,) * len(out_shape),
            scratch_shapes=list(scratch_shapes),
            compiler_params=pltpu.CompilerParams(vmem_limit_bytes=limit),
            name=name,
        )(*args)

    return call


def floats(*shape):
    return jax.ShapeDtypeStruct(shape, jnp.float32)


def add_core_kernel(kept_ref, got_ref, out_ref):
    quarter = out_ref.shape[1] - RESP_ROWS
    tail = pl.ds(4 * quarter, RESP_ROWS)
    resp = kept_ref[tail, :] + got_ref[tail, :]
    for m in range(4):
        rows = pl.ds(m * quarter, quarter)
        out_ref[m, pl.ds(0, quarter), :] = kept_ref[rows, :] + got_ref[rows, :]
        out_ref[m, pl.ds(quarter, RESP_ROWS), :] = resp


def add_core(kept, got):
    quarter = (kept.shape[0] - RESP_ROWS) // 4
    return small_call(add_core_kernel, "add_core", floats(4, quarter + RESP_ROWS, LANES))(kept, got)


def add_near_kernel(parts_ref, out_ref):
    out_ref[...] = (parts_ref[0] + parts_ref[1]) + (parts_ref[2] + parts_ref[3])


def add_kernel(kept_ref, got_ref, out_ref):
    out_ref[...] = kept_ref[...] + got_ref[...]


def add(name, kept, got):
    return small_call(add_kernel, name, floats(*kept.shape))(kept, got)


def finish_kernel(kept_ref, got_ref, packed_ref, resp_ref):
    rows = packed_ref.shape[0]
    packed_ref[...] = kept_ref[pl.ds(0, rows), :] + got_ref[pl.ds(0, rows), :]
    tail = pl.ds(rows, RESP_ROWS)
    resp = kept_ref[tail, :] + got_ref[tail, :]
    real = resp[: RESP_ROWS // 2]
    imag = resp[RESP_ROWS // 2 :]
    power = real * real + imag * imag
    lane = lax.broadcasted_iota(jnp.int32, power.shape, 1)
    mean = jnp.zeros(power.shape, jnp.float32)
    for q in range(PACK):
        mine = lane // NB == q
        part = jnp.sum(jnp.where(mine, power, 0.0), axis=1, keepdims=True) / NB
        mean = jnp.where(mine, part, mean)
    scaling = 1.0 / jnp.sqrt(mean + 1e-06)
    resp_ref[pl.ds(0, RESP_ROWS // 2), :] = real * scaling
    resp_ref[pl.ds(RESP_ROWS // 2, RESP_ROWS // 2), :] = imag * scaling


def finish(kept, got):
    rows = kept.shape[0] - RESP_ROWS
    return small_call(finish_kernel, "finish", (floats(rows, LANES), floats(RESP_ROWS, LANES)))(
        kept, got
    )


def join_y_kernel(own_ref, got_ref, packed_ref):
    rows = own_ref.shape[0]
    for m, ref in enumerate((own_ref, got_ref)):
        packed_ref[pl.ds((y_bit() ^ m) * rows, rows), :] = ref[...]


def unpack_kernel(*refs):
    parts, out_ref = refs[:-1], refs[-1]
    half = NB // 2
    for m, part in enumerate(parts):
        count = part.shape[0] // half
        place = (core_bit() ^ m) * 2 * count if len(parts) > 1 else 0
        for first in range(0, count, 2 * PACK):
            last = min(first + 2 * PACK, count)
            pairs = [part[pl.ds(i * half, half), :] for i in range(first, last)]
            squares = [pair_square(*pairs[i : i + 2]) for i in range(0, len(pairs), 2)]
            for g, both in enumerate(hermitian(squares)):
                for q in range(PACK):
                    freq = place + 2 * first + PACK * g + q
                    for c in range(2):
                        out_ref[freq, c] = both[c][:, q * NB : (q + 1) * NB]


def unpack_gram(*parts):
    count = sum(part.shape[0] for part in parts) * 4 // NB
    return small_call(unpack_kernel, "unpack_gram", floats(count, 2, NB, NB))(*parts)


def modes_kernel(
    total_rows, high_ref, low_hbm, rest_ref, w_ref, table_ref, resp_ref, out_ref, low_ref, a_ref, sems
):
    padded, cols = high_ref.shape
    pieces = sems.shape[0]
    fetches = []
    for i in range(pieces):
        first = padded // LANES * i // pieces * LANES
        last = padded // LANES * (i + 1) // pieces * LANES
        rows = pl.ds(first, last - first)
        fetches.append(pltpu.make_async_copy(low_hbm.at[rows], low_ref.at[rows], sems.at[i]))
    for fetch in fetches:
        fetch.start()
    row = lax.broadcasted_iota(jnp.int32, (RESP_ROWS, 1), 0)
    leaks = window_leaks()
    corrections = []
    groups = RESP_ROWS // 2
    lane = lax.broadcasted_iota(jnp.int32, (RESP_ROWS, LANES), 1)
    left = lane < HALF
    for q in range(PACK):
        resp = resp_ref[...]
        if q:
            resp = pltpu.roll(resp, LANES - q * NB, 1)
        if q < len(leaks):
            total = jnp.sum(jnp.where(lane < NB, resp, 0.0), axis=1, keepdims=True) * leaks[q]
            corrections.append(jnp.where(row % groups == 0, total, 0.0) * rest_ref[pl.ds(0, 1), :])
        else:
            corrections.append(jnp.zeros((RESP_ROWS, cols), jnp.float32))
        real = jnp.concatenate([resp[:groups]] * 2, axis=0)
        imag = jnp.concatenate([resp[groups:]] * 2, axis=0)
        rows = pl.ds(q * RESP_ROWS, RESP_ROWS)
        first = table_ref[0, rows, :]
        second = table_ref[1, rows, :]
        first_turned = pltpu.roll(first, HALF, 1)
        second_turned = pltpu.roll(second, HALF, 1)

        def spread(value, block):
            if 0 <= block < NB:
                return jnp.broadcast_to(value[:, block : block + 1], (RESP_ROWS, LANES))
            return jnp.zeros((RESP_ROWS, LANES), jnp.float32)

        for m in range(padded // LANES):
            value = first_turned * jnp.where(left, spread(real, 2 * m - 1), spread(real, 2 * m + 1))
            value += second_turned * jnp.where(
                left, spread(imag, 2 * m - 1), spread(imag, 2 * m + 1)
            )
            if 2 * m < NB:
                value += first * spread(real, 2 * m) + second * spread(imag, 2 * m)
            high, low = split(value)
            own = pl.ds(m * LANES, LANES)
            a_ref[rows, own] = high
            a_ref[pl.ds(2 * NF + q * RESP_ROWS, RESP_ROWS), own] = low
    both = jnp.dot(a_ref[...], high_ref[...], preferred_element_type=jnp.float32)
    modes = both[: 2 * NF] + both[2 * NF :]
    modes -= jnp.concatenate(corrections, axis=0)
    for fetch in fetches:
        fetch.wait()
    modes += jnp.dot(
        a_ref[pl.ds(0, 2 * NF), :], low_ref[...], preferred_element_type=jnp.float32
    )
    modes = modes * jnp.sqrt(2.0 * total_rows / load_weights(w_ref, cols // LANES))
    n_freq = out_ref.shape[0]
    mine = groups // n_freq
    group = lax.axis_index("freq")
    for q in range(PACK):
        for part in range(2):
            for f in range(n_freq):
                first = q * RESP_ROWS + part * groups + f * mine
                slot = f ^ group if n_freq == 2 else f
                for c in range(cols // LANES):
                    out_ref[slot, 2 * c + part, pl.ds(q, mine, stride=PACK), :] = modes[
                        first : first + mine, c * LANES : (c + 1) * LANES
                    ]


def local_modes(high, low, rest, weight_rows, response, total_rows, n_freq):
    padded, cols = high.shape
    return pl.pallas_call(
        functools.partial(modes_kernel, total_rows),
        out_shape=floats(n_freq, 2 * cols // LANES, NF // n_freq, LANES),
        in_specs=[VMEM, pl.BlockSpec(memory_space=pl.ANY)] + [VMEM] * 4,
        out_specs=VMEM,
        scratch_shapes=[
            pltpu.VMEM((padded, cols), jnp.bfloat16),
            pltpu.VMEM((4 * NF, padded), jnp.bfloat16),
            pltpu.SemaphoreType.DMA((4,)),
        ],
        compiler_params=pltpu.CompilerParams(vmem_limit_bytes=VMEM_LIMIT),
        cost_estimate=pl.CostEstimate(
            flops=3_000_000_000, bytes_accessed=8_000_000, transcendentals=0
        ),
        name="local_modes",
    )(high, low, rest, weight_rows, jnp.asarray(mode_tables()), response)


def join_kernel(kept_ref, got_ref, out_ref):
    tiles = got_ref.shape[0] // 2
    group = lax.axis_index("freq")
    for slot, ref in enumerate((kept_ref.at[0], got_ref)):
        for c in range(tiles):
            lanes = pl.ds(pl.multiple_of(((group ^ slot) * tiles + c) * LANES, LANES), LANES)
            for part in range(2):
                out_ref[:, part, lanes] = ref[2 * c + part]


def join_modes(kept, got):
    tiles, count, _ = got.shape
    return small_call(join_kernel, "join_modes", floats(count, 2, tiles * LANES))(kept, got)


def response_of(gram, start_vec):
    matvec = functools.partial(jnp.einsum, "fjk,fk->fj", precision=lax.Precision.HIGHEST)
    resp_real = matvec(gram[:, 0], start_vec[:, 0]) - matvec(gram[:, 1], start_vec[:, 1])
    resp_imag = matvec(gram[:, 0], start_vec[:, 1]) + matvec(gram[:, 1], start_vec[:, 0])
    scaling = 1.0 / jnp.sqrt(
        jnp.mean(resp_real * resp_real + resp_imag * resp_imag, axis=1, keepdims=True) + 1e-06
    )
    return jnp.stack([resp_real * scaling, resp_imag * scaling], axis=1)


def direction_shards(n_devices, snapshots, weight, start_vec):
    def swap(value, mask):
        return lax.ppermute(value, ("pts", "freq"), [(i, i ^ mask) for i in range(n_devices)])

    x, core, y, z_near, z_far = 1, 2, 4, 8, 16
    near = [
        [first + far, first + far + x, first + far + y, first + far + y + x]
        for far in range(0, n_devices, z_near)
        for first in (0, core)
    ]
    total_rows = float(weight.shape[0] * 16)
    weight_rows = weight.reshape(-1, LANES)
    places = [
        (i // 8 % 2) * 16 + (i // 4 % 2) * 8 + (i // 16) * 4 + i % 4 for i in range(NF // 2)
    ]
    keep, send, high, rest, low = gram_parts(
        snapshots, weight_rows, start_vec, total_rows, places, True
    )
    parts = add_core(keep, swap(send, core))
    parts = lax.all_to_all(
        parts, ("pts", "freq"), 0, 0, axis_index_groups=near, tiled=True
    )
    part = small_call(add_near_kernel, "add_near", floats(*parts.shape[1:]))(parts)
    part = add("add_z", part, swap(part, z_near))
    packed, response = finish(part, swap(part, z_far))
    other = swap(packed, y)
    modes = local_modes(high, low, rest, weight_rows, response, total_rows, 2)
    packed = small_call(join_y_kernel, "join_y", floats(2 * packed.shape[0], LANES))(packed, other)
    gram_mine = unpack_gram(packed, swap(packed, core))
    return gram_mine, join_modes(modes, swap(modes[1], x))


def shards(n_pts, n_freq, snapshots, weight, start_vec):
    cols = snapshots.shape[1]
    total_rows = float(weight.shape[0] * n_pts)
    n_devices = n_pts * n_freq
    mine_count = NF // n_freq
    group = lax.axis_index("freq")
    weight_rows = weight.reshape(-1, LANES)
    places = list(range(NF // 2))
    first, second, high, rest, low = gram_parts(
        snapshots, weight_rows, start_vec, total_rows, places, False
    )
    parts = jnp.concatenate([first[:-RESP_ROWS], second[:-RESP_ROWS]], axis=0)
    share = parts.reshape(n_devices, -1)
    share = jnp.sum(lax.all_to_all(share, ("freq", "pts"), 0, 0, tiled=True), axis=0)
    packed = lax.all_gather(share, "pts", axis=0, tiled=True)
    gram_mine = unpack_gram(packed.reshape(-1, LANES))
    start_mine = lax.dynamic_slice_in_dim(start_vec, group * mine_count, mine_count, 0)
    response = lax.all_gather(response_of(gram_mine, start_mine), "freq", axis=0, tiled=True)
    response = jnp.transpose(response.reshape(NF // PACK, PACK, 2, NB), (2, 0, 1, 3))
    response = response.reshape(RESP_ROWS, LANES)
    modes = local_modes(high, low, rest, weight_rows, response, total_rows, n_freq)
    modes = lax.all_to_all(modes, "freq", 0, 0, tiled=True)
    modes = modes.reshape(n_freq, cols // LANES, 2, mine_count, LANES)
    modes = jnp.transpose(modes, (3, 2, 0, 1, 4)).reshape(mine_count, 2, n_freq * cols)
    return gram_mine, modes


def solution(mesh):
    n_pts, n_freq = mesh.shape["pts"], mesh.shape["freq"]
    if (n_pts, n_freq) == (16, 2):
        body = functools.partial(direction_shards, n_pts * n_freq)
    else:
        body = functools.partial(shards, n_pts, n_freq)
    placed = (P(None, ("pts", "freq")), P("pts"), P())
    return jax.shard_map(
        body,
        mesh=mesh,
        in_specs=placed,
        out_specs=(P("freq", None, None, None), P("freq", None, "pts")),
        check_vma=False,
    )
```

```python
import functools
import math

import jax
import jax.numpy as jnp
import numpy as np
from jax import lax
from jax.experimental import pallas as pl
from jax.experimental.pallas import tpu as pltpu
from jax.sharding import PartitionSpec as P

NFFT = 128
HALF = NFFT // 2
NF = 64
NB = 32
LANES = 128
PACK = 4
VMEM_LIMIT = 51 * 1024 * 1024
SMALL_LIMIT = 8 * 1024 * 1024
VMEM = pl.BlockSpec(memory_space=pltpu.VMEM)


def dft_values():
    times = np.arange(NFFT)
    freqs = np.arange(NF)
    phases = (freqs[:, None] * times[None, :] % NFFT) * (2.0 * math.pi / NFFT)
    window = 0.5 - 0.5 * np.cos(times * (2.0 * math.pi / NFFT))
    weighted = window / np.sqrt(np.sum(window * window))
    return np.cos(phases) * weighted, -np.sin(phases) * weighted


def split_table(table):
    high = table.astype(jnp.bfloat16)
    low = (table - high.astype(np.float64)).astype(jnp.bfloat16)
    return high, low


def mode_tables():
    real, imag = dft_values()
    order = np.arange(NF).reshape(NF // PACK, PACK).T
    real, imag = real[order], imag[order]
    first = np.stack([real, imag], axis=1).reshape(2 * NF, NFFT)
    second = np.stack([-imag, real], axis=1).reshape(2 * NF, NFFT)
    return np.stack([first, second]).astype(np.float32)


def cosine_of_turns(count):
    folded = jnp.minimum(count, NFFT - count)
    angle = (NFFT // 4 - folded).astype(jnp.float32) * (2.0 * math.pi / NFFT)
    square = angle * angle
    series = 1.0
    for n in (10, 8, 6, 4, 2):
        series = 1.0 - square * series * (1.0 / (n * (n + 1)))
    return angle * series


def fill_dft(dft_ref):
    row = lax.broadcasted_iota(jnp.int32, (2 * NF, NFFT), 0)
    time = lax.broadcasted_iota(jnp.int32, (2 * NF, NFFT), 1)
    quarter = jnp.where(row < NF, 0, NFFT // 4)
    wave = cosine_of_turns((row % NF * time + quarter) % NFFT)
    window = 0.5 - 0.5 * np.cos(np.arange(NFFT) * (2.0 * math.pi / NFFT))
    norm = float(np.sqrt(np.sum(window * window)))
    high, low = split(wave * ((0.5 - 0.5 * cosine_of_turns(time)) / norm))
    dft_ref[pl.ds(0, 2 * NF), pl.ds(0, NFFT)] = high
    dft_ref[pl.ds(0, 2 * NF), pl.ds(NFFT, NFFT)] = high
    dft_ref[pl.ds(2 * NF, 2 * NF), pl.ds(0, NFFT)] = low
    dft_ref[pl.ds(2 * NF, 2 * NF), pl.ds(NFFT, NFFT)] = jnp.zeros((2 * NF, NFFT), jnp.bfloat16)


def spread_start(start_ref, spread_ref):
    row = lax.broadcasted_iota(jnp.int32, (NF, LANES), 0)
    lane = lax.broadcasted_iota(jnp.int32, (NF, LANES), 1)
    start = start_ref[pl.ds(0, 2 * NB), pl.ds(0, NF)]
    for g in range(NF // PACK):
        pick = (row == PACK * g + lane // NB).astype(jnp.float32)
        spread_ref[g] = jnp.dot(
            start,
            pick,
            precision=lax.Precision.HIGHEST,
            preferred_element_type=jnp.float32,
        )


def split(value):
    high = value.astype(jnp.bfloat16)
    low = (value - high.astype(jnp.float32)).astype(jnp.bfloat16)
    return high, low


def load_weights(w_ref, col_tiles):
    first = lax.axis_index("freq") * col_tiles
    return jnp.concatenate([w_ref[pl.ds(first + c, 1), :] for c in range(col_tiles)], axis=1)


def flip_groups(groups, flipped):
    turned = flipped.T
    lane = lax.broadcasted_iota(jnp.int32, (NB, LANES), 1)
    out = []
    for g in range(PACK):
        total = groups[g]
        for q in range(PACK):
            block = turned[q * NB : (q + 1) * NB]
            if q != g:
                block = pltpu.roll(block, ((q - g) % PACK) * NB, 1)
            total = total + jnp.where(lane // NB == q, block, 0.0)
        out.append(total)
    return out


TILE = 8


def turn_tiles(tiles):
    row = lax.broadcasted_iota(jnp.int32, (TILE, LANES), 0)
    step = TILE // 2
    while step:
        keep = row % (2 * step) < step
        turned = list(tiles)
        for i in range(TILE):
            if i % (2 * step) < step:
                low, high = tiles[i], tiles[i + step]
                turned[i] = jnp.where(keep, low, pltpu.roll(high, step, 0))
                turned[i + step] = jnp.where(keep, pltpu.roll(low, TILE - step, 0), high)
        tiles = turned
        step //= 2
    return tiles


def core_bit():
    return lax.rem(lax.axis_index("pts"), 2)


def y_bit():
    return lax.rem(lax.div(lax.axis_index("pts"), 2), 2)


RESP_ROWS = 2 * NF // PACK


def give_half(value_ref, bit, keep_ref, send_ref):
    half = keep_ref.shape[0] - RESP_ROWS
    keep_ref[pl.ds(0, half), :] = value_ref[pl.ds(bit * half, half), :]
    send_ref[pl.ds(0, half), :] = value_ref[pl.ds((1 - bit) * half, half), :]
    resp = value_ref[pl.ds(2 * half, RESP_ROWS), :]
    keep_ref[pl.ds(half, RESP_ROWS), :] = resp
    send_ref[pl.ds(half, RESP_ROWS), :] = resp


def gram_kernel(
    total_rows,
    places,
    by_core,
    x_hbm,
    aux_ref,
    keep_ref,
    send_ref,
    high_ref,
    low_hbm,
    x_ref,
    dft_ref,
    low_ref,
    block_even,
    block_odd,
    spec_ref,
    z_even,
    z_odd,
    real_ref,
    imag_ref,
    spread_ref,
    pack_ref,
    in_sems,
    out_sem,
):
    times, cols = x_ref.shape
    halves = times // HALF
    col_tiles = cols // LANES
    block_refs = (block_even, block_odd)
    pieces = in_sems.shape[0]
    piece = times // pieces

    def fetch(i):
        rows = pl.ds(i * piece, piece)
        return pltpu.make_async_copy(x_hbm.at[rows], x_ref.at[rows], in_sems.at[i])

    for i in range(pieces):
        fetch(i).start()
    fill_dft(dft_ref)
    spread_start(aux_ref, spread_ref)

    acc = jnp.zeros((HALF, cols), jnp.float32)
    for i in range(pieces):
        fetch(i).wait()
        for h in range(piece // HALF):
            acc = acc + x_ref[pl.ds(i * piece + h * HALF, HALF), :]
    mean = jnp.sum(acc, axis=0, keepdims=True) / times
    weights = load_weights(aux_ref.at[pl.ds(2 * NB, aux_ref.shape[0] - 2 * NB)], col_tiles)
    scale = jnp.sqrt(weights / (2.0 * total_rows))

    def center(i, carry):
        rows = pl.ds(pl.multiple_of(i * HALF, HALF), HALF)
        high, low = split((x_ref[rows, :] - mean) * scale)
        high_ref[rows, :] = high
        low_ref[rows, :] = low
        return carry

    lax.fori_loop(0, halves, center, 0, unroll=3)
    pad = high_ref.shape[0] - times
    if pad:
        high_ref[pl.ds(times, pad), :] = jnp.zeros((pad, cols), jnp.bfloat16)
        low_ref[pl.ds(times, pad), :] = jnp.zeros((pad, cols), jnp.bfloat16)
    save_low = pltpu.make_async_copy(low_ref, low_hbm, out_sem)
    save_low.start()

    def transform(first):
        for i in range(TILE // 2):
            blocks = []
            for s in range(2):
                rows = pl.ds((first + 2 * i + s) * HALF, NFFT)
                blocks.append(jnp.concatenate([high_ref[rows, :], low_ref[rows, :]], axis=0))
            both = jnp.dot(
                dft_ref[...], jnp.concatenate(blocks, axis=1), preferred_element_type=jnp.float32
            )
            spectrum = both[: 2 * NF] + both[2 * NF :]
            for s in range(2):
                block_refs[first // TILE % 2][2 * i + s] = spectrum[:, s * cols : (s + 1) * cols]

    def arrange(first):
        block_ref = block_refs[first // TILE % 2]
        for c in range(col_tiles):
            lanes = pl.ds(c * LANES, LANES)
            for o in range(2 * NF // TILE):
                rows = pl.ds(o * TILE, TILE)
                tiles = turn_tiles([block_ref[b, rows, lanes] for b in range(TILE)])
                for k in range(TILE):
                    spec_ref[c, o * TILE + k, pl.ds(first, TILE), :] = tiles[k]

    transform(0)
    for first in range(0, NB, TILE):
        if first + TILE < NB:
            transform(first + TILE)
        arrange(first)

    row = lax.broadcasted_iota(jnp.int32, (NB, LANES), 0)
    lane = lax.broadcasted_iota(jnp.int32, (NB, LANES), 1)
    upper = row <= lane % NB
    octets = NF // 8

    def prepare(z_ref, octet, half):
        for part in range(2):
            for q in range(PACK):
                own = pl.ds(part * LANES + q * NB, NB)
                for c in range(col_tiles):
                    value = spec_ref[c, NF * part + TILE * octet + PACK * half + q]
                    high = value.astype(jnp.bfloat16)
                    low = (2.0 * (value - high.astype(jnp.float32))).astype(jnp.bfloat16)
                    z_ref[own, pl.ds(c * LANES, LANES)] = high
                    z_ref[own, pl.ds(cols + c * LANES, LANES)] = low

    def correlate(z_ref, group):
        high = z_ref[:, pl.ds(0, cols)]
        product = lax.dot_general(
            jnp.concatenate([high, high], axis=1),
            z_ref[...],
            (((1,), (1,)), ((), ())),
            preferred_element_type=jnp.float32,
        )
        gram_real = jnp.zeros((NB, LANES), jnp.float32)
        gram_imag = jnp.zeros((NB, LANES), jnp.float32)
        for q in range(PACK):
            mine = lane // NB == q
            real = product[q * NB : (q + 1) * NB]
            imag = product[LANES + q * NB : LANES + (q + 1) * NB]
            gram_real = jnp.where(mine, real[:, :LANES] + imag[:, LANES:], gram_real)
            gram_imag = jnp.where(mine, real[:, LANES:] - imag[:, :LANES], gram_imag)
        real_ref[group] = gram_real
        imag_ref[group] = gram_imag

    prepare(z_even, 0, 0)

    def step(o, carry):
        prepare(z_odd, o, 1)
        correlate(z_even, 2 * o)
        prepare(z_even, jnp.minimum(o + 1, octets - 1), 0)
        correlate(z_odd, 2 * o + 1)
        return carry

    lax.fori_loop(0, octets, step, 0)
    left = lane[: NB // 2] < LANES // 2
    half = NB // 2
    resp_real = []
    resp_imag = []
    for quad in range(NF // PACK // PACK):
        own = pl.ds(quad * PACK, PACK)
        reals = [real_ref[quad * PACK + g] for g in range(PACK)]
        imags = [imag_ref[quad * PACK + g] for g in range(PACK)]
        reals = flip_groups(reals, real_ref[own].reshape(PACK * NB, LANES))
        imags = flip_groups(imags, -imag_ref[own].reshape(PACK * NB, LANES))
        for g, (real, imag) in enumerate(zip(reals, imags)):
            group = quad * PACK + g
            start_real = spread_ref[group, pl.ds(0, NB), :]
            start_imag = spread_ref[group, pl.ds(NB, NB), :]
            resp_real.append(
                jnp.sum(real * start_real + imag * start_imag, axis=0, keepdims=True)
            )
            resp_imag.append(
                jnp.sum(real * start_imag - imag * start_real, axis=0, keepdims=True)
            )
            packed = jnp.where(upper, real, imag)
            top = packed[:half]
            bottom = packed[half:]
            even = jnp.where(left, top, pltpu.roll(bottom, LANES // 2, 1))
            odd = jnp.where(left, pltpu.roll(top, LANES // 2, 1), bottom)
            pack_ref[pl.ds(places[2 * group] * half, half), :] = even
            pack_ref[pl.ds(places[2 * group + 1] * half, half), :] = odd
    resp = jnp.concatenate(resp_real + resp_imag, axis=0)
    pack_ref[pl.ds(NF // 2 * half, RESP_ROWS), :] = resp
    give_half(pack_ref, core_bit() if by_core else 0, keep_ref, send_ref)
    save_low.wait()


def gram_parts(snapshots, weight_rows, start_vec, total_rows, places, by_core):
    times, cols = snapshots.shape
    start = jnp.transpose(start_vec, (1, 2, 0)).reshape(2 * NB, NF)
    start = jnp.pad(start, ((0, 0), (0, LANES - NF)))
    aux = jnp.concatenate([start, weight_rows], axis=0)
    pieces = 11
    any_space = pl.BlockSpec(memory_space=pl.ANY)
    saved = jax.ShapeDtypeStruct((-(-times // LANES) * LANES, cols), jnp.bfloat16)
    half = floats(NF // 4 * NB // 2 + RESP_ROWS, LANES)
    return pl.pallas_call(
        functools.partial(gram_kernel, total_rows, places, by_core),
        out_shape=(half, half, saved, saved),
        in_specs=[any_space, VMEM],
        out_specs=(VMEM, VMEM, VMEM, any_space),
        scratch_shapes=[
            pltpu.VMEM((times, cols), jnp.float32),
            pltpu.VMEM((4 * NF, 2 * NFFT), jnp.bfloat16),
            pltpu.VMEM(saved.shape, jnp.bfloat16),
            pltpu.VMEM((TILE, 2 * NF, cols), jnp.float32),
            pltpu.VMEM((TILE, 2 * NF, cols), jnp.float32),
            pltpu.VMEM((cols // LANES, 2 * NF, NB, LANES), jnp.float32),
            pltpu.VMEM((2 * LANES, 2 * cols), jnp.bfloat16),
            pltpu.VMEM((2 * LANES, 2 * cols), jnp.bfloat16),
            pltpu.VMEM((NF // PACK, NB, LANES), jnp.float32),
            pltpu.VMEM((NF // PACK, NB, LANES), jnp.float32),
            pltpu.VMEM((NF // PACK, 2 * NB, LANES), jnp.float32),
            pltpu.VMEM((NF // 2 * NB // 2 + RESP_ROWS, LANES), jnp.float32),
            pltpu.SemaphoreType.DMA((pieces,)),
            pltpu.SemaphoreType.DMA(()),
        ],
        compiler_params=pltpu.CompilerParams(vmem_limit_bytes=VMEM_LIMIT),
        cost_estimate=pl.CostEstimate(
            flops=5_000_000_000, bytes_accessed=8_000_000, transcendentals=0
        ),
        name="gram_parts",
    )(snapshots, aux)


def pair_square(even, odd):
    left = lax.broadcasted_iota(jnp.int32, (NB // 2, LANES), 1) < LANES // 2
    top = jnp.where(left, even, pltpu.roll(odd, LANES // 2, 1))
    bottom = jnp.where(left, pltpu.roll(even, LANES // 2, 1), odd)
    return jnp.concatenate([top, bottom], axis=0)


def hermitian(squares):
    row = lax.broadcasted_iota(jnp.int32, (NB, LANES), 0)
    col = lax.broadcasted_iota(jnp.int32, (NB, LANES), 1) % NB
    zero = jnp.zeros((NB, LANES), jnp.float32)
    full = squares + [zero] * (PACK - len(squares))
    turned = flip_groups([zero] * PACK, jnp.concatenate(full, axis=0))
    for square, flipped in zip(squares, turned):
        real = jnp.where(row <= col, square, flipped)
        imag = jnp.where(row > col, square, jnp.where(row < col, -flipped, 0.0))
        yield real, imag


def small_call(kernel, name, out_shape, scratch_shapes=(), limit=SMALL_LIMIT):
    def call(*args):
        return pl.pallas_call(
            kernel,
            out_shape=out_shape,
            in_specs=[VMEM] * len(args),
            out_specs=VMEM if isinstance(out_shape, jax.ShapeDtypeStruct) else (VMEM,) * len(out_shape),
            scratch_shapes=list(scratch_shapes),
            compiler_params=pltpu.CompilerParams(vmem_limit_bytes=limit),
            name=name,
        )(*args)

    return call


def floats(*shape):
    return jax.ShapeDtypeStruct(shape, jnp.float32)


def add_core_kernel(kept_ref, got_ref, out_ref):
    quarter = out_ref.shape[1] - RESP_ROWS
    tail = pl.ds(4 * quarter, RESP_ROWS)
    resp = kept_ref[tail, :] + got_ref[tail, :]
    for m in range(4):
        rows = pl.ds(m * quarter, quarter)
        out_ref[m, pl.ds(0, quarter), :] = kept_ref[rows, :] + got_ref[rows, :]
        out_ref[m, pl.ds(quarter, RESP_ROWS), :] = resp


def add_core(kept, got):
    quarter = (kept.shape[0] - RESP_ROWS) // 4
    return small_call(add_core_kernel, "add_core", floats(4, quarter + RESP_ROWS, LANES))(kept, got)


def add_near_kernel(parts_ref, out_ref):
    out_ref[...] = (parts_ref[0] + parts_ref[1]) + (parts_ref[2] + parts_ref[3])


def add_kernel(kept_ref, got_ref, out_ref):
    out_ref[...] = kept_ref[...] + got_ref[...]


def add(name, kept, got):
    return small_call(add_kernel, name, floats(*kept.shape))(kept, got)


def finish_kernel(kept_ref, got_ref, packed_ref, resp_ref):
    rows = packed_ref.shape[0]
    packed_ref[...] = kept_ref[pl.ds(0, rows), :] + got_ref[pl.ds(0, rows), :]
    tail = pl.ds(rows, RESP_ROWS)
    resp = kept_ref[tail, :] + got_ref[tail, :]
    real = resp[: RESP_ROWS // 2]
    imag = resp[RESP_ROWS // 2 :]
    power = real * real + imag * imag
    lane = lax.broadcasted_iota(jnp.int32, power.shape, 1)
    mean = jnp.zeros(power.shape, jnp.float32)
    for q in range(PACK):
        mine = lane // NB == q
        part = jnp.sum(jnp.where(mine, power, 0.0), axis=1, keepdims=True) / NB
        mean = jnp.where(mine, part, mean)
    scaling = 1.0 / jnp.sqrt(mean + 1e-06)
    resp_ref[pl.ds(0, RESP_ROWS // 2), :] = real * scaling
    resp_ref[pl.ds(RESP_ROWS // 2, RESP_ROWS // 2), :] = imag * scaling


def finish(kept, got):
    rows = kept.shape[0] - RESP_ROWS
    return small_call(finish_kernel, "finish", (floats(rows, LANES), floats(RESP_ROWS, LANES)))(
        kept, got
    )


def join_y_kernel(own_ref, got_ref, packed_ref):
    rows = own_ref.shape[0]
    for m, ref in enumerate((own_ref, got_ref)):
        packed_ref[pl.ds((y_bit() ^ m) * rows, rows), :] = ref[...]


def unpack_kernel(*refs):
    parts, out_ref = refs[:-1], refs[-1]
    half = NB // 2
    for m, part in enumerate(parts):
        count = part.shape[0] // half
        place = (core_bit() ^ m) * 2 * count if len(parts) > 1 else 0
        for first in range(0, count, 2 * PACK):
            last = min(first + 2 * PACK, count)
            pairs = [part[pl.ds(i * half, half), :] for i in range(first, last)]
            squares = [pair_square(*pairs[i : i + 2]) for i in range(0, len(pairs), 2)]
            for g, both in enumerate(hermitian(squares)):
                for q in range(PACK):
                    freq = place + 2 * first + PACK * g + q
                    for c in range(2):
                        out_ref[freq, c] = both[c][:, q * NB : (q + 1) * NB]


def unpack_gram(*parts):
    count = sum(part.shape[0] for part in parts) * 4 // NB
    return small_call(unpack_kernel, "unpack_gram", floats(count, 2, NB, NB))(*parts)


def modes_kernel(
    total_rows, high_ref, low_hbm, w_ref, table_ref, resp_ref, out_ref, low_ref, a_ref, sems
):
    padded, cols = high_ref.shape
    pieces = sems.shape[0]
    fetches = []
    for i in range(pieces):
        first = padded // LANES * i // pieces * LANES
        last = padded // LANES * (i + 1) // pieces * LANES
        rows = pl.ds(first, last - first)
        fetches.append(pltpu.make_async_copy(low_hbm.at[rows], low_ref.at[rows], sems.at[i]))
    for fetch in fetches:
        fetch.start()
    groups = RESP_ROWS // 2
    lane = lax.broadcasted_iota(jnp.int32, (RESP_ROWS, LANES), 1)
    left = lane < HALF
    for q in range(PACK):
        resp = resp_ref[...]
        if q:
            resp = pltpu.roll(resp, LANES - q * NB, 1)
        real = jnp.concatenate([resp[:groups]] * 2, axis=0)
        imag = jnp.concatenate([resp[groups:]] * 2, axis=0)
        rows = pl.ds(q * RESP_ROWS, RESP_ROWS)
        first = table_ref[0, rows, :]
        second = table_ref[1, rows, :]
        first_turned = pltpu.roll(first, HALF, 1)
        second_turned = pltpu.roll(second, HALF, 1)

        def spread(value, block):
            if 0 <= block < NB:
                return jnp.broadcast_to(value[:, block : block + 1], (RESP_ROWS, LANES))
            return jnp.zeros((RESP_ROWS, LANES), jnp.float32)

        for m in range(padded // LANES):
            value = first_turned * jnp.where(left, spread(real, 2 * m - 1), spread(real, 2 * m + 1))
            value += second_turned * jnp.where(
                left, spread(imag, 2 * m - 1), spread(imag, 2 * m + 1)
            )
            if 2 * m < NB:
                value += first * spread(real, 2 * m) + second * spread(imag, 2 * m)
            high, low = split(value)
            own = pl.ds(m * LANES, LANES)
            a_ref[rows, own] = high
            a_ref[pl.ds(2 * NF + q * RESP_ROWS, RESP_ROWS), own] = low
    both = jnp.dot(a_ref[...], high_ref[...], preferred_element_type=jnp.float32)
    modes = both[: 2 * NF] + both[2 * NF :]
    for fetch in fetches:
        fetch.wait()
    modes += jnp.dot(
        a_ref[pl.ds(0, 2 * NF), :], low_ref[...], preferred_element_type=jnp.float32
    )
    modes = modes * jnp.sqrt(2.0 * total_rows / load_weights(w_ref, cols // LANES))
    n_freq = out_ref.shape[0]
    mine = groups // n_freq
    group = lax.axis_index("freq")
    for q in range(PACK):
        for part in range(2):
            for f in range(n_freq):
                first = q * RESP_ROWS + part * groups + f * mine
                slot = f ^ group if n_freq == 2 else f
                for c in range(cols // LANES):
                    out_ref[slot, 2 * c + part, pl.ds(q, mine, stride=PACK), :] = modes[
                        first : first + mine, c * LANES : (c + 1) * LANES
                    ]


def local_modes(high, low, weight_rows, response, total_rows, n_freq):
    padded, cols = high.shape
    return pl.pallas_call(
        functools.partial(modes_kernel, total_rows),
        out_shape=floats(n_freq, 2 * cols // LANES, NF // n_freq, LANES),
        in_specs=[VMEM, pl.BlockSpec(memory_space=pl.ANY)] + [VMEM] * 3,
        out_specs=VMEM,
        scratch_shapes=[
            pltpu.VMEM((padded, cols), jnp.bfloat16),
            pltpu.VMEM((4 * NF, padded), jnp.bfloat16),
            pltpu.SemaphoreType.DMA((4,)),
        ],
        compiler_params=pltpu.CompilerParams(vmem_limit_bytes=VMEM_LIMIT),
        cost_estimate=pl.CostEstimate(
            flops=3_000_000_000, bytes_accessed=8_000_000, transcendentals=0
        ),
        name="local_modes",
    )(high, low, weight_rows, jnp.asarray(mode_tables()), response)


def join_kernel(kept_ref, got_ref, out_ref):
    tiles = got_ref.shape[0] // 2
    group = lax.axis_index("freq")
    for slot, ref in enumerate((kept_ref.at[0], got_ref)):
        for c in range(tiles):
            lanes = pl.ds(pl.multiple_of(((group ^ slot) * tiles + c) * LANES, LANES), LANES)
            for part in range(2):
                out_ref[:, part, lanes] = ref[2 * c + part]


def join_modes(kept, got):
    tiles, count, _ = got.shape
    return small_call(join_kernel, "join_modes", floats(count, 2, tiles * LANES))(kept, got)


def response_of(gram, start_vec):
    matvec = functools.partial(jnp.einsum, "fjk,fk->fj", precision=lax.Precision.HIGHEST)
    resp_real = matvec(gram[:, 0], start_vec[:, 0]) - matvec(gram[:, 1], start_vec[:, 1])
    resp_imag = matvec(gram[:, 0], start_vec[:, 1]) + matvec(gram[:, 1], start_vec[:, 0])
    scaling = 1.0 / jnp.sqrt(
        jnp.mean(resp_real * resp_real + resp_imag * resp_imag, axis=1, keepdims=True) + 1e-06
    )
    return jnp.stack([resp_real * scaling, resp_imag * scaling], axis=1)


def direction_shards(n_devices, snapshots, weight, start_vec):
    def swap(value, mask):
        return lax.ppermute(value, ("pts", "freq"), [(i, i ^ mask) for i in range(n_devices)])

    x, core, y, z_near, z_far = 1, 2, 4, 8, 16
    near = [
        [first + far, first + far + x, first + far + y, first + far + y + x]
        for far in range(0, n_devices, z_near)
        for first in (0, core)
    ]
    total_rows = float(weight.shape[0] * 16)
    weight_rows = weight.reshape(-1, LANES)
    places = [
        (i // 8 % 2) * 16 + (i // 4 % 2) * 8 + (i // 16) * 4 + i % 4 for i in range(NF // 2)
    ]
    keep, send, high, low = gram_parts(
        snapshots, weight_rows, start_vec, total_rows, places, True
    )
    parts = add_core(keep, swap(send, core))
    parts = lax.all_to_all(
        parts, ("pts", "freq"), 0, 0, axis_index_groups=near, tiled=True
    )
    part = small_call(add_near_kernel, "add_near", floats(*parts.shape[1:]))(parts)
    part = add("add_z", part, swap(part, z_near))
    packed, response = finish(part, swap(part, z_far))
    other = swap(packed, y)
    modes = local_modes(high, low, weight_rows, response, total_rows, 2)
    packed = small_call(join_y_kernel, "join_y", floats(2 * packed.shape[0], LANES))(packed, other)
    gram_mine = unpack_gram(packed, swap(packed, core))
    return gram_mine, join_modes(modes, swap(modes[1], x))


def shards(n_pts, n_freq, snapshots, weight, start_vec):
    cols = snapshots.shape[1]
    total_rows = float(weight.shape[0] * n_pts)
    n_devices = n_pts * n_freq
    mine_count = NF // n_freq
    group = lax.axis_index("freq")
    weight_rows = weight.reshape(-1, LANES)
    places = list(range(NF // 2))
    first, second, high, low = gram_parts(
        snapshots, weight_rows, start_vec, total_rows, places, False
    )
    parts = jnp.concatenate([first[:-RESP_ROWS], second[:-RESP_ROWS]], axis=0)
    share = parts.reshape(n_devices, -1)
    share = jnp.sum(lax.all_to_all(share, ("freq", "pts"), 0, 0, tiled=True), axis=0)
    packed = lax.all_gather(share, "pts", axis=0, tiled=True)
    gram_mine = unpack_gram(packed.reshape(-1, LANES))
    start_mine = lax.dynamic_slice_in_dim(start_vec, group * mine_count, mine_count, 0)
    response = lax.all_gather(response_of(gram_mine, start_mine), "freq", axis=0, tiled=True)
    response = jnp.transpose(response.reshape(NF // PACK, PACK, 2, NB), (2, 0, 1, 3))
    response = response.reshape(RESP_ROWS, LANES)
    modes = local_modes(high, low, weight_rows, response, total_rows, n_freq)
    modes = lax.all_to_all(modes, "freq", 0, 0, tiled=True)
    modes = modes.reshape(n_freq, cols // LANES, 2, mine_count, LANES)
    modes = jnp.transpose(modes, (3, 2, 0, 1, 4)).reshape(mine_count, 2, n_freq * cols)
    return gram_mine, modes


def solution(mesh):
    n_pts, n_freq = mesh.shape["pts"], mesh.shape["freq"]
    if (n_pts, n_freq) == (16, 2):
        body = functools.partial(direction_shards, n_pts * n_freq)
    else:
        body = functools.partial(shards, n_pts, n_freq)
    placed = (P(None, ("pts", "freq")), P("pts"), P())
    return jax.shard_map(
        body,
        mesh=mesh,
        in_specs=placed,
        out_specs=(P("freq", None, None, None), P("freq", None, "pts")),
        check_vma=False,
    )
```

```python
import functools
import math

import jax
import jax.numpy as jnp
import numpy as np
from jax import lax
from jax.experimental import pallas as pl
from jax.experimental.pallas import tpu as pltpu
from jax.sharding import PartitionSpec as P

NFFT = 128
HALF = NFFT // 2
NF = 64
NB = 32
LANES = 128
PACK = 4
VMEM_LIMIT = 51 * 1024 * 1024
SMALL_LIMIT = 8 * 1024 * 1024
VMEM = pl.BlockSpec(memory_space=pltpu.VMEM)


def dft_values():
    times = np.arange(NFFT)
    freqs = np.arange(NF)
    phases = (freqs[:, None] * times[None, :] % NFFT) * (2.0 * math.pi / NFFT)
    window = 0.5 - 0.5 * np.cos(times * (2.0 * math.pi / NFFT))
    weighted = window / np.sqrt(np.sum(window * window))
    return np.cos(phases) * weighted, -np.sin(phases) * weighted


def split_table(table):
    high = table.astype(jnp.bfloat16)
    low = (table - high.astype(np.float64)).astype(jnp.bfloat16)
    return high, low


def window_leaks():
    real, _ = dft_values()
    return [float(np.sum(real[k])) for k in range(2)]


def mode_tables():
    real, imag = dft_values()
    order = np.arange(NF).reshape(NF // PACK, PACK).T
    real, imag = real[order], imag[order]
    first = np.stack([real, imag], axis=1).reshape(2 * NF, NFFT)
    second = np.stack([-imag, real], axis=1).reshape(2 * NF, NFFT)
    return np.stack([first, second]).astype(np.float32)


def cosine_of_turns(count):
    folded = jnp.minimum(count, NFFT - count)
    angle = (NFFT // 4 - folded).astype(jnp.float32) * (2.0 * math.pi / NFFT)
    square = angle * angle
    series = 1.0
    for n in (10, 8, 6, 4, 2):
        series = 1.0 - square * series * (1.0 / (n * (n + 1)))
    return angle * series


def fill_dft(dft_ref):
    row = lax.broadcasted_iota(jnp.int32, (2 * NF, NFFT), 0)
    time = lax.broadcasted_iota(jnp.int32, (2 * NF, NFFT), 1)
    quarter = jnp.where(row < NF, 0, NFFT // 4)
    wave = cosine_of_turns((row % NF * time + quarter) % NFFT)
    window = 0.5 - 0.5 * np.cos(np.arange(NFFT) * (2.0 * math.pi / NFFT))
    norm = float(np.sqrt(np.sum(window * window)))
    high, low = split(wave * ((0.5 - 0.5 * cosine_of_turns(time)) / norm))
    dft_ref[pl.ds(0, 2 * NF), pl.ds(0, NFFT)] = high
    dft_ref[pl.ds(0, 2 * NF), pl.ds(NFFT, NFFT)] = high
    dft_ref[pl.ds(2 * NF, 2 * NF), pl.ds(0, NFFT)] = low
    dft_ref[pl.ds(2 * NF, 2 * NF), pl.ds(NFFT, NFFT)] = jnp.zeros((2 * NF, NFFT), jnp.bfloat16)


def spread_start(start_ref, spread_ref):
    row = lax.broadcasted_iota(jnp.int32, (NF, LANES), 0)
    lane = lax.broadcasted_iota(jnp.int32, (NF, LANES), 1)
    start = start_ref[pl.ds(0, 2 * NB), pl.ds(0, NF)]
    for g in range(NF // PACK):
        pick = (row == PACK * g + lane // NB).astype(jnp.float32)
        spread_ref[g] = jnp.dot(
            start,
            pick,
            precision=lax.Precision.HIGHEST,
            preferred_element_type=jnp.float32,
        )


def split(value):
    high = value.astype(jnp.bfloat16)
    low = (value - high.astype(jnp.float32)).astype(jnp.bfloat16)
    return high, low


def load_weights(w_ref, col_tiles):
    first = lax.axis_index("freq") * col_tiles
    return jnp.concatenate([w_ref[pl.ds(first + c, 1), :] for c in range(col_tiles)], axis=1)


def flip_groups(groups, flipped):
    turned = flipped.T
    lane = lax.broadcasted_iota(jnp.int32, (NB, LANES), 1)
    out = []
    for g in range(PACK):
        total = groups[g]
        for q in range(PACK):
            block = turned[q * NB : (q + 1) * NB]
            if q != g:
                block = pltpu.roll(block, ((q - g) % PACK) * NB, 1)
            total = total + jnp.where(lane // NB == q, block, 0.0)
        out.append(total)
    return out


TILE = 8


def turn_tiles(tiles):
    row = lax.broadcasted_iota(jnp.int32, (TILE, LANES), 0)
    step = TILE // 2
    while step:
        keep = row % (2 * step) < step
        turned = list(tiles)
        for i in range(TILE):
            if i % (2 * step) < step:
                low, high = tiles[i], tiles[i + step]
                turned[i] = jnp.where(keep, low, pltpu.roll(high, step, 0))
                turned[i + step] = jnp.where(keep, pltpu.roll(low, TILE - step, 0), high)
        tiles = turned
        step //= 2
    return tiles


def core_bit():
    return lax.rem(lax.axis_index("pts"), 2)


def y_bit():
    return lax.rem(lax.div(lax.axis_index("pts"), 2), 2)


RESP_ROWS = 2 * NF // PACK


def give_half(value_ref, bit, keep_ref, send_ref):
    half = keep_ref.shape[0] - RESP_ROWS
    keep_ref[pl.ds(0, half), :] = value_ref[pl.ds(bit * half, half), :]
    send_ref[pl.ds(0, half), :] = value_ref[pl.ds((1 - bit) * half, half), :]
    resp = value_ref[pl.ds(2 * half, RESP_ROWS), :]
    keep_ref[pl.ds(half, RESP_ROWS), :] = resp
    send_ref[pl.ds(half, RESP_ROWS), :] = resp


def gram_kernel(
    total_rows,
    places,
    by_core,
    x_hbm,
    aux_ref,
    keep_ref,
    send_ref,
    high_ref,
    rest_ref,
    low_hbm,
    x_ref,
    dft_ref,
    low_ref,
    block_even,
    block_odd,
    spec_ref,
    z_even,
    z_odd,
    real_ref,
    imag_ref,
    spread_ref,
    pack_ref,
    in_sems,
    out_sem,
):
    times, cols = x_ref.shape
    col_tiles = cols // LANES
    block_refs = (block_even, block_odd)
    cuts = [0] + [(first + TILE + 1) * HALF for first in range(0, NB, TILE)]

    def fetches(i):
        middle = (cuts[i] + cuts[i + 1]) // (2 * HALF) * HALF
        for n, (first, last) in enumerate(((cuts[i], middle), (middle, cuts[i + 1]))):
            rows = pl.ds(first, last - first)
            yield pltpu.make_async_copy(x_hbm.at[rows], x_ref.at[rows], in_sems.at[2 * i + n])

    for i in range(len(cuts) - 1):
        for fetch in fetches(i):
            fetch.start()
    fill_dft(dft_ref)
    spread_start(aux_ref, spread_ref)
    weights = load_weights(aux_ref.at[pl.ds(2 * NB, aux_ref.shape[0] - 2 * NB)], col_tiles)
    scale = jnp.sqrt(weights / (2.0 * total_rows))
    for fetch in fetches(0):
        fetch.wait()
    first_mean = jnp.mean(x_ref[pl.ds(0, NFFT), :], axis=0, keepdims=True)

    def center(i, acc):
        def step(h, acc):
            rows = pl.ds(pl.multiple_of(h * HALF, HALF), HALF)
            value = x_ref[rows, :] - first_mean
            high, low = split(value * scale)
            high_ref[rows, :] = high
            low_ref[rows, :] = low
            return acc + value

        return lax.fori_loop(cuts[i] // HALF, cuts[i + 1] // HALF, step, acc, unroll=True)

    def transform(first):
        for i in range(TILE // 2):
            blocks = []
            for s in range(2):
                rows = pl.ds((first + 2 * i + s) * HALF, NFFT)
                blocks.append(jnp.concatenate([high_ref[rows, :], low_ref[rows, :]], axis=0))
            both = jnp.dot(
                dft_ref[...], jnp.concatenate(blocks, axis=1), preferred_element_type=jnp.float32
            )
            spectrum = both[: 2 * NF] + both[2 * NF :]
            for s in range(2):
                block_refs[first // TILE % 2][2 * i + s] = spectrum[:, s * cols : (s + 1) * cols]

    def arrange(first):
        block_ref = block_refs[first // TILE % 2]
        for c in range(col_tiles):
            lanes = pl.ds(c * LANES, LANES)
            for o in range(2 * NF // TILE):
                rows = pl.ds(o * TILE, TILE)
                tiles = turn_tiles([block_ref[b, rows, lanes] for b in range(TILE)])
                for k in range(TILE):
                    spec_ref[c, o * TILE + k, pl.ds(first, TILE), :] = tiles[k]

    acc = center(0, jnp.zeros((HALF, cols), jnp.float32))
    transform(0)
    for first in range(0, NB, TILE):
        if first + TILE < NB:
            for fetch in fetches(first // TILE + 1):
                fetch.wait()
            acc = center(first // TILE + 1, acc)
            transform(first + TILE)
        arrange(first)
    pad = high_ref.shape[0] - times
    if pad:
        high_ref[pl.ds(times, pad), :] = jnp.zeros((pad, cols), jnp.bfloat16)
        low_ref[pl.ds(times, pad), :] = jnp.zeros((pad, cols), jnp.bfloat16)
    save_low = pltpu.make_async_copy(low_ref, low_hbm, out_sem)
    save_low.start()
    rest = jnp.sum(acc, axis=0, keepdims=True) / times * scale
    rest_ref[...] = jnp.broadcast_to(rest, rest_ref.shape)
    for k, leak in enumerate(window_leaks()):
        for c in range(col_tiles):
            part = rest[:, c * LANES : (c + 1) * LANES]
            spec_ref[c, k] = spec_ref[c, k] - leak * part

    row = lax.broadcasted_iota(jnp.int32, (NB, LANES), 0)
    lane = lax.broadcasted_iota(jnp.int32, (NB, LANES), 1)
    upper = row <= lane % NB
    octets = NF // 8

    def prepare(z_ref, octet, half):
        for part in range(2):
            for q in range(PACK):
                own = pl.ds(part * LANES + q * NB, NB)
                for c in range(col_tiles):
                    value = spec_ref[c, NF * part + TILE * octet + PACK * half + q]
                    high = value.astype(jnp.bfloat16)
                    low = (2.0 * (value - high.astype(jnp.float32))).astype(jnp.bfloat16)
                    z_ref[own, pl.ds(c * LANES, LANES)] = high
                    z_ref[own, pl.ds(cols + c * LANES, LANES)] = low

    def correlate(z_ref, group):
        high = z_ref[:, pl.ds(0, cols)]
        product = lax.dot_general(
            jnp.concatenate([high, high], axis=1),
            z_ref[...],
            (((1,), (1,)), ((), ())),
            preferred_element_type=jnp.float32,
        )
        gram_real = jnp.zeros((NB, LANES), jnp.float32)
        gram_imag = jnp.zeros((NB, LANES), jnp.float32)
        for q in range(PACK):
            mine = lane // NB == q
            real = product[q * NB : (q + 1) * NB]
            imag = product[LANES + q * NB : LANES + (q + 1) * NB]
            gram_real = jnp.where(mine, real[:, :LANES] + imag[:, LANES:], gram_real)
            gram_imag = jnp.where(mine, real[:, LANES:] - imag[:, :LANES], gram_imag)
        real_ref[group] = gram_real
        imag_ref[group] = gram_imag

    prepare(z_even, 0, 0)

    def step(o, carry):
        prepare(z_odd, o, 1)
        correlate(z_even, 2 * o)
        prepare(z_even, jnp.minimum(o + 1, octets - 1), 0)
        correlate(z_odd, 2 * o + 1)
        return carry

    lax.fori_loop(0, octets, step, 0)
    left = lane[: NB // 2] < LANES // 2
    half = NB // 2
    resp_real = []
    resp_imag = []
    for quad in range(NF // PACK // PACK):
        own = pl.ds(quad * PACK, PACK)
        reals = [real_ref[quad * PACK + g] for g in range(PACK)]
        imags = [imag_ref[quad * PACK + g] for g in range(PACK)]
        reals = flip_groups(reals, real_ref[own].reshape(PACK * NB, LANES))
        imags = flip_groups(imags, -imag_ref[own].reshape(PACK * NB, LANES))
        for g, (real, imag) in enumerate(zip(reals, imags)):
            group = quad * PACK + g
            start_real = spread_ref[group, pl.ds(0, NB), :]
            start_imag = spread_ref[group, pl.ds(NB, NB), :]
            resp_real.append(
                jnp.sum(real * start_real + imag * start_imag, axis=0, keepdims=True)
            )
            resp_imag.append(
                jnp.sum(real * start_imag - imag * start_real, axis=0, keepdims=True)
            )
            packed = jnp.where(upper, real, imag)
            top = packed[:half]
            bottom = packed[half:]
            even = jnp.where(left, top, pltpu.roll(bottom, LANES // 2, 1))
            odd = jnp.where(left, pltpu.roll(top, LANES // 2, 1), bottom)
            pack_ref[pl.ds(places[2 * group] * half, half), :] = even
            pack_ref[pl.ds(places[2 * group + 1] * half, half), :] = odd
    resp = jnp.concatenate(resp_real + resp_imag, axis=0)
    pack_ref[pl.ds(NF // 2 * half, RESP_ROWS), :] = resp
    give_half(pack_ref, core_bit() if by_core else 0, keep_ref, send_ref)
    save_low.wait()


def gram_parts(snapshots, weight_rows, start_vec, total_rows, places, by_core):
    times, cols = snapshots.shape
    start = jnp.transpose(start_vec, (1, 2, 0)).reshape(2 * NB, NF)
    start = jnp.pad(start, ((0, 0), (0, LANES - NF)))
    aux = jnp.concatenate([start, weight_rows], axis=0)
    any_space = pl.BlockSpec(memory_space=pl.ANY)
    saved = jax.ShapeDtypeStruct((-(-times // LANES) * LANES, cols), jnp.bfloat16)
    half = floats(NF // 4 * NB // 2 + RESP_ROWS, LANES)
    return pl.pallas_call(
        functools.partial(gram_kernel, total_rows, places, by_core),
        out_shape=(half, half, saved, floats(8, cols), saved),
        in_specs=[any_space, VMEM],
        out_specs=(VMEM, VMEM, VMEM, VMEM, any_space),
        scratch_shapes=[
            pltpu.VMEM((times, cols), jnp.float32),
            pltpu.VMEM((4 * NF, 2 * NFFT), jnp.bfloat16),
            pltpu.VMEM(saved.shape, jnp.bfloat16),
            pltpu.VMEM((TILE, 2 * NF, cols), jnp.float32),
            pltpu.VMEM((TILE, 2 * NF, cols), jnp.float32),
            pltpu.VMEM((cols // LANES, 2 * NF, NB, LANES), jnp.float32),
            pltpu.VMEM((2 * LANES, 2 * cols), jnp.bfloat16),
            pltpu.VMEM((2 * LANES, 2 * cols), jnp.bfloat16),
            pltpu.VMEM((NF // PACK, NB, LANES), jnp.float32),
            pltpu.VMEM((NF // PACK, NB, LANES), jnp.float32),
            pltpu.VMEM((NF // PACK, 2 * NB, LANES), jnp.float32),
            pltpu.VMEM((NF // 2 * NB // 2 + RESP_ROWS, LANES), jnp.float32),
            pltpu.SemaphoreType.DMA((2 * NB // TILE,)),
            pltpu.SemaphoreType.DMA(()),
        ],
        compiler_params=pltpu.CompilerParams(vmem_limit_bytes=VMEM_LIMIT),
        cost_estimate=pl.CostEstimate(
            flops=5_000_000_000, bytes_accessed=8_000_000, transcendentals=0
        ),
        name="gram_parts",
    )(snapshots, aux)


def pair_square(even, odd):
    left = lax.broadcasted_iota(jnp.int32, (NB // 2, LANES), 1) < LANES // 2
    top = jnp.where(left, even, pltpu.roll(odd, LANES // 2, 1))
    bottom = jnp.where(left, pltpu.roll(even, LANES // 2, 1), odd)
    return jnp.concatenate([top, bottom], axis=0)


def hermitian(squares):
    row = lax.broadcasted_iota(jnp.int32, (NB, LANES), 0)
    col = lax.broadcasted_iota(jnp.int32, (NB, LANES), 1) % NB
    zero = jnp.zeros((NB, LANES), jnp.float32)
    full = squares + [zero] * (PACK - len(squares))
    turned = flip_groups([zero] * PACK, jnp.concatenate(full, axis=0))
    for square, flipped in zip(squares, turned):
        real = jnp.where(row <= col, square, flipped)
        imag = jnp.where(row > col, square, jnp.where(row < col, -flipped, 0.0))
        yield real, imag


def small_call(kernel, name, out_shape, scratch_shapes=(), limit=SMALL_LIMIT):
    def call(*args):
        return pl.pallas_call(
            kernel,
            out_shape=out_shape,
            in_specs=[VMEM] * len(args),
            out_specs=VMEM if isinstance(out_shape, jax.ShapeDtypeStruct) else (VMEM,) * len(out_shape),
            scratch_shapes=list(scratch_shapes),
            compiler_params=pltpu.CompilerParams(vmem_limit_bytes=limit),
            name=name,
        )(*args)

    return call


def floats(*shape):
    return jax.ShapeDtypeStruct(shape, jnp.float32)


def add_core_kernel(kept_ref, got_ref, out_ref):
    quarter = out_ref.shape[1] - RESP_ROWS
    tail = pl.ds(4 * quarter, RESP_ROWS)
    resp = kept_ref[tail, :] + got_ref[tail, :]
    for m in range(4):
        rows = pl.ds(m * quarter, quarter)
        out_ref[m, pl.ds(0, quarter), :] = kept_ref[rows, :] + got_ref[rows, :]
        out_ref[m, pl.ds(quarter, RESP_ROWS), :] = resp


def add_core(kept, got):
    quarter = (kept.shape[0] - RESP_ROWS) // 4
    return small_call(add_core_kernel, "add_core", floats(4, quarter + RESP_ROWS, LANES))(kept, got)


def add_near_kernel(parts_ref, out_ref):
    out_ref[...] = (parts_ref[0] + parts_ref[1]) + (parts_ref[2] + parts_ref[3])


def add_kernel(kept_ref, got_ref, out_ref):
    out_ref[...] = kept_ref[...] + got_ref[...]


def add(name, kept, got):
    return small_call(add_kernel, name, floats(*kept.shape))(kept, got)


def finish_kernel(kept_ref, got_ref, packed_ref, resp_ref):
    rows = packed_ref.shape[0]
    packed_ref[...] = kept_ref[pl.ds(0, rows), :] + got_ref[pl.ds(0, rows), :]
    tail = pl.ds(rows, RESP_ROWS)
    resp = kept_ref[tail, :] + got_ref[tail, :]
    real = resp[: RESP_ROWS // 2]
    imag = resp[RESP_ROWS // 2 :]
    power = real * real + imag * imag
    lane = lax.broadcasted_iota(jnp.int32, power.shape, 1)
    mean = jnp.zeros(power.shape, jnp.float32)
    for q in range(PACK):
        mine = lane // NB == q
        part = jnp.sum(jnp.where(mine, power, 0.0), axis=1, keepdims=True) / NB
        mean = jnp.where(mine, part, mean)
    scaling = 1.0 / jnp.sqrt(mean + 1e-06)
    resp_ref[pl.ds(0, RESP_ROWS // 2), :] = real * scaling
    resp_ref[pl.ds(RESP_ROWS // 2, RESP_ROWS // 2), :] = imag * scaling


def finish(kept, got):
    rows = kept.shape[0] - RESP_ROWS
    return small_call(finish_kernel, "finish", (floats(rows, LANES), floats(RESP_ROWS, LANES)))(
        kept, got
    )


def join_y_kernel(own_ref, got_ref, packed_ref):
    rows = own_ref.shape[0]
    for m, ref in enumerate((own_ref, got_ref)):
        packed_ref[pl.ds((y_bit() ^ m) * rows, rows), :] = ref[...]


def unpack_kernel(*refs):
    parts, out_ref = refs[:-1], refs[-1]
    half = NB // 2
    for m, part in enumerate(parts):
        count = part.shape[0] // half
        place = (core_bit() ^ m) * 2 * count if len(parts) > 1 else 0
        for first in range(0, count, 2 * PACK):
            last = min(first + 2 * PACK, count)
            pairs = [part[pl.ds(i * half, half), :] for i in range(first, last)]
            squares = [pair_square(*pairs[i : i + 2]) for i in range(0, len(pairs), 2)]
            for g, both in enumerate(hermitian(squares)):
                for q in range(PACK):
                    freq = place + 2 * first + PACK * g + q
                    for c in range(2):
                        out_ref[freq, c] = both[c][:, q * NB : (q + 1) * NB]


def unpack_gram(*parts):
    count = sum(part.shape[0] for part in parts) * 4 // NB
    return small_call(unpack_kernel, "unpack_gram", floats(count, 2, NB, NB))(*parts)


def modes_kernel(
    total_rows, high_ref, low_hbm, rest_ref, w_ref, table_ref, resp_ref, out_ref, low_ref, a_ref, sems
):
    padded, cols = high_ref.shape
    pieces = sems.shape[0]
    fetches = []
    for i in range(pieces):
        first = padded // LANES * i // pieces * LANES
        last = padded // LANES * (i + 1) // pieces * LANES
        rows = pl.ds(first, last - first)
        fetches.append(pltpu.make_async_copy(low_hbm.at[rows], low_ref.at[rows], sems.at[i]))
    for fetch in fetches:
        fetch.start()
    row = lax.broadcasted_iota(jnp.int32, (RESP_ROWS, 1), 0)
    leaks = window_leaks()
    corrections = []
    groups = RESP_ROWS // 2
    lane = lax.broadcasted_iota(jnp.int32, (RESP_ROWS, LANES), 1)
    left = lane < HALF
    for q in range(PACK):
        resp = resp_ref[...]
        if q:
            resp = pltpu.roll(resp, LANES - q * NB, 1)
        if q < len(leaks):
            total = jnp.sum(jnp.where(lane < NB, resp, 0.0), axis=1, keepdims=True) * leaks[q]
            corrections.append(jnp.where(row % groups == 0, total, 0.0) * rest_ref[pl.ds(0, 1), :])
        else:
            corrections.append(jnp.zeros((RESP_ROWS, cols), jnp.float32))
        real = jnp.concatenate([resp[:groups]] * 2, axis=0)
        imag = jnp.concatenate([resp[groups:]] * 2, axis=0)
        rows = pl.ds(q * RESP_ROWS, RESP_ROWS)
        first = table_ref[0, rows, :]
        second = table_ref[1, rows, :]
        first_turned = pltpu.roll(first, HALF, 1)
        second_turned = pltpu.roll(second, HALF, 1)

        def spread(value, block):
            if 0 <= block < NB:
                return jnp.broadcast_to(value[:, block : block + 1], (RESP_ROWS, LANES))
            return jnp.zeros((RESP_ROWS, LANES), jnp.float32)

        for m in range(padded // LANES):
            value = first_turned * jnp.where(left, spread(real, 2 * m - 1), spread(real, 2 * m + 1))
            value += second_turned * jnp.where(
                left, spread(imag, 2 * m - 1), spread(imag, 2 * m + 1)
            )
            if 2 * m < NB:
                value += first * spread(real, 2 * m) + second * spread(imag, 2 * m)
            high, low = split(value)
            own = pl.ds(m * LANES, LANES)
            a_ref[rows, own] = high
            a_ref[pl.ds(2 * NF + q * RESP_ROWS, RESP_ROWS), own] = low
    both = jnp.dot(a_ref[...], high_ref[...], preferred_element_type=jnp.float32)
    modes = both[: 2 * NF] + both[2 * NF :]
    modes -= jnp.concatenate(corrections, axis=0)
    for fetch in fetches:
        fetch.wait()
    modes += jnp.dot(
        a_ref[pl.ds(0, 2 * NF), :], low_ref[...], preferred_element_type=jnp.float32
    )
    modes = modes * jnp.sqrt(2.0 * total_rows / load_weights(w_ref, cols // LANES))
    n_freq = out_ref.shape[0]
    mine = groups // n_freq
    group = lax.axis_index("freq")
    for q in range(PACK):
        for part in range(2):
            for f in range(n_freq):
                first = q * RESP_ROWS + part * groups + f * mine
                slot = f ^ group if n_freq == 2 else f
                for c in range(cols // LANES):
                    out_ref[slot, 2 * c + part, pl.ds(q, mine, stride=PACK), :] = modes[
                        first : first + mine, c * LANES : (c + 1) * LANES
                    ]


def local_modes(high, low, rest, weight_rows, response, total_rows, n_freq):
    padded, cols = high.shape
    return pl.pallas_call(
        functools.partial(modes_kernel, total_rows),
        out_shape=floats(n_freq, 2 * cols // LANES, NF // n_freq, LANES),
        in_specs=[VMEM, pl.BlockSpec(memory_space=pl.ANY)] + [VMEM] * 4,
        out_specs=VMEM,
        scratch_shapes=[
            pltpu.VMEM((padded, cols), jnp.bfloat16),
            pltpu.VMEM((4 * NF, padded), jnp.bfloat16),
            pltpu.SemaphoreType.DMA((4,)),
        ],
        compiler_params=pltpu.CompilerParams(vmem_limit_bytes=VMEM_LIMIT),
        cost_estimate=pl.CostEstimate(
            flops=3_000_000_000, bytes_accessed=8_000_000, transcendentals=0
        ),
        name="local_modes",
    )(high, low, rest, weight_rows, jnp.asarray(mode_tables()), response)


def join_kernel(kept_ref, got_ref, out_ref):
    tiles = got_ref.shape[0] // 2
    group = lax.axis_index("freq")
    for slot, ref in enumerate((kept_ref.at[0], got_ref)):
        for c in range(tiles):
            lanes = pl.ds(pl.multiple_of(((group ^ slot) * tiles + c) * LANES, LANES), LANES)
            for part in range(2):
                out_ref[:, part, lanes] = ref[2 * c + part]


def join_modes(kept, got):
    tiles, count, _ = got.shape
    return small_call(join_kernel, "join_modes", floats(count, 2, tiles * LANES))(kept, got)


def response_of(gram, start_vec):
    matvec = functools.partial(jnp.einsum, "fjk,fk->fj", precision=lax.Precision.HIGHEST)
    resp_real = matvec(gram[:, 0], start_vec[:, 0]) - matvec(gram[:, 1], start_vec[:, 1])
    resp_imag = matvec(gram[:, 0], start_vec[:, 1]) + matvec(gram[:, 1], start_vec[:, 0])
    scaling = 1.0 / jnp.sqrt(
        jnp.mean(resp_real * resp_real + resp_imag * resp_imag, axis=1, keepdims=True) + 1e-06
    )
    return jnp.stack([resp_real * scaling, resp_imag * scaling], axis=1)


def direction_shards(n_devices, snapshots, weight, start_vec):
    def swap(value, mask):
        return lax.ppermute(value, ("pts", "freq"), [(i, i ^ mask) for i in range(n_devices)])

    x, core, y, z_near, z_far = 1, 2, 4, 8, 16
    near = [
        [first + far, first + far + x, first + far + y, first + far + y + x]
        for far in range(0, n_devices, z_near)
        for first in (0, core)
    ]
    total_rows = float(weight.shape[0] * 16)
    weight_rows = weight.reshape(-1, LANES)
    places = [
        (i // 8 % 2) * 16 + (i // 4 % 2) * 8 + (i // 16) * 4 + i % 4 for i in range(NF // 2)
    ]
    keep, send, high, rest, low = gram_parts(
        snapshots, weight_rows, start_vec, total_rows, places, True
    )
    parts = add_core(keep, swap(send, core))
    parts = lax.all_to_all(
        parts, ("pts", "freq"), 0, 0, axis_index_groups=near, tiled=True
    )
    part = small_call(add_near_kernel, "add_near", floats(*parts.shape[1:]))(parts)
    part = add("add_z", part, swap(part, z_near))
    packed, response = finish(part, swap(part, z_far))
    other = swap(packed, y)
    modes = local_modes(high, low, rest, weight_rows, response, total_rows, 2)
    packed = small_call(join_y_kernel, "join_y", floats(2 * packed.shape[0], LANES))(packed, other)
    gram_mine = unpack_gram(packed, swap(packed, core))
    return gram_mine, join_modes(modes, swap(modes[1], x))


def shards(n_pts, n_freq, snapshots, weight, start_vec):
    cols = snapshots.shape[1]
    total_rows = float(weight.shape[0] * n_pts)
    n_devices = n_pts * n_freq
    mine_count = NF // n_freq
    group = lax.axis_index("freq")
    weight_rows = weight.reshape(-1, LANES)
    places = list(range(NF // 2))
    first, second, high, rest, low = gram_parts(
        snapshots, weight_rows, start_vec, total_rows, places, False
    )
    parts = jnp.concatenate([first[:-RESP_ROWS], second[:-RESP_ROWS]], axis=0)
    share = parts.reshape(n_devices, -1)
    share = jnp.sum(lax.all_to_all(share, ("freq", "pts"), 0, 0, tiled=True), axis=0)
    packed = lax.all_gather(share, "pts", axis=0, tiled=True)
    gram_mine = unpack_gram(packed.reshape(-1, LANES))
    start_mine = lax.dynamic_slice_in_dim(start_vec, group * mine_count, mine_count, 0)
    response = lax.all_gather(response_of(gram_mine, start_mine), "freq", axis=0, tiled=True)
    response = jnp.transpose(response.reshape(NF // PACK, PACK, 2, NB), (2, 0, 1, 3))
    response = response.reshape(RESP_ROWS, LANES)
    modes = local_modes(high, low, rest, weight_rows, response, total_rows, n_freq)
    modes = lax.all_to_all(modes, "freq", 0, 0, tiled=True)
    modes = modes.reshape(n_freq, cols // LANES, 2, mine_count, LANES)
    modes = jnp.transpose(modes, (3, 2, 0, 1, 4)).reshape(mine_count, 2, n_freq * cols)
    return gram_mine, modes


def solution(mesh):
    n_pts, n_freq = mesh.shape["pts"], mesh.shape["freq"]
    if (n_pts, n_freq) == (16, 2):
        body = functools.partial(direction_shards, n_pts * n_freq)
    else:
        body = functools.partial(shards, n_pts, n_freq)
    placed = (P(None, ("pts", "freq")), P("pts"), P())
    return jax.shard_map(
        body,
        mesh=mesh,
        in_specs=placed,
        out_specs=(P("freq", None, None, None), P("freq", None, "pts")),
        check_vma=False,
    )
```

```python
import functools
import math

import jax
import jax.numpy as jnp
import numpy as np
from jax import lax
from jax.experimental import pallas as pl
from jax.experimental.pallas import tpu as pltpu
from jax.sharding import PartitionSpec as P

NFFT = 128
HALF = NFFT // 2
NF = 64
NB = 32
LANES = 128
PACK = 4
VMEM_LIMIT = 51 * 1024 * 1024
SMALL_LIMIT = 8 * 1024 * 1024
UNPACK_LIMIT = 53 * 1024 * 1024
VMEM = pl.BlockSpec(memory_space=pltpu.VMEM)


def dft_values():
    times = np.arange(NFFT)
    freqs = np.arange(NF)
    phases = (freqs[:, None] * times[None, :] % NFFT) * (2.0 * math.pi / NFFT)
    window = 0.5 - 0.5 * np.cos(times * (2.0 * math.pi / NFFT))
    weighted = window / np.sqrt(np.sum(window * window))
    return np.cos(phases) * weighted, -np.sin(phases) * weighted


def split_table(table):
    high = table.astype(jnp.bfloat16)
    low = (table - high.astype(np.float64)).astype(jnp.bfloat16)
    return high, low


def window_leaks():
    real, _ = dft_values()
    return [float(np.sum(real[k])) for k in range(2)]


def mode_tables():
    real, imag = dft_values()
    order = np.arange(NF).reshape(NF // PACK, PACK).T
    real, imag = real[order], imag[order]
    first = np.stack([real, imag], axis=1).reshape(2 * NF, NFFT)
    second = np.stack([-imag, real], axis=1).reshape(2 * NF, NFFT)
    return np.stack([first, second]).astype(np.float32)


def cosine_of_turns(count):
    folded = jnp.minimum(count, NFFT - count)
    angle = (NFFT // 4 - folded).astype(jnp.float32) * (2.0 * math.pi / NFFT)
    square = angle * angle
    series = 1.0
    for n in (10, 8, 6, 4, 2):
        series = 1.0 - square * series * (1.0 / (n * (n + 1)))
    return angle * series


def fill_dft(dft_ref):
    row = lax.broadcasted_iota(jnp.int32, (2 * NF, NFFT), 0)
    time = lax.broadcasted_iota(jnp.int32, (2 * NF, NFFT), 1)
    quarter = jnp.where(row < NF, 0, NFFT // 4)
    wave = cosine_of_turns((row % NF * time + quarter) % NFFT)
    window = 0.5 - 0.5 * np.cos(np.arange(NFFT) * (2.0 * math.pi / NFFT))
    norm = float(np.sqrt(np.sum(window * window)))
    high, low = split(wave * ((0.5 - 0.5 * cosine_of_turns(time)) / norm))
    dft_ref[pl.ds(0, 2 * NF), pl.ds(0, NFFT)] = high
    dft_ref[pl.ds(0, 2 * NF), pl.ds(NFFT, NFFT)] = high
    dft_ref[pl.ds(2 * NF, 2 * NF), pl.ds(0, NFFT)] = low
    dft_ref[pl.ds(2 * NF, 2 * NF), pl.ds(NFFT, NFFT)] = jnp.zeros((2 * NF, NFFT), jnp.bfloat16)


def spread_start(start_ref, spread_ref):
    row = lax.broadcasted_iota(jnp.int32, (NF, LANES), 0)
    lane = lax.broadcasted_iota(jnp.int32, (NF, LANES), 1)
    start = start_ref[pl.ds(0, 2 * NB), pl.ds(0, NF)]
    for g in range(NF // PACK):
        pick = (row == PACK * g + lane // NB).astype(jnp.float32)
        spread_ref[g] = jnp.dot(
            start,
            pick,
            precision=lax.Precision.HIGHEST,
            preferred_element_type=jnp.float32,
        )


def split(value):
    high = value.astype(jnp.bfloat16)
    low = (value - high.astype(jnp.float32)).astype(jnp.bfloat16)
    return high, low


def load_weights(w_ref, col_tiles):
    first = lax.axis_index("freq") * col_tiles
    return jnp.concatenate([w_ref[pl.ds(first + c, 1), :] for c in range(col_tiles)], axis=1)


def flip_groups(groups, flipped):
    turned = flipped.T
    lane = lax.broadcasted_iota(jnp.int32, (NB, LANES), 1)
    out = []
    for g in range(PACK):
        total = groups[g]
        for q in range(PACK):
            block = turned[q * NB : (q + 1) * NB]
            if q != g:
                block = pltpu.roll(block, ((q - g) % PACK) * NB, 1)
            total = total + jnp.where(lane // NB == q, block, 0.0)
        out.append(total)
    return out


TILE = 8


def turn_tiles(tiles):
    row = lax.broadcasted_iota(jnp.int32, (TILE, LANES), 0)
    step = TILE // 2
    while step:
        keep = row % (2 * step) < step
        turned = list(tiles)
        for i in range(TILE):
            if i % (2 * step) < step:
                low, high = tiles[i], tiles[i + step]
                turned[i] = jnp.where(keep, low, pltpu.roll(high, step, 0))
                turned[i + step] = jnp.where(keep, pltpu.roll(low, TILE - step, 0), high)
        tiles = turned
        step //= 2
    return tiles


def core_bit():
    return lax.rem(lax.axis_index("pts"), 2)


def y_bit():
    return lax.rem(lax.div(lax.axis_index("pts"), 2), 2)


RESP_ROWS = 2 * NF // PACK


def give_half(value_ref, bit, keep_ref, send_ref):
    half = keep_ref.shape[0] - RESP_ROWS
    keep_ref[pl.ds(0, half), :] = value_ref[pl.ds(bit * half, half), :]
    send_ref[pl.ds(0, half), :] = value_ref[pl.ds((1 - bit) * half, half), :]
    resp = value_ref[pl.ds(2 * half, RESP_ROWS), :]
    keep_ref[pl.ds(half, RESP_ROWS), :] = resp
    send_ref[pl.ds(half, RESP_ROWS), :] = resp


def gram_kernel(
    total_rows,
    places,
    by_core,
    x_hbm,
    aux_ref,
    keep_ref,
    send_ref,
    high_ref,
    rest_ref,
    low_hbm,
    x_ref,
    dft_ref,
    low_ref,
    block_even,
    block_odd,
    spec_ref,
    z_even,
    z_odd,
    real_ref,
    imag_ref,
    spread_ref,
    pack_ref,
    in_sems,
    out_sem,
):
    times, cols = x_ref.shape
    col_tiles = cols // LANES
    block_refs = (block_even, block_odd)
    cuts = [0] + [(first + TILE + 1) * HALF for first in range(0, NB, TILE)]

    def fetches(i):
        middle = (cuts[i] + cuts[i + 1]) // (2 * HALF) * HALF
        for n, (first, last) in enumerate(((cuts[i], middle), (middle, cuts[i + 1]))):
            rows = pl.ds(first, last - first)
            yield pltpu.make_async_copy(x_hbm.at[rows], x_ref.at[rows], in_sems.at[2 * i + n])

    for i in range(len(cuts) - 1):
        for fetch in fetches(i):
            fetch.start()
    fill_dft(dft_ref)
    spread_start(aux_ref, spread_ref)
    weights = load_weights(aux_ref.at[pl.ds(2 * NB, aux_ref.shape[0] - 2 * NB)], col_tiles)
    scale = jnp.sqrt(weights / (2.0 * total_rows))
    for fetch in fetches(0):
        fetch.wait()
    first_mean = jnp.mean(x_ref[pl.ds(0, NFFT), :], axis=0, keepdims=True)

    def center(i, acc):
        def step(h, acc):
            rows = pl.ds(pl.multiple_of(h * HALF, HALF), HALF)
            value = x_ref[rows, :] - first_mean
            high, low = split(value * scale)
            high_ref[rows, :] = high
            low_ref[rows, :] = low
            return acc + value

        return lax.fori_loop(cuts[i] // HALF, cuts[i + 1] // HALF, step, acc, unroll=True)

    def transform(first):
        for i in range(TILE // 2):
            blocks = []
            for s in range(2):
                rows = pl.ds((first + 2 * i + s) * HALF, NFFT)
                blocks.append(jnp.concatenate([high_ref[rows, :], low_ref[rows, :]], axis=0))
            both = jnp.dot(
                dft_ref[...], jnp.concatenate(blocks, axis=1), preferred_element_type=jnp.float32
            )
            spectrum = both[: 2 * NF] + both[2 * NF :]
            for s in range(2):
                block_refs[first // TILE % 2][2 * i + s] = spectrum[:, s * cols : (s + 1) * cols]

    def arrange(first):
        block_ref = block_refs[first // TILE % 2]
        for c in range(col_tiles):
            lanes = pl.ds(c * LANES, LANES)
            for o in range(2 * NF // TILE):
                rows = pl.ds(o * TILE, TILE)
                tiles = turn_tiles([block_ref[b, rows, lanes] for b in range(TILE)])
                for k in range(TILE):
                    spec_ref[c, o * TILE + k, pl.ds(first, TILE), :] = tiles[k]

    acc = center(0, jnp.zeros((HALF, cols), jnp.float32))
    transform(0)
    for first in range(0, NB, TILE):
        if first + TILE < NB:
            for fetch in fetches(first // TILE + 1):
                fetch.wait()
            acc = center(first // TILE + 1, acc)
            transform(first + TILE)
        arrange(first)
    pad = high_ref.shape[0] - times
    if pad:
        high_ref[pl.ds(times, pad), :] = jnp.zeros((pad, cols), jnp.bfloat16)
        low_ref[pl.ds(times, pad), :] = jnp.zeros((pad, cols), jnp.bfloat16)
    save_low = pltpu.make_async_copy(low_ref, low_hbm, out_sem)
    save_low.start()
    rest = jnp.sum(acc, axis=0, keepdims=True) / times * scale
    rest_ref[...] = jnp.broadcast_to(rest, rest_ref.shape)
    for k, leak in enumerate(window_leaks()):
        for c in range(col_tiles):
            part = rest[:, c * LANES : (c + 1) * LANES]
            spec_ref[c, k] = spec_ref[c, k] - leak * part

    row = lax.broadcasted_iota(jnp.int32, (NB, LANES), 0)
    lane = lax.broadcasted_iota(jnp.int32, (NB, LANES), 1)
    upper = row <= lane % NB
    octets = NF // 8

    def prepare(z_ref, octet, half):
        for part in range(2):
            for q in range(PACK):
                own = pl.ds(part * LANES + q * NB, NB)
                for c in range(col_tiles):
                    value = spec_ref[c, NF * part + TILE * octet + PACK * half + q]
                    high = value.astype(jnp.bfloat16)
                    low = (2.0 * (value - high.astype(jnp.float32))).astype(jnp.bfloat16)
                    z_ref[own, pl.ds(c * LANES, LANES)] = high
                    z_ref[own, pl.ds(cols + c * LANES, LANES)] = low

    def correlate(z_ref, group):
        high = z_ref[:, pl.ds(0, cols)]
        product = lax.dot_general(
            jnp.concatenate([high, high], axis=1),
            z_ref[...],
            (((1,), (1,)), ((), ())),
            preferred_element_type=jnp.float32,
        )
        gram_real = jnp.zeros((NB, LANES), jnp.float32)
        gram_imag = jnp.zeros((NB, LANES), jnp.float32)
        for q in range(PACK):
            mine = lane // NB == q
            real = product[q * NB : (q + 1) * NB]
            imag = product[LANES + q * NB : LANES + (q + 1) * NB]
            gram_real = jnp.where(mine, real[:, :LANES] + imag[:, LANES:], gram_real)
            gram_imag = jnp.where(mine, real[:, LANES:] - imag[:, :LANES], gram_imag)
        real_ref[group] = gram_real
        imag_ref[group] = gram_imag

    left = lane[: NB // 2] < LANES // 2
    half = NB // 2
    resp_real = []
    resp_imag = []

    def finish_quad(quad):
        own = pl.ds(quad * PACK, PACK)
        reals = [real_ref[quad * PACK + g] for g in range(PACK)]
        imags = [imag_ref[quad * PACK + g] for g in range(PACK)]
        reals = flip_groups(reals, real_ref[own].reshape(PACK * NB, LANES))
        imags = flip_groups(imags, -imag_ref[own].reshape(PACK * NB, LANES))
        for g, (real, imag) in enumerate(zip(reals, imags)):
            group = quad * PACK + g
            start_real = spread_ref[group, pl.ds(0, NB), :]
            start_imag = spread_ref[group, pl.ds(NB, NB), :]
            resp_real.append(
                jnp.sum(real * start_real + imag * start_imag, axis=0, keepdims=True)
            )
            resp_imag.append(
                jnp.sum(real * start_imag - imag * start_real, axis=0, keepdims=True)
            )
            packed = jnp.where(upper, real, imag)
            top = packed[:half]
            bottom = packed[half:]
            even = jnp.where(left, top, pltpu.roll(bottom, LANES // 2, 1))
            odd = jnp.where(left, pltpu.roll(top, LANES // 2, 1), bottom)
            pack_ref[pl.ds(places[2 * group] * half, half), :] = even
            pack_ref[pl.ds(places[2 * group + 1] * half, half), :] = odd

    z_refs = (z_even, z_odd)
    groups = NF // PACK
    prepare(z_even, 0, 0)
    for group in range(groups):
        if group + 1 < groups:
            prepare(z_refs[(group + 1) % 2], (group + 1) // 2, (group + 1) % 2)
        correlate(z_refs[group % 2], group)
        if group % PACK == PACK - 1:
            finish_quad(group // PACK)
    resp = jnp.concatenate(resp_real + resp_imag, axis=0)
    pack_ref[pl.ds(NF // 2 * half, RESP_ROWS), :] = resp
    give_half(pack_ref, core_bit() if by_core else 0, keep_ref, send_ref)
    save_low.wait()


def gram_parts(snapshots, weight_rows, start_vec, total_rows, places, by_core):
    times, cols = snapshots.shape
    start = jnp.transpose(start_vec, (1, 2, 0)).reshape(2 * NB, NF)
    start = jnp.pad(start, ((0, 0), (0, LANES - NF)))
    aux = jnp.concatenate([start, weight_rows], axis=0)
    any_space = pl.BlockSpec(memory_space=pl.ANY)
    saved = jax.ShapeDtypeStruct((-(-times // LANES) * LANES, cols), jnp.bfloat16)
    half = floats(NF // 4 * NB // 2 + RESP_ROWS, LANES)
    return pl.pallas_call(
        functools.partial(gram_kernel, total_rows, places, by_core),
        out_shape=(half, half, saved, floats(8, cols), saved),
        in_specs=[any_space, VMEM],
        out_specs=(VMEM, VMEM, VMEM, VMEM, any_space),
        scratch_shapes=[
            pltpu.VMEM((times, cols), jnp.float32),
            pltpu.VMEM((4 * NF, 2 * NFFT), jnp.bfloat16),
            pltpu.VMEM(saved.shape, jnp.bfloat16),
            pltpu.VMEM((TILE, 2 * NF, cols), jnp.float32),
            pltpu.VMEM((TILE, 2 * NF, cols), jnp.float32),
            pltpu.VMEM((cols // LANES, 2 * NF, NB, LANES), jnp.float32),
            pltpu.VMEM((2 * LANES, 2 * cols), jnp.bfloat16),
            pltpu.VMEM((2 * LANES, 2 * cols), jnp.bfloat16),
            pltpu.VMEM((NF // PACK, NB, LANES), jnp.float32),
            pltpu.VMEM((NF // PACK, NB, LANES), jnp.float32),
            pltpu.VMEM((NF // PACK, 2 * NB, LANES), jnp.float32),
            pltpu.VMEM((NF // 2 * NB // 2 + RESP_ROWS, LANES), jnp.float32),
            pltpu.SemaphoreType.DMA((2 * NB // TILE,)),
            pltpu.SemaphoreType.DMA(()),
        ],
        compiler_params=pltpu.CompilerParams(vmem_limit_bytes=VMEM_LIMIT),
        cost_estimate=pl.CostEstimate(
            flops=5_000_000_000, bytes_accessed=8_000_000, transcendentals=0
        ),
        name="gram_parts",
    )(snapshots, aux)


def pair_square(even, odd):
    left = lax.broadcasted_iota(jnp.int32, (NB // 2, LANES), 1) < LANES // 2
    top = jnp.where(left, even, pltpu.roll(odd, LANES // 2, 1))
    bottom = jnp.where(left, pltpu.roll(even, LANES // 2, 1), odd)
    return jnp.concatenate([top, bottom], axis=0)


def hermitian(squares):
    row = lax.broadcasted_iota(jnp.int32, (NB, LANES), 0)
    col = lax.broadcasted_iota(jnp.int32, (NB, LANES), 1) % NB
    zero = jnp.zeros((NB, LANES), jnp.float32)
    full = squares + [zero] * (PACK - len(squares))
    turned = flip_groups([zero] * PACK, jnp.concatenate(full, axis=0))
    for square, flipped in zip(squares, turned):
        real = jnp.where(row <= col, square, flipped)
        imag = jnp.where(row > col, square, jnp.where(row < col, -flipped, 0.0))
        yield real, imag


def small_call(kernel, name, out_shape, scratch_shapes=(), limit=SMALL_LIMIT):
    def call(*args):
        return pl.pallas_call(
            kernel,
            out_shape=out_shape,
            in_specs=[VMEM] * len(args),
            out_specs=VMEM if isinstance(out_shape, jax.ShapeDtypeStruct) else (VMEM,) * len(out_shape),
            scratch_shapes=list(scratch_shapes),
            compiler_params=pltpu.CompilerParams(vmem_limit_bytes=limit),
            name=name,
        )(*args)

    return call


def floats(*shape):
    return jax.ShapeDtypeStruct(shape, jnp.float32)


def add_core_kernel(kept_ref, got_ref, out_ref):
    quarter = out_ref.shape[1] - RESP_ROWS
    tail = pl.ds(4 * quarter, RESP_ROWS)
    resp = kept_ref[tail, :] + got_ref[tail, :]
    for m in range(4):
        rows = pl.ds(m * quarter, quarter)
        out_ref[m, pl.ds(0, quarter), :] = kept_ref[rows, :] + got_ref[rows, :]
        out_ref[m, pl.ds(quarter, RESP_ROWS), :] = resp


def add_core(kept, got):
    quarter = (kept.shape[0] - RESP_ROWS) // 4
    return small_call(add_core_kernel, "add_core", floats(4, quarter + RESP_ROWS, LANES))(kept, got)


def add_near_kernel(parts_ref, out_ref):
    out_ref[...] = (parts_ref[0] + parts_ref[1]) + (parts_ref[2] + parts_ref[3])


def add_kernel(kept_ref, got_ref, out_ref):
    out_ref[...] = kept_ref[...] + got_ref[...]


def add(name, kept, got):
    return small_call(add_kernel, name, floats(*kept.shape))(kept, got)


def finish_kernel(kept_ref, got_ref, packed_ref, resp_ref):
    rows = packed_ref.shape[0]
    packed_ref[...] = kept_ref[pl.ds(0, rows), :] + got_ref[pl.ds(0, rows), :]
    tail = pl.ds(rows, RESP_ROWS)
    resp = kept_ref[tail, :] + got_ref[tail, :]
    real = resp[: RESP_ROWS // 2]
    imag = resp[RESP_ROWS // 2 :]
    power = real * real + imag * imag
    lane = lax.broadcasted_iota(jnp.int32, power.shape, 1)
    mean = jnp.zeros(power.shape, jnp.float32)
    for q in range(PACK):
        mine = lane // NB == q
        part = jnp.sum(jnp.where(mine, power, 0.0), axis=1, keepdims=True) / NB
        mean = jnp.where(mine, part, mean)
    scaling = 1.0 / jnp.sqrt(mean + 1e-06)
    resp_ref[pl.ds(0, RESP_ROWS // 2), :] = real * scaling
    resp_ref[pl.ds(RESP_ROWS // 2, RESP_ROWS // 2), :] = imag * scaling


def finish(kept, got):
    rows = kept.shape[0] - RESP_ROWS
    return small_call(finish_kernel, "finish", (floats(rows, LANES), floats(RESP_ROWS, LANES)))(
        kept, got
    )


def join_y_kernel(own_ref, got_ref, packed_ref):
    rows = own_ref.shape[0]
    for m, ref in enumerate((own_ref, got_ref)):
        packed_ref[pl.ds((y_bit() ^ m) * rows, rows), :] = ref[...]


def unpack_kernel(part_index, *refs):
    part_ref, out_hbm, full_ref, sem = refs[-4:]
    half = NB // 2
    count = part_ref.shape[0] // half
    for first in range(0, count, 2 * PACK):
        last = min(first + 2 * PACK, count)
        pairs = [part_ref[pl.ds(i * half, half), :] for i in range(first, last)]
        squares = [pair_square(*pairs[i : i + 2]) for i in range(0, len(pairs), 2)]
        for g, both in enumerate(hermitian(squares)):
            for q in range(PACK):
                freq = 2 * first + PACK * g + q
                for c in range(2):
                    full_ref[freq, c] = both[c][:, q * NB : (q + 1) * NB]
    start = 0 if part_index is None else (core_bit() ^ part_index) * 2 * count
    copy = pltpu.make_async_copy(full_ref, out_hbm.at[pl.ds(start, 2 * count)], sem)
    copy.start()
    copy.wait()


def unpack_gram(part, part_index=None, done=None):
    count = part.shape[0] * 4 // NB
    total = count if part_index is None else 2 * count
    any_space = pl.BlockSpec(memory_space=pl.ANY)
    before = () if done is None else (done,)
    return pl.pallas_call(
        functools.partial(unpack_kernel, part_index),
        out_shape=floats(total, 2, NB, NB),
        in_specs=[any_space] * len(before) + [VMEM],
        out_specs=any_space,
        scratch_shapes=[
            pltpu.VMEM((count, 2, NB, NB), jnp.float32),
            pltpu.SemaphoreType.DMA(()),
        ],
        input_output_aliases={0: 0} if before else {},
        compiler_params=pltpu.CompilerParams(vmem_limit_bytes=UNPACK_LIMIT),
        name="unpack_own" if part_index == 0 else "unpack_other",
    )(*before, part)


def modes_kernel(
    total_rows,
    slot,
    high_ref,
    low_hbm,
    rest_ref,
    w_ref,
    table_ref,
    resp_ref,
    out_ref,
    low_ref,
    a_ref,
    sems,
):
    padded, cols = high_ref.shape
    pieces = sems.shape[0]
    fetches = []
    for i in range(pieces):
        first = padded // LANES * i // pieces * LANES
        last = padded // LANES * (i + 1) // pieces * LANES
        rows = pl.ds(first, last - first)
        fetches.append(pltpu.make_async_copy(low_hbm.at[rows], low_ref.at[rows], sems.at[i]))
    for fetch in fetches:
        fetch.start()
    all_groups = RESP_ROWS // 2
    groups = all_groups if slot is None else all_groups // 2
    start = 0 if slot is None else (lax.axis_index("freq") ^ slot) * groups
    count = 2 * groups
    total = PACK * count
    leaks = window_leaks()
    corrections = []
    row = lax.broadcasted_iota(jnp.int32, (count, 1), 0)
    lane = lax.broadcasted_iota(jnp.int32, (count, LANES), 1)
    left = lane < HALF
    parts = [pl.ds(part * all_groups + start, groups) for part in range(2)]
    resp_all = jnp.concatenate([resp_ref[rows, :] for rows in parts], axis=0)
    for q in range(PACK):
        resp = pltpu.roll(resp_all, LANES - q * NB, 1) if q else resp_all
        if q < len(leaks):
            sums = jnp.sum(jnp.where(lane < NB, resp, 0.0), axis=1, keepdims=True) * leaks[q]
            sums = jnp.where(row % groups + start == 0, sums, 0.0)
            corrections.append(sums * rest_ref[pl.ds(0, 1), :])
        else:
            corrections.append(jnp.zeros((count, cols), jnp.float32))
        real = jnp.concatenate([resp[:groups]] * 2, axis=0)
        imag = jnp.concatenate([resp[groups:]] * 2, axis=0)
        tables = []
        for kind in range(2):
            pieces = [
                table_ref[kind, pl.ds(q * RESP_ROWS + part * all_groups + start, groups), :]
                for part in range(2)
            ]
            tables.append(jnp.concatenate(pieces, axis=0))
        first, second = tables
        first_turned = pltpu.roll(first, HALF, 1)
        second_turned = pltpu.roll(second, HALF, 1)

        def spread(value, block):
            if 0 <= block < NB:
                return jnp.broadcast_to(value[:, block : block + 1], (count, LANES))
            return jnp.zeros((count, LANES), jnp.float32)

        for m in range(padded // LANES):
            value = first_turned * jnp.where(left, spread(real, 2 * m - 1), spread(real, 2 * m + 1))
            value += second_turned * jnp.where(
                left, spread(imag, 2 * m - 1), spread(imag, 2 * m + 1)
            )
            if 2 * m < NB:
                value += first * spread(real, 2 * m) + second * spread(imag, 2 * m)
            high, low = split(value)
            own = pl.ds(m * LANES, LANES)
            a_ref[pl.ds(q * count, count), own] = high
            a_ref[pl.ds(total + q * count, count), own] = low
    both = jnp.dot(a_ref[...], high_ref[...], preferred_element_type=jnp.float32)
    modes = both[:total] + both[total:] - jnp.concatenate(corrections, axis=0)
    for fetch in fetches:
        fetch.wait()
    modes += jnp.dot(a_ref[pl.ds(0, total), :], low_ref[...], preferred_element_type=jnp.float32)
    modes = modes * jnp.sqrt(2.0 * total_rows / load_weights(w_ref, cols // LANES))
    for q in range(PACK):
        for part in range(2):
            rows = q * count + part * groups
            for c in range(cols // LANES):
                out_ref[2 * c + part, pl.ds(q, groups, stride=PACK), :] = modes[
                    rows : rows + groups, c * LANES : (c + 1) * LANES
                ]


def local_modes(high, low, rest, weight_rows, response, total_rows, slot):
    padded, cols = high.shape
    count = NF if slot is None else NF // 2
    return pl.pallas_call(
        functools.partial(modes_kernel, total_rows, slot),
        out_shape=floats(2 * cols // LANES, count, LANES),
        in_specs=[VMEM, pl.BlockSpec(memory_space=pl.ANY)] + [VMEM] * 4,
        out_specs=VMEM,
        scratch_shapes=[
            pltpu.VMEM((padded, cols), jnp.bfloat16),
            pltpu.VMEM((4 * count, padded), jnp.bfloat16),
            pltpu.SemaphoreType.DMA((4,)),
        ],
        compiler_params=pltpu.CompilerParams(vmem_limit_bytes=VMEM_LIMIT),
        cost_estimate=pl.CostEstimate(
            flops=2_000_000_000, bytes_accessed=6_000_000, transcendentals=0
        ),
        name="own_modes" if slot == 0 else "sent_modes",
    )(high, low, rest, weight_rows, jnp.asarray(mode_tables()), response)


def join_kernel(kept_ref, got_ref, out_ref):
    tiles = got_ref.shape[0] // 2
    group = lax.axis_index("freq")
    for slot, ref in enumerate((kept_ref, got_ref)):
        for c in range(tiles):
            lanes = pl.ds(pl.multiple_of(((group ^ slot) * tiles + c) * LANES, LANES), LANES)
            for part in range(2):
                out_ref[:, part, lanes] = ref[2 * c + part]


def join_modes(kept, got):
    tiles, count, _ = got.shape
    return small_call(join_kernel, "join_modes", floats(count, 2, tiles * LANES))(kept, got)


def response_of(gram, start_vec):
    matvec = functools.partial(jnp.einsum, "fjk,fk->fj", precision=lax.Precision.HIGHEST)
    resp_real = matvec(gram[:, 0], start_vec[:, 0]) - matvec(gram[:, 1], start_vec[:, 1])
    resp_imag = matvec(gram[:, 0], start_vec[:, 1]) + matvec(gram[:, 1], start_vec[:, 0])
    scaling = 1.0 / jnp.sqrt(
        jnp.mean(resp_real * resp_real + resp_imag * resp_imag, axis=1, keepdims=True) + 1e-06
    )
    return jnp.stack([resp_real * scaling, resp_imag * scaling], axis=1)


def direction_shards(n_devices, snapshots, weight, start_vec):
    def swap(value, mask):
        return lax.ppermute(value, ("pts", "freq"), [(i, i ^ mask) for i in range(n_devices)])

    x, core, y, z_near, z_far = 1, 2, 4, 8, 16
    near = [
        [first + far, first + far + x, first + far + y, first + far + y + x]
        for far in range(0, n_devices, z_near)
        for first in (0, core)
    ]
    total_rows = float(weight.shape[0] * 16)
    weight_rows = weight.reshape(-1, LANES)
    places = [
        (i // 8 % 2) * 16 + (i // 4 % 2) * 8 + (i // 16) * 4 + i % 4 for i in range(NF // 2)
    ]
    keep, send, high, rest, low = gram_parts(
        snapshots, weight_rows, start_vec, total_rows, places, True
    )
    parts = add_core(keep, swap(send, core))
    parts = lax.all_to_all(
        parts, ("pts", "freq"), 0, 0, axis_index_groups=near, tiled=True
    )
    part = small_call(add_near_kernel, "add_near", floats(*parts.shape[1:]))(parts)
    part = add("add_z", part, swap(part, z_near))
    packed, response = finish(part, swap(part, z_far))
    other = swap(packed, y)
    modes_args = (high, low, rest, weight_rows, response, total_rows)
    got = swap(local_modes(*modes_args, 1), x)
    kept = local_modes(*modes_args, 0)
    packed = small_call(join_y_kernel, "join_y", floats(2 * packed.shape[0], LANES))(packed, other)
    gram_mine = unpack_gram(packed, 0)
    gram_mine = unpack_gram(swap(packed, core), 1, gram_mine)
    return gram_mine, join_modes(kept, got)


def shards(n_pts, n_freq, snapshots, weight, start_vec):
    cols = snapshots.shape[1]
    total_rows = float(weight.shape[0] * n_pts)
    n_devices = n_pts * n_freq
    mine_count = NF // n_freq
    group = lax.axis_index("freq")
    weight_rows = weight.reshape(-1, LANES)
    places = list(range(NF // 2))
    first, second, high, rest, low = gram_parts(
        snapshots, weight_rows, start_vec, total_rows, places, False
    )
    parts = jnp.concatenate([first[:-RESP_ROWS], second[:-RESP_ROWS]], axis=0)
    share = parts.reshape(n_devices, -1)
    share = jnp.sum(lax.all_to_all(share, ("freq", "pts"), 0, 0, tiled=True), axis=0)
    packed = lax.all_gather(share, "pts", axis=0, tiled=True)
    gram_mine = unpack_gram(packed.reshape(-1, LANES))
    start_mine = lax.dynamic_slice_in_dim(start_vec, group * mine_count, mine_count, 0)
    response = lax.all_gather(response_of(gram_mine, start_mine), "freq", axis=0, tiled=True)
    response = jnp.transpose(response.reshape(NF // PACK, PACK, 2, NB), (2, 0, 1, 3))
    response = response.reshape(RESP_ROWS, LANES)
    modes = local_modes(high, low, rest, weight_rows, response, total_rows, None)
    modes = modes.reshape(-1, n_freq, mine_count, LANES)
    modes = lax.all_to_all(jnp.moveaxis(modes, 1, 0), "freq", 0, 0, tiled=True)
    modes = modes.reshape(n_freq, cols // LANES, 2, mine_count, LANES)
    modes = jnp.transpose(modes, (3, 2, 0, 1, 4)).reshape(mine_count, 2, n_freq * cols)
    return gram_mine, modes


def solution(mesh):
    n_pts, n_freq = mesh.shape["pts"], mesh.shape["freq"]
    if (n_pts, n_freq) == (16, 2):
        body = functools.partial(direction_shards, n_pts * n_freq)
    else:
        body = functools.partial(shards, n_pts, n_freq)
    placed = (P(None, ("pts", "freq")), P("pts"), P())
    return jax.shard_map(
        body,
        mesh=mesh,
        in_specs=placed,
        out_specs=(P("freq", None, None, None), P("freq", None, "pts")),
        check_vma=False,
    )
```

```python
import functools
import math

import jax
import jax.numpy as jnp
import numpy as np
from jax import lax
from jax.experimental import pallas as pl
from jax.experimental.pallas import tpu as pltpu
from jax.sharding import PartitionSpec as P

NFFT = 128
HALF = NFFT // 2
NF = 64
NB = 32
LANES = 128
PACK = 4
VMEM_LIMIT = 51 * 1024 * 1024
SMALL_LIMIT = 8 * 1024 * 1024
MODES_LIMIT = 24 * 1024 * 1024
VMEM = pl.BlockSpec(memory_space=pltpu.VMEM)


def dft_values():
    times = np.arange(NFFT)
    freqs = np.arange(NF)
    phases = (freqs[:, None] * times[None, :] % NFFT) * (2.0 * math.pi / NFFT)
    window = 0.5 - 0.5 * np.cos(times * (2.0 * math.pi / NFFT))
    weighted = window / np.sqrt(np.sum(window * window))
    return np.cos(phases) * weighted, -np.sin(phases) * weighted


def split_table(table):
    high = table.astype(jnp.bfloat16)
    low = (table - high.astype(np.float64)).astype(jnp.bfloat16)
    return high, low


def window_leaks():
    real, _ = dft_values()
    return [float(np.sum(real[k])) for k in range(2)]


def mode_tables():
    real, imag = dft_values()
    order = np.arange(NF).reshape(NF // PACK, PACK).T
    real, imag = real[order], imag[order]
    first = np.stack([real, imag], axis=1).reshape(2 * NF, NFFT)
    second = np.stack([-imag, real], axis=1).reshape(2 * NF, NFFT)
    return np.stack([first, second]).astype(np.float32)


def cosine_of_turns(count):
    folded = jnp.minimum(count, NFFT - count)
    angle = (NFFT // 4 - folded).astype(jnp.float32) * (2.0 * math.pi / NFFT)
    square = angle * angle
    series = 1.0
    for n in (10, 8, 6, 4, 2):
        series = 1.0 - square * series * (1.0 / (n * (n + 1)))
    return angle * series


def fill_dft(dft_ref):
    row = lax.broadcasted_iota(jnp.int32, (2 * NF, NFFT), 0)
    time = lax.broadcasted_iota(jnp.int32, (2 * NF, NFFT), 1)
    quarter = jnp.where(row < NF, 0, NFFT // 4)
    wave = cosine_of_turns((row % NF * time + quarter) % NFFT)
    window = 0.5 - 0.5 * np.cos(np.arange(NFFT) * (2.0 * math.pi / NFFT))
    norm = float(np.sqrt(np.sum(window * window)))
    high, low = split(wave * ((0.5 - 0.5 * cosine_of_turns(time)) / norm))
    dft_ref[pl.ds(0, 2 * NF), pl.ds(0, NFFT)] = high
    dft_ref[pl.ds(0, 2 * NF), pl.ds(NFFT, NFFT)] = high
    dft_ref[pl.ds(2 * NF, 2 * NF), pl.ds(0, NFFT)] = low
    dft_ref[pl.ds(2 * NF, 2 * NF), pl.ds(NFFT, NFFT)] = jnp.zeros((2 * NF, NFFT), jnp.bfloat16)


def spread_start(start_ref, spread_ref):
    row = lax.broadcasted_iota(jnp.int32, (NF, LANES), 0)
    lane = lax.broadcasted_iota(jnp.int32, (NF, LANES), 1)
    start = start_ref[pl.ds(0, 2 * NB), pl.ds(0, NF)]
    for g in range(NF // PACK):
        pick = (row == PACK * g + lane // NB).astype(jnp.float32)
        spread_ref[g] = jnp.dot(
            start,
            pick,
            precision=lax.Precision.HIGHEST,
            preferred_element_type=jnp.float32,
        )


def split(value):
    high = value.astype(jnp.bfloat16)
    low = (value - high.astype(jnp.float32)).astype(jnp.bfloat16)
    return high, low


def load_weights(w_ref, col_tiles):
    first = lax.axis_index("freq") * col_tiles
    return jnp.concatenate([w_ref[pl.ds(first + c, 1), :] for c in range(col_tiles)], axis=1)


def flip_groups(groups, flipped):
    turned = flipped.T
    lane = lax.broadcasted_iota(jnp.int32, (NB, LANES), 1)
    out = []
    for g in range(PACK):
        total = groups[g]
        for q in range(PACK):
            block = turned[q * NB : (q + 1) * NB]
            if q != g:
                block = pltpu.roll(block, ((q - g) % PACK) * NB, 1)
            total = total + jnp.where(lane // NB == q, block, 0.0)
        out.append(total)
    return out


TILE = 8


def turn_tiles(tiles):
    row = lax.broadcasted_iota(jnp.int32, (TILE, LANES), 0)
    step = TILE // 2
    while step:
        keep = row % (2 * step) < step
        turned = list(tiles)
        for i in range(TILE):
            if i % (2 * step) < step:
                low, high = tiles[i], tiles[i + step]
                turned[i] = jnp.where(keep, low, pltpu.roll(high, step, 0))
                turned[i + step] = jnp.where(keep, pltpu.roll(low, TILE - step, 0), high)
        tiles = turned
        step //= 2
    return tiles


def core_bit():
    return lax.rem(lax.axis_index("pts"), 2)


def y_bit():
    return lax.rem(lax.div(lax.axis_index("pts"), 2), 2)


RESP_ROWS = 2 * NF // PACK


def give_half(value_ref, bit, keep_ref, send_ref):
    half = keep_ref.shape[0] - RESP_ROWS
    keep_ref[pl.ds(0, half), :] = value_ref[pl.ds(bit * half, half), :]
    send_ref[pl.ds(0, half), :] = value_ref[pl.ds((1 - bit) * half, half), :]
    resp = value_ref[pl.ds(2 * half, RESP_ROWS), :]
    keep_ref[pl.ds(half, RESP_ROWS), :] = resp
    send_ref[pl.ds(half, RESP_ROWS), :] = resp


def gram_kernel(
    total_rows,
    places,
    by_core,
    x_hbm,
    aux_ref,
    keep_ref,
    send_ref,
    high_ref,
    rest_ref,
    low_hbm,
    x_ref,
    dft_ref,
    low_ref,
    block_even,
    block_odd,
    spec_ref,
    z_even,
    z_odd,
    real_ref,
    imag_ref,
    spread_ref,
    pack_ref,
    in_sems,
    out_sem,
):
    times, cols = x_ref.shape
    col_tiles = cols // LANES
    block_refs = (block_even, block_odd)
    cuts = [0] + [(first + TILE + 1) * HALF for first in range(0, NB, TILE)]

    def fetches(i):
        middle = (cuts[i] + cuts[i + 1]) // (2 * HALF) * HALF
        for n, (first, last) in enumerate(((cuts[i], middle), (middle, cuts[i + 1]))):
            rows = pl.ds(first, last - first)
            yield pltpu.make_async_copy(x_hbm.at[rows], x_ref.at[rows], in_sems.at[2 * i + n])

    for i in range(len(cuts) - 1):
        for fetch in fetches(i):
            fetch.start()
    fill_dft(dft_ref)
    spread_start(aux_ref, spread_ref)
    weights = load_weights(aux_ref.at[pl.ds(2 * NB, aux_ref.shape[0] - 2 * NB)], col_tiles)
    scale = jnp.sqrt(weights / (2.0 * total_rows))
    for fetch in fetches(0):
        fetch.wait()
    first_mean = jnp.mean(x_ref[pl.ds(0, NFFT), :], axis=0, keepdims=True)

    def center(i, acc):
        def step(h, acc):
            rows = pl.ds(pl.multiple_of(h * HALF, HALF), HALF)
            value = x_ref[rows, :] - first_mean
            high, low = split(value * scale)
            high_ref[rows, :] = high
            low_ref[rows, :] = low
            return acc + value

        return lax.fori_loop(cuts[i] // HALF, cuts[i + 1] // HALF, step, acc, unroll=True)

    def transform(first):
        for i in range(TILE // 2):
            blocks = []
            for s in range(2):
                rows = pl.ds((first + 2 * i + s) * HALF, NFFT)
                blocks.append(jnp.concatenate([high_ref[rows, :], low_ref[rows, :]], axis=0))
            both = jnp.dot(
                dft_ref[...], jnp.concatenate(blocks, axis=1), preferred_element_type=jnp.float32
            )
            spectrum = both[: 2 * NF] + both[2 * NF :]
            for s in range(2):
                block_refs[first // TILE % 2][2 * i + s] = spectrum[:, s * cols : (s + 1) * cols]

    def arrange(first):
        block_ref = block_refs[first // TILE % 2]
        for c in range(col_tiles):
            lanes = pl.ds(c * LANES, LANES)
            for o in range(2 * NF // TILE):
                rows = pl.ds(o * TILE, TILE)
                tiles = turn_tiles([block_ref[b, rows, lanes] for b in range(TILE)])
                for k in range(TILE):
                    spec_ref[c, o * TILE + k, pl.ds(first, TILE), :] = tiles[k]

    acc = center(0, jnp.zeros((HALF, cols), jnp.float32))
    transform(0)
    for first in range(0, NB, TILE):
        if first + TILE < NB:
            for fetch in fetches(first // TILE + 1):
                fetch.wait()
            acc = center(first // TILE + 1, acc)
            transform(first + TILE)
        arrange(first)
    pad = high_ref.shape[0] - times
    if pad:
        high_ref[pl.ds(times, pad), :] = jnp.zeros((pad, cols), jnp.bfloat16)
        low_ref[pl.ds(times, pad), :] = jnp.zeros((pad, cols), jnp.bfloat16)
    save_low = pltpu.make_async_copy(low_ref, low_hbm, out_sem)
    save_low.start()
    rest = jnp.sum(acc, axis=0, keepdims=True) / times * scale
    rest_ref[...] = jnp.broadcast_to(rest, rest_ref.shape)
    for k, leak in enumerate(window_leaks()):
        for c in range(col_tiles):
            part = rest[:, c * LANES : (c + 1) * LANES]
            spec_ref[c, k] = spec_ref[c, k] - leak * part

    row = lax.broadcasted_iota(jnp.int32, (NB, LANES), 0)
    lane = lax.broadcasted_iota(jnp.int32, (NB, LANES), 1)
    upper = row <= lane % NB
    octets = NF // 8

    def prepare(z_ref, octet, half):
        for part in range(2):
            for q in range(PACK):
                own = pl.ds(part * LANES + q * NB, NB)
                for c in range(col_tiles):
                    value = spec_ref[c, NF * part + TILE * octet + PACK * half + q]
                    high = value.astype(jnp.bfloat16)
                    low = (2.0 * (value - high.astype(jnp.float32))).astype(jnp.bfloat16)
                    z_ref[own, pl.ds(c * LANES, LANES)] = high
                    z_ref[own, pl.ds(cols + c * LANES, LANES)] = low

    def correlate(z_ref, group):
        high = z_ref[:, pl.ds(0, cols)]
        product = lax.dot_general(
            jnp.concatenate([high, high], axis=1),
            z_ref[...],
            (((1,), (1,)), ((), ())),
            preferred_element_type=jnp.float32,
        )
        gram_real = jnp.zeros((NB, LANES), jnp.float32)
        gram_imag = jnp.zeros((NB, LANES), jnp.float32)
        for q in range(PACK):
            mine = lane // NB == q
            real = product[q * NB : (q + 1) * NB]
            imag = product[LANES + q * NB : LANES + (q + 1) * NB]
            gram_real = jnp.where(mine, real[:, :LANES] + imag[:, LANES:], gram_real)
            gram_imag = jnp.where(mine, real[:, LANES:] - imag[:, :LANES], gram_imag)
        real_ref[group] = gram_real
        imag_ref[group] = gram_imag

    left = lane[: NB // 2] < LANES // 2
    half = NB // 2
    resp_real = []
    resp_imag = []

    def finish_quad(quad):
        own = pl.ds(quad * PACK, PACK)
        reals = [real_ref[quad * PACK + g] for g in range(PACK)]
        imags = [imag_ref[quad * PACK + g] for g in range(PACK)]
        reals = flip_groups(reals, real_ref[own].reshape(PACK * NB, LANES))
        imags = flip_groups(imags, -imag_ref[own].reshape(PACK * NB, LANES))
        for g, (real, imag) in enumerate(zip(reals, imags)):
            group = quad * PACK + g
            start_real = spread_ref[group, pl.ds(0, NB), :]
            start_imag = spread_ref[group, pl.ds(NB, NB), :]
            resp_real.append(
                jnp.sum(real * start_real + imag * start_imag, axis=0, keepdims=True)
            )
            resp_imag.append(
                jnp.sum(real * start_imag - imag * start_real, axis=0, keepdims=True)
            )
            packed = jnp.where(upper, real, imag)
            top = packed[:half]
            bottom = packed[half:]
            even = jnp.where(left, top, pltpu.roll(bottom, LANES // 2, 1))
            odd = jnp.where(left, pltpu.roll(top, LANES // 2, 1), bottom)
            pack_ref[pl.ds(places[2 * group] * half, half), :] = even
            pack_ref[pl.ds(places[2 * group + 1] * half, half), :] = odd

    z_refs = (z_even, z_odd)
    groups = NF // PACK
    prepare(z_even, 0, 0)
    for group in range(groups):
        if group + 1 < groups:
            prepare(z_refs[(group + 1) % 2], (group + 1) // 2, (group + 1) % 2)
        correlate(z_refs[group % 2], group)
        if group % PACK == PACK - 1:
            finish_quad(group // PACK)
    resp = jnp.concatenate(resp_real + resp_imag, axis=0)
    pack_ref[pl.ds(NF // 2 * half, RESP_ROWS), :] = resp
    give_half(pack_ref, core_bit() if by_core else 0, keep_ref, send_ref)
    save_low.wait()


def gram_parts(snapshots, weight_rows, start_vec, total_rows, places, by_core):
    times, cols = snapshots.shape
    start = jnp.transpose(start_vec, (1, 2, 0)).reshape(2 * NB, NF)
    start = jnp.pad(start, ((0, 0), (0, LANES - NF)))
    aux = jnp.concatenate([start, weight_rows], axis=0)
    any_space = pl.BlockSpec(memory_space=pl.ANY)
    saved = jax.ShapeDtypeStruct((-(-times // LANES) * LANES, cols), jnp.bfloat16)
    half = floats(NF // 4 * NB // 2 + RESP_ROWS, LANES)
    return pl.pallas_call(
        functools.partial(gram_kernel, total_rows, places, by_core),
        out_shape=(half, half, saved, floats(8, cols), saved),
        in_specs=[any_space, VMEM],
        out_specs=(VMEM, VMEM, VMEM, VMEM, any_space),
        scratch_shapes=[
            pltpu.VMEM((times, cols), jnp.float32),
            pltpu.VMEM((4 * NF, 2 * NFFT), jnp.bfloat16),
            pltpu.VMEM(saved.shape, jnp.bfloat16),
            pltpu.VMEM((TILE, 2 * NF, cols), jnp.float32),
            pltpu.VMEM((TILE, 2 * NF, cols), jnp.float32),
            pltpu.VMEM((cols // LANES, 2 * NF, NB, LANES), jnp.float32),
            pltpu.VMEM((2 * LANES, 2 * cols), jnp.bfloat16),
            pltpu.VMEM((2 * LANES, 2 * cols), jnp.bfloat16),
            pltpu.VMEM((NF // PACK, NB, LANES), jnp.float32),
            pltpu.VMEM((NF // PACK, NB, LANES), jnp.float32),
            pltpu.VMEM((NF // PACK, 2 * NB, LANES), jnp.float32),
            pltpu.VMEM((NF // 2 * NB // 2 + RESP_ROWS, LANES), jnp.float32),
            pltpu.SemaphoreType.DMA((2 * NB // TILE,)),
            pltpu.SemaphoreType.DMA(()),
        ],
        compiler_params=pltpu.CompilerParams(vmem_limit_bytes=VMEM_LIMIT),
        cost_estimate=pl.CostEstimate(
            flops=5_000_000_000, bytes_accessed=8_000_000, transcendentals=0
        ),
        name="gram_parts",
    )(snapshots, aux)


def pair_square(even, odd):
    left = lax.broadcasted_iota(jnp.int32, (NB // 2, LANES), 1) < LANES // 2
    top = jnp.where(left, even, pltpu.roll(odd, LANES // 2, 1))
    bottom = jnp.where(left, pltpu.roll(even, LANES // 2, 1), odd)
    return jnp.concatenate([top, bottom], axis=0)


def hermitian(squares):
    row = lax.broadcasted_iota(jnp.int32, (NB, LANES), 0)
    col = lax.broadcasted_iota(jnp.int32, (NB, LANES), 1) % NB
    zero = jnp.zeros((NB, LANES), jnp.float32)
    full = squares + [zero] * (PACK - len(squares))
    turned = flip_groups([zero] * PACK, jnp.concatenate(full, axis=0))
    for square, flipped in zip(squares, turned):
        real = jnp.where(row <= col, square, flipped)
        imag = jnp.where(row > col, square, jnp.where(row < col, -flipped, 0.0))
        yield real, imag


def small_call(kernel, name, out_shape, scratch_shapes=(), limit=SMALL_LIMIT):
    def call(*args):
        return pl.pallas_call(
            kernel,
            out_shape=out_shape,
            in_specs=[VMEM] * len(args),
            out_specs=VMEM if isinstance(out_shape, jax.ShapeDtypeStruct) else (VMEM,) * len(out_shape),
            scratch_shapes=list(scratch_shapes),
            compiler_params=pltpu.CompilerParams(vmem_limit_bytes=limit),
            name=name,
        )(*args)

    return call


def floats(*shape):
    return jax.ShapeDtypeStruct(shape, jnp.float32)


def add_core_kernel(kept_ref, got_ref, out_ref):
    quarter = out_ref.shape[1] - RESP_ROWS
    tail = pl.ds(4 * quarter, RESP_ROWS)
    resp = kept_ref[tail, :] + got_ref[tail, :]
    for m in range(4):
        rows = pl.ds(m * quarter, quarter)
        out_ref[m, pl.ds(0, quarter), :] = kept_ref[rows, :] + got_ref[rows, :]
        out_ref[m, pl.ds(quarter, RESP_ROWS), :] = resp


def add_core(kept, got):
    quarter = (kept.shape[0] - RESP_ROWS) // 4
    return small_call(add_core_kernel, "add_core", floats(4, quarter + RESP_ROWS, LANES))(kept, got)


def add_near_kernel(parts_ref, out_ref):
    out_ref[...] = (parts_ref[0] + parts_ref[1]) + (parts_ref[2] + parts_ref[3])


def add_kernel(kept_ref, got_ref, out_ref):
    out_ref[...] = kept_ref[...] + got_ref[...]


def add(name, kept, got):
    return small_call(add_kernel, name, floats(*kept.shape))(kept, got)


def finish_kernel(kept_ref, got_ref, packed_ref, resp_ref):
    rows = packed_ref.shape[0]
    packed_ref[...] = kept_ref[pl.ds(0, rows), :] + got_ref[pl.ds(0, rows), :]
    tail = pl.ds(rows, RESP_ROWS)
    resp = kept_ref[tail, :] + got_ref[tail, :]
    real = resp[: RESP_ROWS // 2]
    imag = resp[RESP_ROWS // 2 :]
    power = real * real + imag * imag
    lane = lax.broadcasted_iota(jnp.int32, power.shape, 1)
    mean = jnp.zeros(power.shape, jnp.float32)
    for q in range(PACK):
        mine = lane // NB == q
        part = jnp.sum(jnp.where(mine, power, 0.0), axis=1, keepdims=True) / NB
        mean = jnp.where(mine, part, mean)
    scaling = 1.0 / jnp.sqrt(mean + 1e-06)
    resp_ref[pl.ds(0, RESP_ROWS // 2), :] = real * scaling
    resp_ref[pl.ds(RESP_ROWS // 2, RESP_ROWS // 2), :] = imag * scaling


def finish(kept, got):
    rows = kept.shape[0] - RESP_ROWS
    return small_call(finish_kernel, "finish", (floats(rows, LANES), floats(RESP_ROWS, LANES)))(
        kept, got
    )


def join_y_kernel(own_ref, got_ref, packed_ref):
    rows = own_ref.shape[0]
    for m, ref in enumerate((own_ref, got_ref)):
        packed_ref[pl.ds((y_bit() ^ m) * rows, rows), :] = ref[...]


def unpack_kernel(*refs):
    parts, out_ref = refs[:-1], refs[-1]
    half = NB // 2
    for m, part in enumerate(parts):
        count = part.shape[0] // half
        place = (core_bit() ^ m) * 2 * count if len(parts) > 1 else 0
        for first in range(0, count, 2 * PACK):
            last = min(first + 2 * PACK, count)
            pairs = [part[pl.ds(i * half, half), :] for i in range(first, last)]
            squares = [pair_square(*pairs[i : i + 2]) for i in range(0, len(pairs), 2)]
            for g, both in enumerate(hermitian(squares)):
                for q in range(PACK):
                    freq = place + 2 * first + PACK * g + q
                    for c in range(2):
                        out_ref[freq, c] = both[c][:, q * NB : (q + 1) * NB]


def unpack_gram(*parts):
    count = sum(part.shape[0] for part in parts) * 4 // NB
    return small_call(unpack_kernel, "unpack_gram", floats(count, 2, NB, NB))(*parts)


def hand_on_kernel(low_hbm, after_ref, out_ref, token_ref, sem):
    copy = pltpu.make_async_copy(low_hbm, out_ref, sem)
    copy.start()
    token_ref[...] = after_ref[pl.ds(0, TILE), :]
    copy.wait()


def hand_on(low, after):
    return pl.pallas_call(
        hand_on_kernel,
        out_shape=(jax.ShapeDtypeStruct(low.shape, low.dtype), floats(TILE, LANES)),
        in_specs=[pl.BlockSpec(memory_space=pl.ANY), VMEM],
        out_specs=(VMEM, VMEM),
        scratch_shapes=[pltpu.SemaphoreType.DMA(())],
        compiler_params=pltpu.CompilerParams(vmem_limit_bytes=SMALL_LIMIT),
        name="hand_on",
    )(low, after)


def modes_kernel(
    total_rows,
    slot,
    high_ref,
    low_ref,
    rest_ref,
    w_ref,
    table_ref,
    resp_ref,
    out_ref,
    a_ref,
):
    cols = high_ref.shape[1]
    padded = high_ref.shape[0]
    all_groups = RESP_ROWS // 2
    groups = all_groups if slot is None else all_groups // 2
    start = 0 if slot is None else (lax.axis_index("freq") ^ slot) * groups
    count = 2 * groups
    total = PACK * count
    leaks = window_leaks()
    corrections = []
    row = lax.broadcasted_iota(jnp.int32, (count, 1), 0)
    lane = lax.broadcasted_iota(jnp.int32, (count, LANES), 1)
    left = lane < HALF
    parts = [pl.ds(part * all_groups + start, groups) for part in range(2)]
    resp_all = jnp.concatenate([resp_ref[rows, :] for rows in parts], axis=0)
    for q in range(PACK):
        resp = pltpu.roll(resp_all, LANES - q * NB, 1) if q else resp_all
        if q < len(leaks):
            sums = jnp.sum(jnp.where(lane < NB, resp, 0.0), axis=1, keepdims=True) * leaks[q]
            sums = jnp.where(row % groups + start == 0, sums, 0.0)
            corrections.append(sums * rest_ref[pl.ds(0, 1), :])
        else:
            corrections.append(jnp.zeros((count, cols), jnp.float32))
        real = jnp.concatenate([resp[:groups]] * 2, axis=0)
        imag = jnp.concatenate([resp[groups:]] * 2, axis=0)
        tables = []
        for kind in range(2):
            pieces = [
                table_ref[kind, pl.ds(q * RESP_ROWS + part * all_groups + start, groups), :]
                for part in range(2)
            ]
            tables.append(jnp.concatenate(pieces, axis=0))
        first, second = tables
        first_turned = pltpu.roll(first, HALF, 1)
        second_turned = pltpu.roll(second, HALF, 1)

        def spread(value, block):
            if 0 <= block < NB:
                return jnp.broadcast_to(value[:, block : block + 1], (count, LANES))
            return jnp.zeros((count, LANES), jnp.float32)

        for m in range(padded // LANES):
            value = first_turned * jnp.where(left, spread(real, 2 * m - 1), spread(real, 2 * m + 1))
            value += second_turned * jnp.where(
                left, spread(imag, 2 * m - 1), spread(imag, 2 * m + 1)
            )
            if 2 * m < NB:
                value += first * spread(real, 2 * m) + second * spread(imag, 2 * m)
            high, low = split(value)
            own = pl.ds(m * LANES, LANES)
            a_ref[pl.ds(q * count, count), own] = high
            a_ref[pl.ds(total + q * count, count), own] = low
    both = jnp.dot(a_ref[...], high_ref[...], preferred_element_type=jnp.float32)
    modes = both[:total] + both[total:] - jnp.concatenate(corrections, axis=0)
    modes += jnp.dot(a_ref[pl.ds(0, total), :], low_ref[...], preferred_element_type=jnp.float32)
    modes = modes * jnp.sqrt(2.0 * total_rows / load_weights(w_ref, cols // LANES))
    for q in range(PACK):
        for part in range(2):
            rows = q * count + part * groups
            for c in range(cols // LANES):
                out_ref[2 * c + part, pl.ds(q, groups, stride=PACK), :] = modes[
                    rows : rows + groups, c * LANES : (c + 1) * LANES
                ]


def local_modes(high, low, rest, weight_rows, response, total_rows, slot):
    padded, cols = high.shape
    count = NF if slot is None else NF // 2
    return pl.pallas_call(
        functools.partial(modes_kernel, total_rows, slot),
        out_shape=floats(2 * cols // LANES, count, LANES),
        in_specs=[VMEM] * 6,
        out_specs=VMEM,
        scratch_shapes=[pltpu.VMEM((4 * count, padded), jnp.bfloat16)],
        compiler_params=pltpu.CompilerParams(vmem_limit_bytes=MODES_LIMIT),
        cost_estimate=pl.CostEstimate(
            flops=2_000_000_000, bytes_accessed=6_000_000, transcendentals=0
        ),
        name="own_modes" if slot == 0 else "sent_modes",
    )(high, low, rest, weight_rows, jnp.asarray(mode_tables()), response)


def join_kernel(kept_ref, got_ref, out_ref):
    tiles = got_ref.shape[0] // 2
    group = lax.axis_index("freq")
    for slot, ref in enumerate((kept_ref, got_ref)):
        for c in range(tiles):
            lanes = pl.ds(pl.multiple_of(((group ^ slot) * tiles + c) * LANES, LANES), LANES)
            for part in range(2):
                out_ref[:, part, lanes] = ref[2 * c + part]


def join_modes(kept, got):
    tiles, count, _ = got.shape
    return small_call(join_kernel, "join_modes", floats(count, 2, tiles * LANES))(kept, got)


def response_of(gram, start_vec):
    matvec = functools.partial(jnp.einsum, "fjk,fk->fj", precision=lax.Precision.HIGHEST)
    resp_real = matvec(gram[:, 0], start_vec[:, 0]) - matvec(gram[:, 1], start_vec[:, 1])
    resp_imag = matvec(gram[:, 0], start_vec[:, 1]) + matvec(gram[:, 1], start_vec[:, 0])
    scaling = 1.0 / jnp.sqrt(
        jnp.mean(resp_real * resp_real + resp_imag * resp_imag, axis=1, keepdims=True) + 1e-06
    )
    return jnp.stack([resp_real * scaling, resp_imag * scaling], axis=1)


def direction_shards(n_devices, snapshots, weight, start_vec):
    def swap(value, mask):
        return lax.ppermute(value, ("pts", "freq"), [(i, i ^ mask) for i in range(n_devices)])

    x, core, y, z_near, z_far = 1, 2, 4, 8, 16
    near = [
        [first + far, first + far + x, first + far + y, first + far + y + x]
        for far in range(0, n_devices, z_near)
        for first in (0, core)
    ]
    total_rows = float(weight.shape[0] * 16)
    weight_rows = weight.reshape(-1, LANES)
    places = [
        (i // 8 % 2) * 16 + (i // 4 % 2) * 8 + (i // 16) * 4 + i % 4 for i in range(NF // 2)
    ]
    keep, send, high, rest, low = gram_parts(
        snapshots, weight_rows, start_vec, total_rows, places, True
    )
    parts = add_core(keep, swap(send, core))
    parts = lax.all_to_all(
        parts, ("pts", "freq"), 0, 0, axis_index_groups=near, tiled=True
    )
    part = small_call(add_near_kernel, "add_near", floats(*parts.shape[1:]))(parts)
    part = add("add_z", part, swap(part, z_near))
    got = swap(part, z_far)
    low, token = hand_on(low, part)
    got, token = lax.optimization_barrier((got, token))
    packed, response = finish(part, got)
    other = swap(packed, y)
    modes_args = (high, low, rest, weight_rows, response, total_rows)
    got = swap(local_modes(*modes_args, 1), x)
    kept = local_modes(*modes_args, 0)
    packed = small_call(join_y_kernel, "join_y", floats(2 * packed.shape[0], LANES))(packed, other)
    gram_mine = unpack_gram(packed, swap(packed, core))
    return gram_mine, join_modes(kept, got)


def shards(n_pts, n_freq, snapshots, weight, start_vec):
    cols = snapshots.shape[1]
    total_rows = float(weight.shape[0] * n_pts)
    n_devices = n_pts * n_freq
    mine_count = NF // n_freq
    group = lax.axis_index("freq")
    weight_rows = weight.reshape(-1, LANES)
    places = list(range(NF // 2))
    first, second, high, rest, low = gram_parts(
        snapshots, weight_rows, start_vec, total_rows, places, False
    )
    parts = jnp.concatenate([first[:-RESP_ROWS], second[:-RESP_ROWS]], axis=0)
    share = parts.reshape(n_devices, -1)
    share = jnp.sum(lax.all_to_all(share, ("freq", "pts"), 0, 0, tiled=True), axis=0)
    packed = lax.all_gather(share, "pts", axis=0, tiled=True)
    gram_mine = unpack_gram(packed.reshape(-1, LANES))
    start_mine = lax.dynamic_slice_in_dim(start_vec, group * mine_count, mine_count, 0)
    response = lax.all_gather(response_of(gram_mine, start_mine), "freq", axis=0, tiled=True)
    response = jnp.transpose(response.reshape(NF // PACK, PACK, 2, NB), (2, 0, 1, 3))
    response = response.reshape(RESP_ROWS, LANES)
    modes = local_modes(high, low, rest, weight_rows, response, total_rows, None)
    modes = modes.reshape(-1, n_freq, mine_count, LANES)
    modes = lax.all_to_all(jnp.moveaxis(modes, 1, 0), "freq", 0, 0, tiled=True)
    modes = modes.reshape(n_freq, cols // LANES, 2, mine_count, LANES)
    modes = jnp.transpose(modes, (3, 2, 0, 1, 4)).reshape(mine_count, 2, n_freq * cols)
    return gram_mine, modes


def solution(mesh):
    n_pts, n_freq = mesh.shape["pts"], mesh.shape["freq"]
    if (n_pts, n_freq) == (16, 2):
        body = functools.partial(direction_shards, n_pts * n_freq)
    else:
        body = functools.partial(shards, n_pts, n_freq)
    placed = (P(None, ("pts", "freq")), P("pts"), P())
    return jax.shard_map(
        body,
        mesh=mesh,
        in_specs=placed,
        out_specs=(P("freq", None, None, None), P("freq", None, "pts")),
        check_vma=False,
    )
```

```python
import functools
import math

import jax
import jax.numpy as jnp
import numpy as np
from jax import lax
from jax.experimental import pallas as pl
from jax.experimental.pallas import tpu as pltpu
from jax.sharding import PartitionSpec as P

NFFT = 128
HALF = NFFT // 2
NF = 64
NB = 32
LANES = 128
PACK = 4
VMEM_LIMIT = 51 * 1024 * 1024
SMALL_LIMIT = 8 * 1024 * 1024
MODES_LIMIT = 24 * 1024 * 1024
UNPACK_LIMIT = 53 * 1024 * 1024
VMEM = pl.BlockSpec(memory_space=pltpu.VMEM)


def dft_values():
    times = np.arange(NFFT)
    freqs = np.arange(NF)
    phases = (freqs[:, None] * times[None, :] % NFFT) * (2.0 * math.pi / NFFT)
    window = 0.5 - 0.5 * np.cos(times * (2.0 * math.pi / NFFT))
    weighted = window / np.sqrt(np.sum(window * window))
    return np.cos(phases) * weighted, -np.sin(phases) * weighted


def split_table(table):
    high = table.astype(jnp.bfloat16)
    low = (table - high.astype(np.float64)).astype(jnp.bfloat16)
    return high, low


def window_leaks():
    real, _ = dft_values()
    return [float(np.sum(real[k])) for k in range(2)]


def mode_tables():
    real, imag = dft_values()
    order = np.arange(NF).reshape(NF // PACK, PACK).T
    real, imag = real[order], imag[order]
    first = np.stack([real, imag], axis=1).reshape(2 * NF, NFFT)
    second = np.stack([-imag, real], axis=1).reshape(2 * NF, NFFT)
    return np.stack([first, second]).astype(np.float32)


def cosine_of_turns(count):
    folded = jnp.minimum(count, NFFT - count)
    angle = (NFFT // 4 - folded).astype(jnp.float32) * (2.0 * math.pi / NFFT)
    square = angle * angle
    series = 1.0
    for n in (10, 8, 6, 4, 2):
        series = 1.0 - square * series * (1.0 / (n * (n + 1)))
    return angle * series


def fill_dft(dft_ref):
    row = lax.broadcasted_iota(jnp.int32, (2 * NF, NFFT), 0)
    time = lax.broadcasted_iota(jnp.int32, (2 * NF, NFFT), 1)
    quarter = jnp.where(row < NF, 0, NFFT // 4)
    wave = cosine_of_turns((row % NF * time + quarter) % NFFT)
    window = 0.5 - 0.5 * np.cos(np.arange(NFFT) * (2.0 * math.pi / NFFT))
    norm = float(np.sqrt(np.sum(window * window)))
    high, low = split(wave * ((0.5 - 0.5 * cosine_of_turns(time)) / norm))
    dft_ref[pl.ds(0, 2 * NF), pl.ds(0, NFFT)] = high
    dft_ref[pl.ds(0, 2 * NF), pl.ds(NFFT, NFFT)] = high
    dft_ref[pl.ds(2 * NF, 2 * NF), pl.ds(0, NFFT)] = low
    dft_ref[pl.ds(2 * NF, 2 * NF), pl.ds(NFFT, NFFT)] = jnp.zeros((2 * NF, NFFT), jnp.bfloat16)


def spread_start(start_ref, spread_ref):
    row = lax.broadcasted_iota(jnp.int32, (NF, LANES), 0)
    lane = lax.broadcasted_iota(jnp.int32, (NF, LANES), 1)
    start = start_ref[pl.ds(0, 2 * NB), pl.ds(0, NF)]
    for g in range(NF // PACK):
        pick = (row == PACK * g + lane // NB).astype(jnp.float32)
        spread_ref[g] = jnp.dot(
            start,
            pick,
            precision=lax.Precision.HIGHEST,
            preferred_element_type=jnp.float32,
        )


def split(value):
    high = value.astype(jnp.bfloat16)
    low = (value - high.astype(jnp.float32)).astype(jnp.bfloat16)
    return high, low


def load_weights(w_ref, col_tiles):
    first = lax.axis_index("freq") * col_tiles
    return jnp.concatenate([w_ref[pl.ds(first + c, 1), :] for c in range(col_tiles)], axis=1)


def flip_groups(groups, flipped):
    turned = flipped.T
    lane = lax.broadcasted_iota(jnp.int32, (NB, LANES), 1)
    out = []
    for g in range(PACK):
        total = groups[g]
        for q in range(PACK):
            block = turned[q * NB : (q + 1) * NB]
            if q != g:
                block = pltpu.roll(block, ((q - g) % PACK) * NB, 1)
            total = total + jnp.where(lane // NB == q, block, 0.0)
        out.append(total)
    return out


TILE = 8


def turn_tiles(tiles):
    row = lax.broadcasted_iota(jnp.int32, (TILE, LANES), 0)
    step = TILE // 2
    while step:
        keep = row % (2 * step) < step
        turned = list(tiles)
        for i in range(TILE):
            if i % (2 * step) < step:
                low, high = tiles[i], tiles[i + step]
                turned[i] = jnp.where(keep, low, pltpu.roll(high, step, 0))
                turned[i + step] = jnp.where(keep, pltpu.roll(low, TILE - step, 0), high)
        tiles = turned
        step //= 2
    return tiles


def core_bit():
    return lax.rem(lax.axis_index("pts"), 2)


def y_bit():
    return lax.rem(lax.div(lax.axis_index("pts"), 2), 2)


RESP_ROWS = 2 * NF // PACK


def give_half(value_ref, bit, keep_ref, send_ref):
    half = keep_ref.shape[0] - RESP_ROWS
    keep_ref[pl.ds(0, half), :] = value_ref[pl.ds(bit * half, half), :]
    send_ref[pl.ds(0, half), :] = value_ref[pl.ds((1 - bit) * half, half), :]
    resp = value_ref[pl.ds(2 * half, RESP_ROWS), :]
    keep_ref[pl.ds(half, RESP_ROWS), :] = resp
    send_ref[pl.ds(half, RESP_ROWS), :] = resp


def gram_kernel(
    total_rows,
    places,
    by_core,
    x_hbm,
    aux_ref,
    keep_ref,
    send_ref,
    high_ref,
    rest_ref,
    low_hbm,
    x_ref,
    dft_ref,
    low_ref,
    block_even,
    block_odd,
    spec_ref,
    z_even,
    z_odd,
    real_ref,
    imag_ref,
    spread_ref,
    pack_ref,
    in_sems,
    out_sem,
):
    times, cols = x_ref.shape
    col_tiles = cols // LANES
    block_refs = (block_even, block_odd)
    cuts = [0] + [(first + TILE + 1) * HALF for first in range(0, NB, TILE)]

    def fetches(i):
        middle = (cuts[i] + cuts[i + 1]) // (2 * HALF) * HALF
        for n, (first, last) in enumerate(((cuts[i], middle), (middle, cuts[i + 1]))):
            rows = pl.ds(first, last - first)
            yield pltpu.make_async_copy(x_hbm.at[rows], x_ref.at[rows], in_sems.at[2 * i + n])

    for i in range(len(cuts) - 1):
        for fetch in fetches(i):
            fetch.start()
    fill_dft(dft_ref)
    spread_start(aux_ref, spread_ref)
    weights = load_weights(aux_ref.at[pl.ds(2 * NB, aux_ref.shape[0] - 2 * NB)], col_tiles)
    scale = jnp.sqrt(weights / (2.0 * total_rows))
    for fetch in fetches(0):
        fetch.wait()
    first_mean = jnp.mean(x_ref[pl.ds(0, NFFT), :], axis=0, keepdims=True)

    def center(i, acc):
        def step(h, acc):
            rows = pl.ds(pl.multiple_of(h * HALF, HALF), HALF)
            value = x_ref[rows, :] - first_mean
            high, low = split(value * scale)
            high_ref[rows, :] = high
            low_ref[rows, :] = low
            return acc + value

        return lax.fori_loop(cuts[i] // HALF, cuts[i + 1] // HALF, step, acc, unroll=True)

    def transform(first):
        for i in range(TILE // 2):
            blocks = []
            for s in range(2):
                rows = pl.ds((first + 2 * i + s) * HALF, NFFT)
                blocks.append(jnp.concatenate([high_ref[rows, :], low_ref[rows, :]], axis=0))
            both = jnp.dot(
                dft_ref[...], jnp.concatenate(blocks, axis=1), preferred_element_type=jnp.float32
            )
            spectrum = both[: 2 * NF] + both[2 * NF :]
            for s in range(2):
                block_refs[first // TILE % 2][2 * i + s] = spectrum[:, s * cols : (s + 1) * cols]

    def arrange(first):
        block_ref = block_refs[first // TILE % 2]
        for c in range(col_tiles):
            lanes = pl.ds(c * LANES, LANES)
            for o in range(2 * NF // TILE):
                rows = pl.ds(o * TILE, TILE)
                tiles = turn_tiles([block_ref[b, rows, lanes] for b in range(TILE)])
                for k in range(TILE):
                    spec_ref[c, o * TILE + k, pl.ds(first, TILE), :] = tiles[k]

    acc = center(0, jnp.zeros((HALF, cols), jnp.float32))
    transform(0)
    for first in range(0, NB, TILE):
        if first + TILE < NB:
            for fetch in fetches(first // TILE + 1):
                fetch.wait()
            acc = center(first // TILE + 1, acc)
            transform(first + TILE)
        arrange(first)
    pad = high_ref.shape[0] - times
    if pad:
        high_ref[pl.ds(times, pad), :] = jnp.zeros((pad, cols), jnp.bfloat16)
        low_ref[pl.ds(times, pad), :] = jnp.zeros((pad, cols), jnp.bfloat16)
    save_low = pltpu.make_async_copy(low_ref, low_hbm, out_sem)
    save_low.start()
    rest = jnp.sum(acc, axis=0, keepdims=True) / times * scale
    rest_ref[...] = jnp.broadcast_to(rest, rest_ref.shape)
    for k, leak in enumerate(window_leaks()):
        for c in range(col_tiles):
            part = rest[:, c * LANES : (c + 1) * LANES]
            spec_ref[c, k] = spec_ref[c, k] - leak * part

    row = lax.broadcasted_iota(jnp.int32, (NB, LANES), 0)
    lane = lax.broadcasted_iota(jnp.int32, (NB, LANES), 1)
    upper = row <= lane % NB
    octets = NF // 8

    def prepare(z_ref, octet, half):
        for part in range(2):
            for q in range(PACK):
                own = pl.ds(part * LANES + q * NB, NB)
                for c in range(col_tiles):
                    value = spec_ref[c, NF * part + TILE * octet + PACK * half + q]
                    high = value.astype(jnp.bfloat16)
                    low = (2.0 * (value - high.astype(jnp.float32))).astype(jnp.bfloat16)
                    z_ref[own, pl.ds(c * LANES, LANES)] = high
                    z_ref[own, pl.ds(cols + c * LANES, LANES)] = low

    def correlate(z_ref, group):
        high = z_ref[:, pl.ds(0, cols)]
        product = lax.dot_general(
            jnp.concatenate([high, high], axis=1),
            z_ref[...],
            (((1,), (1,)), ((), ())),
            preferred_element_type=jnp.float32,
        )
        gram_real = jnp.zeros((NB, LANES), jnp.float32)
        gram_imag = jnp.zeros((NB, LANES), jnp.float32)
        for q in range(PACK):
            mine = lane // NB == q
            real = product[q * NB : (q + 1) * NB]
            imag = product[LANES + q * NB : LANES + (q + 1) * NB]
            gram_real = jnp.where(mine, real[:, :LANES] + imag[:, LANES:], gram_real)
            gram_imag = jnp.where(mine, real[:, LANES:] - imag[:, :LANES], gram_imag)
        real_ref[group] = gram_real
        imag_ref[group] = gram_imag

    left = lane[: NB // 2] < LANES // 2
    half = NB // 2
    resp_real = []
    resp_imag = []

    def finish_quad(quad):
        own = pl.ds(quad * PACK, PACK)
        reals = [real_ref[quad * PACK + g] for g in range(PACK)]
        imags = [imag_ref[quad * PACK + g] for g in range(PACK)]
        reals = flip_groups(reals, real_ref[own].reshape(PACK * NB, LANES))
        imags = flip_groups(imags, -imag_ref[own].reshape(PACK * NB, LANES))
        for g, (real, imag) in enumerate(zip(reals, imags)):
            group = quad * PACK + g
            start_real = spread_ref[group, pl.ds(0, NB), :]
            start_imag = spread_ref[group, pl.ds(NB, NB), :]
            resp_real.append(
                jnp.sum(real * start_real + imag * start_imag, axis=0, keepdims=True)
            )
            resp_imag.append(
                jnp.sum(real * start_imag - imag * start_real, axis=0, keepdims=True)
            )
            packed = jnp.where(upper, real, imag)
            top = packed[:half]
            bottom = packed[half:]
            even = jnp.where(left, top, pltpu.roll(bottom, LANES // 2, 1))
            odd = jnp.where(left, pltpu.roll(top, LANES // 2, 1), bottom)
            pack_ref[pl.ds(places[2 * group] * half, half), :] = even
            pack_ref[pl.ds(places[2 * group + 1] * half, half), :] = odd

    z_refs = (z_even, z_odd)
    groups = NF // PACK
    prepare(z_even, 0, 0)
    for group in range(groups):
        if group + 1 < groups:
            prepare(z_refs[(group + 1) % 2], (group + 1) // 2, (group + 1) % 2)
        correlate(z_refs[group % 2], group)
        if group % PACK == PACK - 1:
            finish_quad(group // PACK)
    resp = jnp.concatenate(resp_real + resp_imag, axis=0)
    pack_ref[pl.ds(NF // 2 * half, RESP_ROWS), :] = resp
    give_half(pack_ref, core_bit() if by_core else 0, keep_ref, send_ref)
    save_low.wait()


def gram_parts(snapshots, weight_rows, start_vec, total_rows, places, by_core):
    times, cols = snapshots.shape
    start = jnp.transpose(start_vec, (1, 2, 0)).reshape(2 * NB, NF)
    start = jnp.pad(start, ((0, 0), (0, LANES - NF)))
    aux = jnp.concatenate([start, weight_rows], axis=0)
    any_space = pl.BlockSpec(memory_space=pl.ANY)
    saved = jax.ShapeDtypeStruct((-(-times // LANES) * LANES, cols), jnp.bfloat16)
    half = floats(NF // 4 * NB // 2 + RESP_ROWS, LANES)
    return pl.pallas_call(
        functools.partial(gram_kernel, total_rows, places, by_core),
        out_shape=(half, half, saved, floats(8, cols), saved),
        in_specs=[any_space, VMEM],
        out_specs=(VMEM, VMEM, VMEM, VMEM, any_space),
        scratch_shapes=[
            pltpu.VMEM((times, cols), jnp.float32),
            pltpu.VMEM((4 * NF, 2 * NFFT), jnp.bfloat16),
            pltpu.VMEM(saved.shape, jnp.bfloat16),
            pltpu.VMEM((TILE, 2 * NF, cols), jnp.float32),
            pltpu.VMEM((TILE, 2 * NF, cols), jnp.float32),
            pltpu.VMEM((cols // LANES, 2 * NF, NB, LANES), jnp.float32),
            pltpu.VMEM((2 * LANES, 2 * cols), jnp.bfloat16),
            pltpu.VMEM((2 * LANES, 2 * cols), jnp.bfloat16),
            pltpu.VMEM((NF // PACK, NB, LANES), jnp.float32),
            pltpu.VMEM((NF // PACK, NB, LANES), jnp.float32),
            pltpu.VMEM((NF // PACK, 2 * NB, LANES), jnp.float32),
            pltpu.VMEM((NF // 2 * NB // 2 + RESP_ROWS, LANES), jnp.float32),
            pltpu.SemaphoreType.DMA((2 * NB // TILE,)),
            pltpu.SemaphoreType.DMA(()),
        ],
        compiler_params=pltpu.CompilerParams(vmem_limit_bytes=VMEM_LIMIT),
        cost_estimate=pl.CostEstimate(
            flops=5_000_000_000, bytes_accessed=8_000_000, transcendentals=0
        ),
        name="gram_parts",
    )(snapshots, aux)


def pair_square(even, odd):
    left = lax.broadcasted_iota(jnp.int32, (NB // 2, LANES), 1) < LANES // 2
    top = jnp.where(left, even, pltpu.roll(odd, LANES // 2, 1))
    bottom = jnp.where(left, pltpu.roll(even, LANES // 2, 1), odd)
    return jnp.concatenate([top, bottom], axis=0)


def hermitian(squares):
    row = lax.broadcasted_iota(jnp.int32, (NB, LANES), 0)
    col = lax.broadcasted_iota(jnp.int32, (NB, LANES), 1) % NB
    zero = jnp.zeros((NB, LANES), jnp.float32)
    full = squares + [zero] * (PACK - len(squares))
    turned = flip_groups([zero] * PACK, jnp.concatenate(full, axis=0))
    for square, flipped in zip(squares, turned):
        real = jnp.where(row <= col, square, flipped)
        imag = jnp.where(row > col, square, jnp.where(row < col, -flipped, 0.0))
        yield real, imag


def small_call(kernel, name, out_shape, scratch_shapes=(), limit=SMALL_LIMIT):
    def call(*args):
        return pl.pallas_call(
            kernel,
            out_shape=out_shape,
            in_specs=[VMEM] * len(args),
            out_specs=VMEM if isinstance(out_shape, jax.ShapeDtypeStruct) else (VMEM,) * len(out_shape),
            scratch_shapes=list(scratch_shapes),
            compiler_params=pltpu.CompilerParams(vmem_limit_bytes=limit),
            name=name,
        )(*args)

    return call


def floats(*shape):
    return jax.ShapeDtypeStruct(shape, jnp.float32)


def add_core_kernel(kept_ref, got_ref, out_ref):
    quarter = out_ref.shape[1] - RESP_ROWS
    tail = pl.ds(4 * quarter, RESP_ROWS)
    resp = kept_ref[tail, :] + got_ref[tail, :]
    for m in range(4):
        rows = pl.ds(m * quarter, quarter)
        out_ref[m, pl.ds(0, quarter), :] = kept_ref[rows, :] + got_ref[rows, :]
        out_ref[m, pl.ds(quarter, RESP_ROWS), :] = resp


def add_core(kept, got):
    quarter = (kept.shape[0] - RESP_ROWS) // 4
    return small_call(add_core_kernel, "add_core", floats(4, quarter + RESP_ROWS, LANES))(kept, got)


def add_near_kernel(parts_ref, out_ref):
    out_ref[...] = (parts_ref[0] + parts_ref[1]) + (parts_ref[2] + parts_ref[3])


def add_kernel(kept_ref, got_ref, out_ref):
    out_ref[...] = kept_ref[...] + got_ref[...]


def add(name, kept, got):
    return small_call(add_kernel, name, floats(*kept.shape))(kept, got)


def finish_kernel(kept_ref, got_ref, packed_ref, resp_ref):
    rows = packed_ref.shape[0]
    packed_ref[...] = kept_ref[pl.ds(0, rows), :] + got_ref[pl.ds(0, rows), :]
    tail = pl.ds(rows, RESP_ROWS)
    resp = kept_ref[tail, :] + got_ref[tail, :]
    real = resp[: RESP_ROWS // 2]
    imag = resp[RESP_ROWS // 2 :]
    power = real * real + imag * imag
    lane = lax.broadcasted_iota(jnp.int32, power.shape, 1)
    mean = jnp.zeros(power.shape, jnp.float32)
    for q in range(PACK):
        mine = lane // NB == q
        part = jnp.sum(jnp.where(mine, power, 0.0), axis=1, keepdims=True) / NB
        mean = jnp.where(mine, part, mean)
    scaling = 1.0 / jnp.sqrt(mean + 1e-06)
    resp_ref[pl.ds(0, RESP_ROWS // 2), :] = real * scaling
    resp_ref[pl.ds(RESP_ROWS // 2, RESP_ROWS // 2), :] = imag * scaling


def finish(kept, got):
    rows = kept.shape[0] - RESP_ROWS
    return small_call(finish_kernel, "finish", (floats(rows, LANES), floats(RESP_ROWS, LANES)))(
        kept, got
    )


def join_y_kernel(own_ref, got_ref, packed_ref):
    rows = own_ref.shape[0]
    for m, ref in enumerate((own_ref, got_ref)):
        packed_ref[pl.ds((y_bit() ^ m) * rows, rows), :] = ref[...]


def unpack_kernel(part_index, *refs):
    part_ref, out_hbm, full_ref, sem = refs[-4:]
    half = NB // 2
    count = part_ref.shape[0] // half
    for first in range(0, count, 2 * PACK):
        last = min(first + 2 * PACK, count)
        pairs = [part_ref[pl.ds(i * half, half), :] for i in range(first, last)]
        squares = [pair_square(*pairs[i : i + 2]) for i in range(0, len(pairs), 2)]
        for g, both in enumerate(hermitian(squares)):
            for q in range(PACK):
                freq = 2 * first + PACK * g + q
                for c in range(2):
                    full_ref[freq, c] = both[c][:, q * NB : (q + 1) * NB]
    start = 0 if part_index is None else (core_bit() ^ part_index) * 2 * count
    copy = pltpu.make_async_copy(full_ref, out_hbm.at[pl.ds(start, 2 * count)], sem)
    copy.start()
    copy.wait()


def unpack_gram(part, part_index=None, done=None):
    count = part.shape[0] * 4 // NB
    total = count if part_index is None else 2 * count
    any_space = pl.BlockSpec(memory_space=pl.ANY)
    before = () if done is None else (done,)
    return pl.pallas_call(
        functools.partial(unpack_kernel, part_index),
        out_shape=floats(total, 2, NB, NB),
        in_specs=[any_space] * len(before) + [VMEM],
        out_specs=any_space,
        scratch_shapes=[
            pltpu.VMEM((count, 2, NB, NB), jnp.float32),
            pltpu.SemaphoreType.DMA(()),
        ],
        input_output_aliases={0: 0} if before else {},
        compiler_params=pltpu.CompilerParams(vmem_limit_bytes=UNPACK_LIMIT),
        name="unpack_own" if part_index == 0 else "unpack_other",
    )(*before, part)


def hand_on_kernel(low_hbm, after_ref, out_ref, token_ref, sem):
    copy = pltpu.make_async_copy(low_hbm, out_ref, sem)
    copy.start()
    token_ref[...] = after_ref[pl.ds(0, TILE), :]
    copy.wait()


def hand_on(low, after):
    return pl.pallas_call(
        hand_on_kernel,
        out_shape=(jax.ShapeDtypeStruct(low.shape, low.dtype), floats(TILE, LANES)),
        in_specs=[pl.BlockSpec(memory_space=pl.ANY), VMEM],
        out_specs=(VMEM, VMEM),
        scratch_shapes=[pltpu.SemaphoreType.DMA(())],
        compiler_params=pltpu.CompilerParams(vmem_limit_bytes=SMALL_LIMIT),
        name="hand_on",
    )(low, after)


def modes_kernel(
    total_rows,
    slot,
    high_ref,
    low_ref,
    rest_ref,
    w_ref,
    table_ref,
    resp_ref,
    out_ref,
    a_ref,
):
    cols = high_ref.shape[1]
    padded = high_ref.shape[0]
    all_groups = RESP_ROWS // 2
    groups = all_groups if slot is None else all_groups // 2
    start = 0 if slot is None else (lax.axis_index("freq") ^ slot) * groups
    count = 2 * groups
    total = PACK * count
    leaks = window_leaks()
    corrections = []
    row = lax.broadcasted_iota(jnp.int32, (count, 1), 0)
    lane = lax.broadcasted_iota(jnp.int32, (count, LANES), 1)
    left = lane < HALF
    parts = [pl.ds(part * all_groups + start, groups) for part in range(2)]
    resp_all = jnp.concatenate([resp_ref[rows, :] for rows in parts], axis=0)
    for q in range(PACK):
        resp = pltpu.roll(resp_all, LANES - q * NB, 1) if q else resp_all
        if q < len(leaks):
            sums = jnp.sum(jnp.where(lane < NB, resp, 0.0), axis=1, keepdims=True) * leaks[q]
            sums = jnp.where(row % groups + start == 0, sums, 0.0)
            corrections.append(sums * rest_ref[pl.ds(0, 1), :])
        else:
            corrections.append(jnp.zeros((count, cols), jnp.float32))
        real = jnp.concatenate([resp[:groups]] * 2, axis=0)
        imag = jnp.concatenate([resp[groups:]] * 2, axis=0)
        tables = []
        for kind in range(2):
            pieces = [
                table_ref[kind, pl.ds(q * RESP_ROWS + part * all_groups + start, groups), :]
                for part in range(2)
            ]
            tables.append(jnp.concatenate(pieces, axis=0))
        first, second = tables
        first_turned = pltpu.roll(first, HALF, 1)
        second_turned = pltpu.roll(second, HALF, 1)

        def spread(value, block):
            if 0 <= block < NB:
                return jnp.broadcast_to(value[:, block : block + 1], (count, LANES))
            return jnp.zeros((count, LANES), jnp.float32)

        for m in range(padded // LANES):
            value = first_turned * jnp.where(left, spread(real, 2 * m - 1), spread(real, 2 * m + 1))
            value += second_turned * jnp.where(
                left, spread(imag, 2 * m - 1), spread(imag, 2 * m + 1)
            )
            if 2 * m < NB:
                value += first * spread(real, 2 * m) + second * spread(imag, 2 * m)
            high, low = split(value)
            own = pl.ds(m * LANES, LANES)
            a_ref[pl.ds(q * count, count), own] = high
            a_ref[pl.ds(total + q * count, count), own] = low
    both = jnp.dot(a_ref[...], high_ref[...], preferred_element_type=jnp.float32)
    modes = both[:total] + both[total:] - jnp.concatenate(corrections, axis=0)
    modes += jnp.dot(a_ref[pl.ds(0, total), :], low_ref[...], preferred_element_type=jnp.float32)
    modes = modes * jnp.sqrt(2.0 * total_rows / load_weights(w_ref, cols // LANES))
    for q in range(PACK):
        for part in range(2):
            rows = q * count + part * groups
            for c in range(cols // LANES):
                out_ref[2 * c + part, pl.ds(q, groups, stride=PACK), :] = modes[
                    rows : rows + groups, c * LANES : (c + 1) * LANES
                ]


def local_modes(high, low, rest, weight_rows, response, total_rows, slot):
    padded, cols = high.shape
    count = NF if slot is None else NF // 2
    return pl.pallas_call(
        functools.partial(modes_kernel, total_rows, slot),
        out_shape=floats(2 * cols // LANES, count, LANES),
        in_specs=[VMEM] * 6,
        out_specs=VMEM,
        scratch_shapes=[pltpu.VMEM((4 * count, padded), jnp.bfloat16)],
        compiler_params=pltpu.CompilerParams(vmem_limit_bytes=MODES_LIMIT),
        cost_estimate=pl.CostEstimate(
            flops=2_000_000_000, bytes_accessed=6_000_000, transcendentals=0
        ),
        name="own_modes" if slot == 0 else "sent_modes",
    )(high, low, rest, weight_rows, jnp.asarray(mode_tables()), response)


def join_kernel(kept_ref, got_ref, out_ref):
    tiles = got_ref.shape[0] // 2
    group = lax.axis_index("freq")
    for slot, ref in enumerate((kept_ref, got_ref)):
        for c in range(tiles):
            lanes = pl.ds(pl.multiple_of(((group ^ slot) * tiles + c) * LANES, LANES), LANES)
            for part in range(2):
                out_ref[:, part, lanes] = ref[2 * c + part]


def join_modes(kept, got):
    tiles, count, _ = got.shape
    return small_call(join_kernel, "join_modes", floats(count, 2, tiles * LANES))(kept, got)


def response_of(gram, start_vec):
    matvec = functools.partial(jnp.einsum, "fjk,fk->fj", precision=lax.Precision.HIGHEST)
    resp_real = matvec(gram[:, 0], start_vec[:, 0]) - matvec(gram[:, 1], start_vec[:, 1])
    resp_imag = matvec(gram[:, 0], start_vec[:, 1]) + matvec(gram[:, 1], start_vec[:, 0])
    scaling = 1.0 / jnp.sqrt(
        jnp.mean(resp_real * resp_real + resp_imag * resp_imag, axis=1, keepdims=True) + 1e-06
    )
    return jnp.stack([resp_real * scaling, resp_imag * scaling], axis=1)


def direction_shards(n_devices, snapshots, weight, start_vec):
    def swap(value, mask):
        return lax.ppermute(value, ("pts", "freq"), [(i, i ^ mask) for i in range(n_devices)])

    x, core, y, z_near, z_far = 1, 2, 4, 8, 16
    near = [
        [first + far, first + far + x, first + far + y, first + far + y + x]
        for far in range(0, n_devices, z_near)
        for first in (0, core)
    ]
    total_rows = float(weight.shape[0] * 16)
    weight_rows = weight.reshape(-1, LANES)
    places = [
        (i // 8 % 2) * 16 + (i // 4 % 2) * 8 + (i // 16) * 4 + i % 4 for i in range(NF // 2)
    ]
    keep, send, high, rest, low = gram_parts(
        snapshots, weight_rows, start_vec, total_rows, places, True
    )
    parts = add_core(keep, swap(send, core))
    parts = lax.all_to_all(
        parts, ("pts", "freq"), 0, 0, axis_index_groups=near, tiled=True
    )
    part = small_call(add_near_kernel, "add_near", floats(*parts.shape[1:]))(parts)
    part = add("add_z", part, swap(part, z_near))
    got = swap(part, z_far)
    low, token = hand_on(low, part)
    got, token = lax.optimization_barrier((got, token))
    packed, response = finish(part, got)
    other = swap(packed, y)
    modes_args = (high, low, rest, weight_rows, response, total_rows)
    got = swap(local_modes(*modes_args, 1), x)
    kept = local_modes(*modes_args, 0)
    other, kept = lax.optimization_barrier((other, kept))
    packed = small_call(join_y_kernel, "join_y", floats(2 * packed.shape[0], LANES))(packed, other)
    gram_mine = unpack_gram(packed, 0)
    gram_mine = unpack_gram(swap(packed, core), 1, gram_mine)
    gram_mine, got = lax.optimization_barrier((gram_mine, got))
    return gram_mine, join_modes(kept, got)


def shards(n_pts, n_freq, snapshots, weight, start_vec):
    cols = snapshots.shape[1]
    total_rows = float(weight.shape[0] * n_pts)
    n_devices = n_pts * n_freq
    mine_count = NF // n_freq
    group = lax.axis_index("freq")
    weight_rows = weight.reshape(-1, LANES)
    places = list(range(NF // 2))
    first, second, high, rest, low = gram_parts(
        snapshots, weight_rows, start_vec, total_rows, places, False
    )
    parts = jnp.concatenate([first[:-RESP_ROWS], second[:-RESP_ROWS]], axis=0)
    share = parts.reshape(n_devices, -1)
    share = jnp.sum(lax.all_to_all(share, ("freq", "pts"), 0, 0, tiled=True), axis=0)
    packed = lax.all_gather(share, "pts", axis=0, tiled=True)
    gram_mine = unpack_gram(packed.reshape(-1, LANES))
    start_mine = lax.dynamic_slice_in_dim(start_vec, group * mine_count, mine_count, 0)
    response = lax.all_gather(response_of(gram_mine, start_mine), "freq", axis=0, tiled=True)
    response = jnp.transpose(response.reshape(NF // PACK, PACK, 2, NB), (2, 0, 1, 3))
    response = response.reshape(RESP_ROWS, LANES)
    modes = local_modes(high, low, rest, weight_rows, response, total_rows, None)
    modes = modes.reshape(-1, n_freq, mine_count, LANES)
    modes = lax.all_to_all(jnp.moveaxis(modes, 1, 0), "freq", 0, 0, tiled=True)
    modes = modes.reshape(n_freq, cols // LANES, 2, mine_count, LANES)
    modes = jnp.transpose(modes, (3, 2, 0, 1, 4)).reshape(mine_count, 2, n_freq * cols)
    return gram_mine, modes


def solution(mesh):
    n_pts, n_freq = mesh.shape["pts"], mesh.shape["freq"]
    if (n_pts, n_freq) == (16, 2):
        body = functools.partial(direction_shards, n_pts * n_freq)
    else:
        body = functools.partial(shards, n_pts, n_freq)
    placed = (P(None, ("pts", "freq")), P("pts"), P())
    return jax.shard_map(
        body,
        mesh=mesh,
        in_specs=placed,
        out_specs=(P("freq", None, None, None), P("freq", None, "pts")),
        check_vma=False,
    )
```

```python
import functools
import math

import jax
import jax.numpy as jnp
import numpy as np
from jax import lax
from jax.experimental import pallas as pl
from jax.experimental.pallas import tpu as pltpu
from jax.sharding import PartitionSpec as P

NFFT = 128
HALF = NFFT // 2
NF = 64
NB = 32
LANES = 128
PACK = 4
VMEM_LIMIT = 51 * 1024 * 1024
SMALL_LIMIT = 8 * 1024 * 1024
MODES_LIMIT = 24 * 1024 * 1024
UNPACK_LIMIT = 53 * 1024 * 1024
VMEM = pl.BlockSpec(memory_space=pltpu.VMEM)


def dft_values():
    times = np.arange(NFFT)
    freqs = np.arange(NF)
    phases = (freqs[:, None] * times[None, :] % NFFT) * (2.0 * math.pi / NFFT)
    window = 0.5 - 0.5 * np.cos(times * (2.0 * math.pi / NFFT))
    weighted = window / np.sqrt(np.sum(window * window))
    return np.cos(phases) * weighted, -np.sin(phases) * weighted


def split_table(table):
    high = table.astype(jnp.bfloat16)
    low = (table - high.astype(np.float64)).astype(jnp.bfloat16)
    return high, low


def window_leaks():
    real, _ = dft_values()
    return [float(np.sum(real[k])) for k in range(2)]


def mode_tables():
    real, imag = dft_values()
    order = np.arange(NF).reshape(NF // PACK, PACK).T
    real, imag = real[order], imag[order]
    first = np.stack([real, imag], axis=1).reshape(2 * NF, NFFT)
    second = np.stack([-imag, real], axis=1).reshape(2 * NF, NFFT)
    return np.stack([first, second]).astype(np.float32)


def cosine_of_turns(count):
    folded = jnp.minimum(count, NFFT - count)
    angle = (NFFT // 4 - folded).astype(jnp.float32) * (2.0 * math.pi / NFFT)
    square = angle * angle
    series = 1.0
    for n in (10, 8, 6, 4, 2):
        series = 1.0 - square * series * (1.0 / (n * (n + 1)))
    return angle * series


def fill_dft(dft_ref):
    row = lax.broadcasted_iota(jnp.int32, (2 * NF, NFFT), 0)
    time = lax.broadcasted_iota(jnp.int32, (2 * NF, NFFT), 1)
    quarter = jnp.where(row < NF, 0, NFFT // 4)
    wave = cosine_of_turns((row % NF * time + quarter) % NFFT)
    window = 0.5 - 0.5 * np.cos(np.arange(NFFT) * (2.0 * math.pi / NFFT))
    norm = float(np.sqrt(np.sum(window * window)))
    high, low = split(wave * ((0.5 - 0.5 * cosine_of_turns(time)) / norm))
    dft_ref[pl.ds(0, 2 * NF), pl.ds(0, NFFT)] = high
    dft_ref[pl.ds(0, 2 * NF), pl.ds(NFFT, NFFT)] = high
    dft_ref[pl.ds(2 * NF, 2 * NF), pl.ds(0, NFFT)] = low
    dft_ref[pl.ds(2 * NF, 2 * NF), pl.ds(NFFT, NFFT)] = jnp.zeros((2 * NF, NFFT), jnp.bfloat16)


def spread_start(start_ref, spread_ref):
    row = lax.broadcasted_iota(jnp.int32, (NF, LANES), 0)
    lane = lax.broadcasted_iota(jnp.int32, (NF, LANES), 1)
    start = start_ref[pl.ds(0, 2 * NB), pl.ds(0, NF)]
    for g in range(NF // PACK):
        pick = (row == PACK * g + lane // NB).astype(jnp.float32)
        spread_ref[g] = jnp.dot(
            start,
            pick,
            precision=lax.Precision.HIGHEST,
            preferred_element_type=jnp.float32,
        )


def split(value):
    high = value.astype(jnp.bfloat16)
    low = (value - high.astype(jnp.float32)).astype(jnp.bfloat16)
    return high, low


def load_weights(w_ref, col_tiles):
    first = lax.axis_index("freq") * col_tiles
    return jnp.concatenate([w_ref[pl.ds(first + c, 1), :] for c in range(col_tiles)], axis=1)


def flip_groups(groups, flipped):
    turned = flipped.T
    lane = lax.broadcasted_iota(jnp.int32, (NB, LANES), 1)
    out = []
    for g in range(PACK):
        total = groups[g]
        for q in range(PACK):
            block = turned[q * NB : (q + 1) * NB]
            if q != g:
                block = pltpu.roll(block, ((q - g) % PACK) * NB, 1)
            total = total + jnp.where(lane // NB == q, block, 0.0)
        out.append(total)
    return out


TILE = 8


def turn_tiles(tiles):
    row = lax.broadcasted_iota(jnp.int32, (TILE, LANES), 0)
    step = TILE // 2
    while step:
        keep = row % (2 * step) < step
        turned = list(tiles)
        for i in range(TILE):
            if i % (2 * step) < step:
                low, high = tiles[i], tiles[i + step]
                turned[i] = jnp.where(keep, low, pltpu.roll(high, step, 0))
                turned[i + step] = jnp.where(keep, pltpu.roll(low, TILE - step, 0), high)
        tiles = turned
        step //= 2
    return tiles


def core_bit():
    return lax.rem(lax.axis_index("pts"), 2)


def y_bit():
    return lax.rem(lax.div(lax.axis_index("pts"), 2), 2)


RESP_ROWS = 2 * NF // PACK


def give_half(value_ref, bit, keep_ref, send_ref):
    half = keep_ref.shape[0] - RESP_ROWS
    keep_ref[pl.ds(0, half), :] = value_ref[pl.ds(bit * half, half), :]
    send_ref[pl.ds(0, half), :] = value_ref[pl.ds((1 - bit) * half, half), :]
    resp = value_ref[pl.ds(2 * half, RESP_ROWS), :]
    keep_ref[pl.ds(half, RESP_ROWS), :] = resp
    send_ref[pl.ds(half, RESP_ROWS), :] = resp


def gram_kernel(
    total_rows,
    places,
    by_core,
    x_hbm,
    aux_ref,
    keep_ref,
    send_ref,
    high_ref,
    rest_ref,
    low_hbm,
    x_ref,
    dft_ref,
    low_ref,
    block_even,
    block_odd,
    spec_ref,
    z_even,
    z_odd,
    real_ref,
    imag_ref,
    spread_ref,
    pack_ref,
    in_sems,
    out_sem,
):
    times, cols = x_ref.shape
    col_tiles = cols // LANES
    block_refs = (block_even, block_odd)
    cuts = [0] + [(first + TILE + 1) * HALF for first in range(0, NB, TILE)]

    def fetches(i):
        middle = (cuts[i] + cuts[i + 1]) // (2 * HALF) * HALF
        for n, (first, last) in enumerate(((cuts[i], middle), (middle, cuts[i + 1]))):
            rows = pl.ds(first, last - first)
            yield pltpu.make_async_copy(x_hbm.at[rows], x_ref.at[rows], in_sems.at[2 * i + n])

    for i in range(len(cuts) - 1):
        for fetch in fetches(i):
            fetch.start()
    fill_dft(dft_ref)
    spread_start(aux_ref, spread_ref)
    weights = load_weights(aux_ref.at[pl.ds(2 * NB, aux_ref.shape[0] - 2 * NB)], col_tiles)
    scale = jnp.sqrt(weights / (2.0 * total_rows))
    for fetch in fetches(0):
        fetch.wait()
    first_mean = jnp.mean(x_ref[pl.ds(0, NFFT), :], axis=0, keepdims=True)

    def center(i, acc):
        def step(h, acc):
            rows = pl.ds(pl.multiple_of(h * HALF, HALF), HALF)
            value = x_ref[rows, :] - first_mean
            high, low = split(value * scale)
            high_ref[rows, :] = high
            low_ref[rows, :] = low
            return acc + value

        return lax.fori_loop(cuts[i] // HALF, cuts[i + 1] // HALF, step, acc, unroll=True)

    def transform(first):
        for i in range(TILE // 2):
            blocks = []
            for s in range(2):
                rows = pl.ds((first + 2 * i + s) * HALF, NFFT)
                blocks.append(jnp.concatenate([high_ref[rows, :], low_ref[rows, :]], axis=0))
            both = jnp.dot(
                dft_ref[...], jnp.concatenate(blocks, axis=1), preferred_element_type=jnp.float32
            )
            spectrum = both[: 2 * NF] + both[2 * NF :]
            for s in range(2):
                block_refs[first // TILE % 2][2 * i + s] = spectrum[:, s * cols : (s + 1) * cols]

    def arrange(first):
        block_ref = block_refs[first // TILE % 2]
        for c in range(col_tiles):
            lanes = pl.ds(c * LANES, LANES)
            for o in range(2 * NF // TILE):
                rows = pl.ds(o * TILE, TILE)
                tiles = turn_tiles([block_ref[b, rows, lanes] for b in range(TILE)])
                for k in range(TILE):
                    spec_ref[c, o * TILE + k, pl.ds(first, TILE), :] = tiles[k]

    acc = center(0, jnp.zeros((HALF, cols), jnp.float32))
    transform(0)
    for first in range(0, NB, TILE):
        if first + TILE < NB:
            for fetch in fetches(first // TILE + 1):
                fetch.wait()
            acc = center(first // TILE + 1, acc)
            transform(first + TILE)
        arrange(first)
    pad = high_ref.shape[0] - times
    if pad:
        high_ref[pl.ds(times, pad), :] = jnp.zeros((pad, cols), jnp.bfloat16)
        low_ref[pl.ds(times, pad), :] = jnp.zeros((pad, cols), jnp.bfloat16)
    save_low = pltpu.make_async_copy(low_ref, low_hbm, out_sem)
    save_low.start()
    rest = jnp.sum(acc, axis=0, keepdims=True) / times * scale
    rest_ref[...] = jnp.broadcast_to(rest, rest_ref.shape)
    for k, leak in enumerate(window_leaks()):
        for c in range(col_tiles):
            part = rest[:, c * LANES : (c + 1) * LANES]
            spec_ref[c, k] = spec_ref[c, k] - leak * part

    row = lax.broadcasted_iota(jnp.int32, (NB, LANES), 0)
    lane = lax.broadcasted_iota(jnp.int32, (NB, LANES), 1)
    upper = row <= lane % NB
    octets = NF // 8

    def prepare(z_ref, octet, half):
        for part in range(2):
            for q in range(PACK):
                own = pl.ds(part * LANES + q * NB, NB)
                for c in range(col_tiles):
                    value = spec_ref[c, NF * part + TILE * octet + PACK * half + q]
                    high = value.astype(jnp.bfloat16)
                    low = (2.0 * (value - high.astype(jnp.float32))).astype(jnp.bfloat16)
                    z_ref[own, pl.ds(c * LANES, LANES)] = high
                    z_ref[own, pl.ds(cols + c * LANES, LANES)] = low

    def correlate(z_ref, group):
        high = z_ref[:, pl.ds(0, cols)]
        product = lax.dot_general(
            jnp.concatenate([high, high], axis=1),
            z_ref[...],
            (((1,), (1,)), ((), ())),
            preferred_element_type=jnp.float32,
        )
        gram_real = jnp.zeros((NB, LANES), jnp.float32)
        gram_imag = jnp.zeros((NB, LANES), jnp.float32)
        for q in range(PACK):
            mine = lane // NB == q
            real = product[q * NB : (q + 1) * NB]
            imag = product[LANES + q * NB : LANES + (q + 1) * NB]
            gram_real = jnp.where(mine, real[:, :LANES] + imag[:, LANES:], gram_real)
            gram_imag = jnp.where(mine, real[:, LANES:] - imag[:, :LANES], gram_imag)
        real_ref[group] = gram_real
        imag_ref[group] = gram_imag

    left = lane[: NB // 2] < LANES // 2
    half = NB // 2
    resp_real = []
    resp_imag = []

    def finish_quad(quad):
        own = pl.ds(quad * PACK, PACK)
        reals = [real_ref[quad * PACK + g] for g in range(PACK)]
        imags = [imag_ref[quad * PACK + g] for g in range(PACK)]
        reals = flip_groups(reals, real_ref[own].reshape(PACK * NB, LANES))
        imags = flip_groups(imags, -imag_ref[own].reshape(PACK * NB, LANES))
        for g, (real, imag) in enumerate(zip(reals, imags)):
            group = quad * PACK + g
            start_real = spread_ref[group, pl.ds(0, NB), :]
            start_imag = spread_ref[group, pl.ds(NB, NB), :]
            resp_real.append(
                jnp.sum(real * start_real + imag * start_imag, axis=0, keepdims=True)
            )
            resp_imag.append(
                jnp.sum(real * start_imag - imag * start_real, axis=0, keepdims=True)
            )
            packed = jnp.where(upper, real, imag)
            top = packed[:half]
            bottom = packed[half:]
            even = jnp.where(left, top, pltpu.roll(bottom, LANES // 2, 1))
            odd = jnp.where(left, pltpu.roll(top, LANES // 2, 1), bottom)
            pack_ref[pl.ds(places[2 * group] * half, half), :] = even
            pack_ref[pl.ds(places[2 * group + 1] * half, half), :] = odd

    z_refs = (z_even, z_odd)
    groups = NF // PACK
    prepare(z_even, 0, 0)
    for group in range(groups):
        if group + 1 < groups:
            prepare(z_refs[(group + 1) % 2], (group + 1) // 2, (group + 1) % 2)
        correlate(z_refs[group % 2], group)
        if group % PACK == PACK - 1:
            finish_quad(group // PACK)
    resp = jnp.concatenate(resp_real + resp_imag, axis=0)
    pack_ref[pl.ds(NF // 2 * half, RESP_ROWS), :] = resp
    give_half(pack_ref, core_bit() if by_core else 0, keep_ref, send_ref)
    save_low.wait()


def gram_parts(snapshots, weight_rows, start_vec, total_rows, places, by_core):
    times, cols = snapshots.shape
    start = jnp.transpose(start_vec, (1, 2, 0)).reshape(2 * NB, NF)
    start = jnp.pad(start, ((0, 0), (0, LANES - NF)))
    aux = jnp.concatenate([start, weight_rows], axis=0)
    any_space = pl.BlockSpec(memory_space=pl.ANY)
    saved = jax.ShapeDtypeStruct((-(-times // LANES) * LANES, cols), jnp.bfloat16)
    half = floats(NF // 4 * NB // 2 + RESP_ROWS, LANES)
    return pl.pallas_call(
        functools.partial(gram_kernel, total_rows, places, by_core),
        out_shape=(half, half, saved, floats(8, cols), saved),
        in_specs=[any_space, VMEM],
        out_specs=(VMEM, VMEM, VMEM, VMEM, any_space),
        scratch_shapes=[
            pltpu.VMEM((times, cols), jnp.float32),
            pltpu.VMEM((4 * NF, 2 * NFFT), jnp.bfloat16),
            pltpu.VMEM(saved.shape, jnp.bfloat16),
            pltpu.VMEM((TILE, 2 * NF, cols), jnp.float32),
            pltpu.VMEM((TILE, 2 * NF, cols), jnp.float32),
            pltpu.VMEM((cols // LANES, 2 * NF, NB, LANES), jnp.float32),
            pltpu.VMEM((2 * LANES, 2 * cols), jnp.bfloat16),
            pltpu.VMEM((2 * LANES, 2 * cols), jnp.bfloat16),
            pltpu.VMEM((NF // PACK, NB, LANES), jnp.float32),
            pltpu.VMEM((NF // PACK, NB, LANES), jnp.float32),
            pltpu.VMEM((NF // PACK, 2 * NB, LANES), jnp.float32),
            pltpu.VMEM((NF // 2 * NB // 2 + RESP_ROWS, LANES), jnp.float32),
            pltpu.SemaphoreType.DMA((2 * NB // TILE,)),
            pltpu.SemaphoreType.DMA(()),
        ],
        compiler_params=pltpu.CompilerParams(vmem_limit_bytes=VMEM_LIMIT),
        cost_estimate=pl.CostEstimate(
            flops=5_000_000_000, bytes_accessed=8_000_000, transcendentals=0
        ),
        name="gram_parts",
    )(snapshots, aux)


def pair_square(even, odd):
    left = lax.broadcasted_iota(jnp.int32, (NB // 2, LANES), 1) < LANES // 2
    top = jnp.where(left, even, pltpu.roll(odd, LANES // 2, 1))
    bottom = jnp.where(left, pltpu.roll(even, LANES // 2, 1), odd)
    return jnp.concatenate([top, bottom], axis=0)


def hermitian(squares):
    row = lax.broadcasted_iota(jnp.int32, (NB, LANES), 0)
    col = lax.broadcasted_iota(jnp.int32, (NB, LANES), 1) % NB
    zero = jnp.zeros((NB, LANES), jnp.float32)
    full = squares + [zero] * (PACK - len(squares))
    turned = flip_groups([zero] * PACK, jnp.concatenate(full, axis=0))
    for square, flipped in zip(squares, turned):
        real = jnp.where(row <= col, square, flipped)
        imag = jnp.where(row > col, square, jnp.where(row < col, -flipped, 0.0))
        yield real, imag


def small_call(kernel, name, out_shape, scratch_shapes=(), limit=SMALL_LIMIT):
    def call(*args):
        return pl.pallas_call(
            kernel,
            out_shape=out_shape,
            in_specs=[VMEM] * len(args),
            out_specs=VMEM if isinstance(out_shape, jax.ShapeDtypeStruct) else (VMEM,) * len(out_shape),
            scratch_shapes=list(scratch_shapes),
            compiler_params=pltpu.CompilerParams(vmem_limit_bytes=limit),
            name=name,
        )(*args)

    return call


def floats(*shape):
    return jax.ShapeDtypeStruct(shape, jnp.float32)


def add_split_kernel(bit, kept_ref, got_ref, keep_ref, send_ref, sum_ref):
    sum_ref[...] = kept_ref[...] + got_ref[...]
    give_half(sum_ref, bit(), keep_ref, send_ref)


def add_split(bit, name, kept, got):
    half = floats((kept.shape[0] - RESP_ROWS) // 2 + RESP_ROWS, LANES)
    scratch = [pltpu.VMEM(kept.shape, jnp.float32)]
    return small_call(functools.partial(add_split_kernel, bit), name, (half, half), scratch)(
        kept, got
    )


def add_kernel(kept_ref, got_ref, out_ref):
    out_ref[...] = kept_ref[...] + got_ref[...]


def add(name, kept, got):
    return small_call(add_kernel, name, floats(*kept.shape))(kept, got)


def finish_kernel(kept_ref, got_ref, packed_ref, resp_ref):
    rows = packed_ref.shape[0]
    packed_ref[...] = kept_ref[pl.ds(0, rows), :] + got_ref[pl.ds(0, rows), :]
    tail = pl.ds(rows, RESP_ROWS)
    resp = kept_ref[tail, :] + got_ref[tail, :]
    real = resp[: RESP_ROWS // 2]
    imag = resp[RESP_ROWS // 2 :]
    power = real * real + imag * imag
    lane = lax.broadcasted_iota(jnp.int32, power.shape, 1)
    mean = jnp.zeros(power.shape, jnp.float32)
    for q in range(PACK):
        mine = lane // NB == q
        part = jnp.sum(jnp.where(mine, power, 0.0), axis=1, keepdims=True) / NB
        mean = jnp.where(mine, part, mean)
    scaling = 1.0 / jnp.sqrt(mean + 1e-06)
    resp_ref[pl.ds(0, RESP_ROWS // 2), :] = real * scaling
    resp_ref[pl.ds(RESP_ROWS // 2, RESP_ROWS // 2), :] = imag * scaling


def finish(kept, got):
    rows = kept.shape[0] - RESP_ROWS
    return small_call(finish_kernel, "finish", (floats(rows, LANES), floats(RESP_ROWS, LANES)))(
        kept, got
    )


def join_y_kernel(own_ref, got_ref, packed_ref):
    rows = own_ref.shape[0]
    for m, ref in enumerate((own_ref, got_ref)):
        packed_ref[pl.ds((y_bit() ^ m) * rows, rows), :] = ref[...]


def unpack_kernel(part_index, *refs):
    part_ref, out_hbm, full_ref, sem = refs[-4:]
    half = NB // 2
    count = part_ref.shape[0] // half
    for first in range(0, count, 2 * PACK):
        last = min(first + 2 * PACK, count)
        pairs = [part_ref[pl.ds(i * half, half), :] for i in range(first, last)]
        squares = [pair_square(*pairs[i : i + 2]) for i in range(0, len(pairs), 2)]
        for g, both in enumerate(hermitian(squares)):
            for q in range(PACK):
                freq = 2 * first + PACK * g + q
                for c in range(2):
                    full_ref[freq, c] = both[c][:, q * NB : (q + 1) * NB]
    start = 0 if part_index is None else (core_bit() ^ part_index) * 2 * count
    copy = pltpu.make_async_copy(full_ref, out_hbm.at[pl.ds(start, 2 * count)], sem)
    copy.start()
    copy.wait()


def unpack_gram(part, part_index=None, done=None):
    count = part.shape[0] * 4 // NB
    total = count if part_index is None else 2 * count
    any_space = pl.BlockSpec(memory_space=pl.ANY)
    before = () if done is None else (done,)
    return pl.pallas_call(
        functools.partial(unpack_kernel, part_index),
        out_shape=floats(total, 2, NB, NB),
        in_specs=[any_space] * len(before) + [VMEM],
        out_specs=any_space,
        scratch_shapes=[
            pltpu.VMEM((count, 2, NB, NB), jnp.float32),
            pltpu.SemaphoreType.DMA(()),
        ],
        input_output_aliases={0: 0} if before else {},
        compiler_params=pltpu.CompilerParams(vmem_limit_bytes=UNPACK_LIMIT),
        name="unpack_own" if part_index == 0 else "unpack_other",
    )(*before, part)


def hand_on_kernel(low_hbm, after_ref, out_ref, token_ref, sem):
    copy = pltpu.make_async_copy(low_hbm, out_ref, sem)
    copy.start()
    token_ref[...] = after_ref[pl.ds(0, TILE), :]
    copy.wait()


def hand_on(low, after):
    return pl.pallas_call(
        hand_on_kernel,
        out_shape=(jax.ShapeDtypeStruct(low.shape, low.dtype), floats(TILE, LANES)),
        in_specs=[pl.BlockSpec(memory_space=pl.ANY), VMEM],
        out_specs=(VMEM, VMEM),
        scratch_shapes=[pltpu.SemaphoreType.DMA(())],
        compiler_params=pltpu.CompilerParams(vmem_limit_bytes=SMALL_LIMIT),
        name="hand_on",
    )(low, after)


def modes_kernel(
    total_rows,
    slot,
    high_ref,
    low_ref,
    rest_ref,
    w_ref,
    table_ref,
    resp_ref,
    out_ref,
    a_ref,
):
    cols = high_ref.shape[1]
    padded = high_ref.shape[0]
    all_groups = RESP_ROWS // 2
    groups = all_groups if slot is None else all_groups // 2
    start = 0 if slot is None else (lax.axis_index("freq") ^ slot) * groups
    count = 2 * groups
    total = PACK * count
    leaks = window_leaks()
    corrections = []
    row = lax.broadcasted_iota(jnp.int32, (count, 1), 0)
    lane = lax.broadcasted_iota(jnp.int32, (count, LANES), 1)
    left = lane < HALF
    parts = [pl.ds(part * all_groups + start, groups) for part in range(2)]
    resp_all = jnp.concatenate([resp_ref[rows, :] for rows in parts], axis=0)
    for q in range(PACK):
        resp = pltpu.roll(resp_all, LANES - q * NB, 1) if q else resp_all
        if q < len(leaks):
            sums = jnp.sum(jnp.where(lane < NB, resp, 0.0), axis=1, keepdims=True) * leaks[q]
            sums = jnp.where(row % groups + start == 0, sums, 0.0)
            corrections.append(sums * rest_ref[pl.ds(0, 1), :])
        else:
            corrections.append(jnp.zeros((count, cols), jnp.float32))
        real = jnp.concatenate([resp[:groups]] * 2, axis=0)
        imag = jnp.concatenate([resp[groups:]] * 2, axis=0)
        tables = []
        for kind in range(2):
            pieces = [
                table_ref[kind, pl.ds(q * RESP_ROWS + part * all_groups + start, groups), :]
                for part in range(2)
            ]
            tables.append(jnp.concatenate(pieces, axis=0))
        first, second = tables
        first_turned = pltpu.roll(first, HALF, 1)
        second_turned = pltpu.roll(second, HALF, 1)

        def spread(value, block):
            if 0 <= block < NB:
                return jnp.broadcast_to(value[:, block : block + 1], (count, LANES))
            return jnp.zeros((count, LANES), jnp.float32)

        for m in range(padded // LANES):
            value = first_turned * jnp.where(left, spread(real, 2 * m - 1), spread(real, 2 * m + 1))
            value += second_turned * jnp.where(
                left, spread(imag, 2 * m - 1), spread(imag, 2 * m + 1)
            )
            if 2 * m < NB:
                value += first * spread(real, 2 * m) + second * spread(imag, 2 * m)
            high, low = split(value)
            own = pl.ds(m * LANES, LANES)
            a_ref[pl.ds(q * count, count), own] = high
            a_ref[pl.ds(total + q * count, count), own] = low
    both = jnp.dot(a_ref[...], high_ref[...], preferred_element_type=jnp.float32)
    modes = both[:total] + both[total:] - jnp.concatenate(corrections, axis=0)
    modes += jnp.dot(a_ref[pl.ds(0, total), :], low_ref[...], preferred_element_type=jnp.float32)
    modes = modes * jnp.sqrt(2.0 * total_rows / load_weights(w_ref, cols // LANES))
    for q in range(PACK):
        for part in range(2):
            rows = q * count + part * groups
            for c in range(cols // LANES):
                out_ref[2 * c + part, pl.ds(q, groups, stride=PACK), :] = modes[
                    rows : rows + groups, c * LANES : (c + 1) * LANES
                ]


def local_modes(high, low, rest, weight_rows, response, total_rows, slot):
    padded, cols = high.shape
    count = NF if slot is None else NF // 2
    return pl.pallas_call(
        functools.partial(modes_kernel, total_rows, slot),
        out_shape=floats(2 * cols // LANES, count, LANES),
        in_specs=[VMEM] * 6,
        out_specs=VMEM,
        scratch_shapes=[pltpu.VMEM((4 * count, padded), jnp.bfloat16)],
        compiler_params=pltpu.CompilerParams(vmem_limit_bytes=MODES_LIMIT),
        cost_estimate=pl.CostEstimate(
            flops=2_000_000_000, bytes_accessed=6_000_000, transcendentals=0
        ),
        name="own_modes" if slot == 0 else "sent_modes",
    )(high, low, rest, weight_rows, jnp.asarray(mode_tables()), response)


def join_kernel(kept_ref, got_ref, out_ref):
    tiles = got_ref.shape[0] // 2
    group = lax.axis_index("freq")
    for slot, ref in enumerate((kept_ref, got_ref)):
        for c in range(tiles):
            lanes = pl.ds(pl.multiple_of(((group ^ slot) * tiles + c) * LANES, LANES), LANES)
            for part in range(2):
                out_ref[:, part, lanes] = ref[2 * c + part]


def join_modes(kept, got):
    tiles, count, _ = got.shape
    return small_call(join_kernel, "join_modes", floats(count, 2, tiles * LANES))(kept, got)


def response_of(gram, start_vec):
    matvec = functools.partial(jnp.einsum, "fjk,fk->fj", precision=lax.Precision.HIGHEST)
    resp_real = matvec(gram[:, 0], start_vec[:, 0]) - matvec(gram[:, 1], start_vec[:, 1])
    resp_imag = matvec(gram[:, 0], start_vec[:, 1]) + matvec(gram[:, 1], start_vec[:, 0])
    scaling = 1.0 / jnp.sqrt(
        jnp.mean(resp_real * resp_real + resp_imag * resp_imag, axis=1, keepdims=True) + 1e-06
    )
    return jnp.stack([resp_real * scaling, resp_imag * scaling], axis=1)


def direction_shards(n_devices, snapshots, weight, start_vec):
    def swap(value, mask):
        return lax.ppermute(value, ("pts", "freq"), [(i, i ^ mask) for i in range(n_devices)])

    x, core, y, z_near, z_far = 1, 2, 4, 8, 16
    total_rows = float(weight.shape[0] * 16)
    weight_rows = weight.reshape(-1, LANES)
    places = [(i // 8 % 2) * 16 + (i // 16) * 8 + i % 8 for i in range(NF // 2)]
    keep, send, high, rest, low = gram_parts(
        snapshots, weight_rows, start_vec, total_rows, places, True
    )
    keep, send = add_split(lambda: lax.axis_index("freq"), "add_core", keep, swap(send, core))
    keep, send = add_split(y_bit, "add_x", keep, swap(send, x))
    part = add("add_y", keep, swap(send, y))
    part = add("add_z", part, swap(part, z_near))
    got = swap(part, z_far)
    low, token = hand_on(low, part)
    got, token = lax.optimization_barrier((got, token))
    packed, response = finish(part, got)
    other = swap(packed, y)
    modes_args = (high, low, rest, weight_rows, response, total_rows)
    got = swap(local_modes(*modes_args, 1), x)
    kept = local_modes(*modes_args, 0)
    other, kept = lax.optimization_barrier((other, kept))
    packed = small_call(join_y_kernel, "join_y", floats(2 * packed.shape[0], LANES))(packed, other)
    gram_mine = unpack_gram(packed, 0)
    gram_mine = unpack_gram(swap(packed, core), 1, gram_mine)
    gram_mine, got = lax.optimization_barrier((gram_mine, got))
    return gram_mine, join_modes(kept, got)


def shards(n_pts, n_freq, snapshots, weight, start_vec):
    cols = snapshots.shape[1]
    total_rows = float(weight.shape[0] * n_pts)
    n_devices = n_pts * n_freq
    mine_count = NF // n_freq
    group = lax.axis_index("freq")
    weight_rows = weight.reshape(-1, LANES)
    places = list(range(NF // 2))
    first, second, high, rest, low = gram_parts(
        snapshots, weight_rows, start_vec, total_rows, places, False
    )
    parts = jnp.concatenate([first[:-RESP_ROWS], second[:-RESP_ROWS]], axis=0)
    share = parts.reshape(n_devices, -1)
    share = jnp.sum(lax.all_to_all(share, ("freq", "pts"), 0, 0, tiled=True), axis=0)
    packed = lax.all_gather(share, "pts", axis=0, tiled=True)
    gram_mine = unpack_gram(packed.reshape(-1, LANES))
    start_mine = lax.dynamic_slice_in_dim(start_vec, group * mine_count, mine_count, 0)
    response = lax.all_gather(response_of(gram_mine, start_mine), "freq", axis=0, tiled=True)
    response = jnp.transpose(response.reshape(NF // PACK, PACK, 2, NB), (2, 0, 1, 3))
    response = response.reshape(RESP_ROWS, LANES)
    modes = local_modes(high, low, rest, weight_rows, response, total_rows, None)
    modes = modes.reshape(-1, n_freq, mine_count, LANES)
    modes = lax.all_to_all(jnp.moveaxis(modes, 1, 0), "freq", 0, 0, tiled=True)
    modes = modes.reshape(n_freq, cols // LANES, 2, mine_count, LANES)
    modes = jnp.transpose(modes, (3, 2, 0, 1, 4)).reshape(mine_count, 2, n_freq * cols)
    return gram_mine, modes


def solution(mesh):
    n_pts, n_freq = mesh.shape["pts"], mesh.shape["freq"]
    if (n_pts, n_freq) == (16, 2):
        body = functools.partial(direction_shards, n_pts * n_freq)
    else:
        body = functools.partial(shards, n_pts, n_freq)
    placed = (P(None, ("pts", "freq")), P("pts"), P())
    return jax.shard_map(
        body,
        mesh=mesh,
        in_specs=placed,
        out_specs=(P("freq", None, None, None), P("freq", None, "pts")),
        check_vma=False,
    )
```
